32 devices in a mesh: groups: 2 (over x), prow: 16 (over z, y, core).
Axes of the slice: x: 2, y: 2, z: 4, core: 2. Of those that a mesh axis runs over, the one named last changes fastest.
Arguments:
- green_same: bfloat16 [18432, 512], P(('groups', 'prow')), parts along dimension 0, may hold values from -6 to 6
- green_opp: bfloat16 [18432, 512], P(('groups', 'prow')), parts along dimension 0, may hold values from -6 to 6
- interaction: bfloat16 [18432, 9216], P(('groups', 'prow')), parts along dimension 0, may hold values from -0.0625 to 0.0625
- pattern: int32 [192, 96], P('groups'), parts along dimension 0, may hold values 0 or 1
- occupation: float32 [192], P('groups'), parts along dimension 0, may hold values from 0.05 to 0.95
- hopping: float32 [192, 96], P('groups'), parts along dimension 0, may hold values from -0.625 to 0.625
Outputs:
- slope_same: float32 [18432, 512], P(('groups', 'prow')), parts along dimension 0
- slope_opp: float32 [18432, 512], P(('groups', 'prow')), parts along dimension 0
- next_same: bfloat16 [18432, 512], P(('groups', 'prow')), parts along dimension 0
- next_opp: bfloat16 [18432, 512], P(('groups', 'prow')), parts along dimension 0
- collision: float32 [192, 512], P('groups'), parts along dimension 0
The draws below stay inside these ranges and needn't reach their ends.
There are 2 independent parts, one for each index of `groups`. The reference program is written for one: setup_inputs(seed, part) draws one part's arguments, and reference() takes and returns one part's arrays. A program takes and returns all parts, laid end to end along the dimension named above; each array names one. Nothing has to cross between parts.
All inputs are finite; a program needn't handle non-finite values.
Results may differ from the reference program's by a relative error of at most 0.0035.
Values may be sent and summed in bfloat16 or wider, within the bound.
No kernel may reach another device: no remote copies, remote signals or barrier semaphores. Data moves between devices by JAX's collectives and lax.ppermute only.
A program may use at most 256 MiB of HBM per device.

```python
import math
import jax
import jax.numpy as jnp
from jax import lax

NO = 96
P_SIZE = 9216
W = 512


def set_ends(array, rng, smallest, high):
    shape = array.shape
    spot = [jax.random.randint(jax.random.fold_in(rng, axis), (), 0, shape[axis]) for axis in range(len(shape))]
    array = array.at[tuple(spot)].set(smallest)
    longest = shape.index(max(shape))
    spot[longest] = (spot[longest] + 1) % shape[longest]
    return array.at[tuple(spot)].set(high)


def levels(own_key, extent, cuts, smallest, top_value):
    gain = 1.0
    for position, parts in cuts:
        heights = jax.random.uniform(jax.random.fold_in(jax.random.fold_in(own_key, 6), position), (parts,), jnp.float32, smallest / len(cuts), top_value / len(cuts))
        gain = gain * jnp.repeat(jnp.exp(heights), extent[position] // parts).reshape((-1,) + (1,) * (len(extent) - 1 - position))
    return gain


def normal_values(own_key, dims, spread, most, shards=(), held_as=jnp.bfloat16):
    gain = levels(own_key, dims, shards, -0.22, 0.18) if shards else 1.0
    drawn = jax.random.normal(own_key, dims, jnp.float32) * spread * gain
    return jnp.minimum(jnp.maximum(drawn, -most), most).astype(held_as)


def setup_inputs(seed: int = 0, part: int = 0) -> dict:
    keys = jax.random.split(jax.random.key(seed), 7)
    part_keys = jax.random.split(jax.random.fold_in(keys[6], part), 7)
    green_same = normal_values(part_keys[0], (P_SIZE, W), 1.0, 6.0, ((0, 16),))
    green_opp = normal_values(part_keys[1], (P_SIZE, W), 1.0, 6.0, ((0, 16),))
    interaction = normal_values(part_keys[2], (P_SIZE, P_SIZE), (NO * NO) ** -0.5, 0.0625, ((0, 16),))
    pattern = set_ends((jax.random.randint(part_keys[3], (NO, NO), 0, 2) < 1).astype(jnp.int32), jax.random.fold_in(part_keys[3], 1), 0, 1)
    occupation = jnp.clip(jax.random.uniform(part_keys[4], (NO,), jnp.float32, 0.05, 0.95), 0.05, 0.95)
    hopping = normal_values(part_keys[5], (NO, NO), NO ** -0.5, 0.625, (), jnp.float32)
    return {"green_same": green_same, "green_opp": green_opp, "interaction": interaction, "pattern": pattern, "occupation": occupation, "hopping": hopping}


def swap_orbitals(block):
    return block.reshape(NO, NO, -1).transpose(1, 0, 2).reshape(NO * NO, -1)

def reference(green_same, green_opp, interaction, pattern, occupation, hopping):
    swapped_same = swap_orbitals(green_same)
    swapped_opp = swap_orbitals(green_opp)
    polar_factor = occupation[:, None] - occupation[None, :]
    ladder_factor = 1.0 - occupation[:, None] - occupation[None, :]
    identity = jnp.eye(NO, dtype=jnp.float32)
    scale = 1.0 / math.sqrt(NO)

    def one_block(first):
        block_rows = lax.dynamic_slice_in_dim(interaction, first * NO, NO, 0)
        linked = lax.dynamic_index_in_dim(pattern, first, 0, keepdims=False).astype(jnp.float32)
        screened = block_rows.astype(jnp.float32).reshape(NO, NO, NO) * linked[None, :, None]
        polar_terms = screened * polar_factor[None]
        hop_row = lax.dynamic_index_in_dim(hopping, first, 0, keepdims=False)
        unit = (jnp.arange(NO, dtype=jnp.int32) == first).astype(jnp.float32)
        pair_hopping = hop_row[None, :, None] * identity[:, None, :] + unit[None, :, None] * hopping[:, None, :]
        kernel_direct = (polar_terms + pair_hopping).astype(jnp.bfloat16).reshape(NO, NO * NO)
        kernel_polar = polar_terms.astype(jnp.bfloat16).reshape(NO, NO * NO)
        kernel_ladder = (screened * ladder_factor[None]).astype(jnp.bfloat16).reshape(NO, NO * NO)
        slope_a = jnp.dot(kernel_direct, green_same, preferred_element_type=jnp.float32) + jnp.dot(kernel_polar, green_opp, preferred_element_type=jnp.float32) + jnp.dot(kernel_ladder, swapped_same, preferred_element_type=jnp.float32)
        slope_b = jnp.dot(kernel_direct, green_opp, preferred_element_type=jnp.float32) + jnp.dot(kernel_polar, green_same, preferred_element_type=jnp.float32) + jnp.dot(kernel_ladder, swapped_opp, preferred_element_type=jnp.float32)
        summed = lax.optimization_barrier(jnp.sum(slope_a + slope_b, axis=0)) * scale
        return (slope_a, slope_b, summed)
    blocks_a, blocks_b, collision = lax.map(one_block, jnp.arange(NO, dtype=jnp.int32))
    slope_same = blocks_a.reshape(NO * NO, -1)
    slope_opp = blocks_b.reshape(NO * NO, -1)
    next_same = (green_same.astype(jnp.float32) + 0.5 * slope_same).astype(jnp.bfloat16)
    next_opp = (green_opp.astype(jnp.float32) + 0.5 * slope_opp).astype(jnp.bfloat16)
    return (slope_same, slope_opp, next_same, next_opp, collision)
```

```python
import functools
import math

import jax
import jax.numpy as jnp
from jax import lax
from jax.experimental import pallas as pl
from jax.experimental.pallas import tpu as pltpu
from jax.sharding import PartitionSpec as P

MIB = 1 << 20


def swap_orbitals(block, orbitals):
    count = block.shape[1]
    return (
        block.reshape(orbitals, orbitals, count)
        .transpose(1, 0, 2)
        .reshape(orbitals * orbitals, count)
    )


def product(left, right):
    return jnp.dot(left, right, preferred_element_type=jnp.float32)


def plain_form(green_same, green_opp, interaction, pattern, occupation, hopping):
    rows, width = green_same.shape
    orbitals = hopping.shape[0]
    pairs = orbitals * orbitals
    highest = lax.Precision.HIGHEST
    row_ids = lax.axis_index("prow") * rows + jnp.arange(rows, dtype=jnp.int32)
    orbit_ids = jnp.arange(orbitals, dtype=jnp.int32)
    first_hot = (row_ids[:, None] // orbitals == orbit_ids[None, :]).astype(jnp.float32)
    second_hot = (row_ids[:, None] % orbitals == orbit_ids[None, :]).astype(jnp.float32)
    linked = jnp.dot(first_hot, pattern.astype(jnp.float32), precision=highest)
    screened = (
        interaction.astype(jnp.float32).reshape(rows, orbitals, orbitals) * linked[:, :, None]
    )
    polar_factor = occupation[:, None] - occupation[None, :]
    ladder_factor = 1.0 - occupation[:, None] - occupation[None, :]
    polar_terms = screened * polar_factor[None]
    hop_first = jnp.dot(first_hot, hopping, precision=highest)
    hop_second = jnp.dot(second_hot, hopping, precision=highest)
    pair_hopping = (
        hop_first[:, :, None] * second_hot[:, None, :]
        + first_hot[:, :, None] * hop_second[:, None, :]
    )
    kernel_direct = (polar_terms + pair_hopping).astype(jnp.bfloat16).reshape(rows, pairs)
    kernel_polar = polar_terms.astype(jnp.bfloat16).reshape(rows, pairs)
    kernel_ladder = (screened * ladder_factor[None]).astype(jnp.bfloat16).reshape(rows, pairs)
    same_piece = lax.all_gather(green_same, "prow", axis=0, tiled=True)
    opp_piece = lax.all_gather(green_opp, "prow", axis=0, tiled=True)
    new_same = (
        product(kernel_direct, same_piece)
        + product(kernel_polar, opp_piece)
        + product(kernel_ladder, swap_orbitals(same_piece, orbitals))
    )
    new_opp = (
        product(kernel_direct, opp_piece)
        + product(kernel_polar, same_piece)
        + product(kernel_ladder, swap_orbitals(opp_piece, orbitals))
    )
    next_same = (green_same.astype(jnp.float32) + 0.5 * new_same).astype(jnp.bfloat16)
    next_opp = (green_opp.astype(jnp.float32) + 0.5 * new_opp).astype(jnp.bfloat16)
    share = jnp.dot(first_hot.T, new_same + new_opp, precision=highest) * (
        1.0 / math.sqrt(orbitals)
    )
    collision = lax.psum(share, "prow")
    return (new_same, new_opp, next_same, next_opp, collision)


def build_body(orbitals, firsts, span, pairs, *refs):
    inter_ref, rows_ref, eye_ref, hop_ref = refs[:4]
    direct_ref, polar_ref, ladder_ref, turned_ref = refs[-4:]
    tiles = pairs // span
    per_tile = span // orbitals
    strips = -(-firsts * orbitals // 128)

    @pl.loop(0, tiles)
    def _(tile):
        cols = pl.ds(pl.multiple_of(tile * span, 128), span)
        block = inter_ref[:, cols].astype(jnp.float32)
        for strip in range(strips):
            piece = block[strip * 128 : (strip + 1) * 128]
            if piece.shape[0] < 128:
                piece = jnp.concatenate(
                    [piece, jnp.zeros((128 - piece.shape[0], span), jnp.float32)], axis=0
                )
            turned_ref[pl.ds(pl.multiple_of(strip * pairs + tile * span, 128), span), :] = piece.T
        for first in range(firsts):
            part = slice(first * orbitals, (first + 1) * orbitals)
            facts = rows_ref[first, :, cols]
            polar = block[part] * facts[0:1]
            hop = facts[2:3] * eye_ref[...] + facts[3:4] * hop_ref[...]
            polar_ref[part, cols] = polar.astype(jnp.bfloat16)
            direct_ref[part, cols] = (polar + hop).astype(jnp.bfloat16)

    @pl.loop(0, tiles)
    def _(tile):
        cols = pl.ds(pl.multiple_of(tile * span, 128), span)
        blocks = []
        for strip in range(strips):
            pieces = [
                turned_ref[
                    pl.ds(strip * pairs + tile * per_tile + inner, orbitals, stride=orbitals), :
                ]
                for inner in range(per_tile)
            ]
            blocks.append(jnp.concatenate(pieces, axis=0).T)
        block = jnp.concatenate(blocks, axis=0)
        for first in range(firsts):
            part = slice(first * orbitals, (first + 1) * orbitals)
            ladder = block[part] * rows_ref[first, 1:2, cols]
            ladder_ref[part, cols] = ladder.astype(jnp.bfloat16)


def build_kernels(interaction, facts, eye, hop, orbitals, firsts):
    rows, pairs = interaction.shape
    height = firsts * orbitals
    span = 4 * orbitals
    shape = jax.ShapeDtypeStruct((rows, pairs), jnp.bfloat16)
    made = ()
    for step in range(rows // height):
        wide = pl.BlockSpec((height, pairs), lambda g, step=step: (step, 0))
        made = pl.pallas_call(
            functools.partial(build_body, orbitals, firsts, span, pairs),
            grid=(1,),
            in_specs=[
                wide,
                pl.BlockSpec((firsts, 4, pairs), lambda g, step=step: (step, 0, 0)),
                pl.BlockSpec((orbitals, span), lambda g: (0, 0)),
                pl.BlockSpec((orbitals, span), lambda g: (0, 0)),
            ]
            + [pl.BlockSpec(memory_space=pl.ANY)] * len(made),
            out_specs=[wide] * 3,
            out_shape=[shape] * 3,
            scratch_shapes=[pltpu.VMEM((-(-height // 128) * pairs, 128), jnp.float32)],
            input_output_aliases={4 + n: n for n in range(len(made))},
            compiler_params=pltpu.CompilerParams(vmem_limit_bytes=56 * MIB),
            cost_estimate=pl.CostEstimate(
                flops=20 * height * pairs, bytes_accessed=8 * height * pairs, transcendentals=0
            ),
            name="build_kernels",
        )(interaction, facts, eye, hop, *made)
    return made


def step_body(chips, opening, closing, orbitals, scale, *refs):
    place_ref = refs[0]
    refs = list(refs[1:])
    mats = [[refs.pop(0) for _ in range(chips)] for _ in range(3)]
    greens = [[[refs.pop(0) for _ in range(2)] for _ in range(2)] for _ in range(chips)]
    sums = [] if opening else [refs.pop(0) for _ in range(2)]
    olds = [refs.pop(0) for _ in range(2)] if closing else []
    held = refs.pop()
    core = place_ref[0]
    rows = greens[0][0][0].shape[0]

    @pl.when(pl.program_id(0) == 0)
    def _():
        for chip in range(chips):
            for kind in range(2):
                for which in range(2):
                    lane = core if which == 0 else 1 - core
                    held[2 * chip + kind, pl.ds(pl.multiple_of(lane * rows, 64), rows), :] = greens[
                        chip
                    ][kind][which][...]

    totals = [None, None]
    for kind in range(2):
        total = None
        for chip in range(chips):
            mine = held[2 * chip + kind]
            other = held[2 * chip + 1 - kind]
            term = (
                product(mats[0][chip][...], mine)
                + product(mats[1][chip][...], other)
                + product(mats[2][chip][...], mine)
            )
            total = term if total is None else total + term
        totals[kind] = total if opening else sums[kind][...] + total
    refs[0][...] = totals[0]
    refs[1][...] = totals[1]
    if closing:
        for kind in range(2):
            old = olds[kind][...].astype(jnp.float32)
            refs[2 + kind][...] = (old + 0.5 * totals[kind]).astype(jnp.bfloat16)
        both = totals[0] + totals[1]
        count = both.shape[0] // orbitals
        for first in range(count):
            refs[4][0, first : first + 1, :] = (
                jnp.sum(both[first * orbitals : (first + 1) * orbitals], axis=0, keepdims=True)
                * scale
            )


def step(place, mats, greens, sums, olds, orbitals):
    chips = len(greens)
    opening, closing = not sums, bool(olds)
    rows, width = greens[0][0][0].shape
    height = 2 * orbitals
    wide = 2 * rows
    tall = pl.BlockSpec((height, width), lambda g, p: (g, 0))
    mat_specs = [
        pl.BlockSpec((height, wide), lambda g, p, chip=chip: (g, p[1 + chip]))
        for _ in range(3)
        for chip in range(chips)
    ]
    whole = pl.BlockSpec((rows, width), lambda g, p: (0, 0))
    out_specs = [tall, tall]
    out_shape = [jax.ShapeDtypeStruct((rows, width), jnp.float32)] * 2
    if closing:
        out_specs += [tall, tall, pl.BlockSpec((1, 2, width), lambda g, p: (g, 0, 0))]
        out_shape += [jax.ShapeDtypeStruct((rows, width), jnp.bfloat16)] * 2
        out_shape += [jax.ShapeDtypeStruct((rows // height, 2, width), jnp.float32)]
    operands = [mats[m] for m in range(3) for _ in range(chips)]
    operands += [greens[c][k][w] for c in range(chips) for k in range(2) for w in range(2)]
    in_specs = mat_specs + [whole] * (4 * chips)
    aliases = {}
    if not opening:
        aliases = {1 + len(operands): 0, 2 + len(operands): 1}
        operands += list(sums)
        in_specs += [tall, tall]
    if closing:
        operands += list(olds)
        in_specs += [tall, tall]
    return pl.pallas_call(
        functools.partial(
            step_body, chips, opening, closing, orbitals, 1.0 / math.sqrt(orbitals)
        ),
        grid_spec=pltpu.PrefetchScalarGridSpec(
            num_scalar_prefetch=1,
            grid=(rows // height,),
            in_specs=in_specs,
            out_specs=out_specs,
            scratch_shapes=[pltpu.VMEM((2 * chips, wide, width), jnp.bfloat16)],
        ),
        out_shape=out_shape,
        input_output_aliases=aliases,
        compiler_params=pltpu.CompilerParams(vmem_limit_bytes=56 * MIB),
        cost_estimate=pl.CostEstimate(
            flops=12 * chips * rows * wide * width,
            bytes_accessed=6 * chips * rows * wide + 16 * rows * width,
            transcendentals=0,
        ),
        name="add_products",
    )(place, *operands)


def ring_form(green_same, green_opp, interaction, pattern, occupation, hopping):
    rows, width = green_same.shape
    orbitals = hopping.shape[0]
    pairs = orbitals * orbitals
    devices = pairs // rows
    chips = devices // 2
    me = lax.axis_index("prow")
    core, chip = me % 2, me // 2
    order = list(range(0, chips, 2)) + list(range(chips - 1, 0, -2))
    spot = [order.index(c) for c in range(chips)]
    ahead = [order[(spot[c] + 1) % chips] for c in range(chips)]
    right = [(2 * c + k, 2 * ahead[c] + k) for c in range(chips) for k in range(2)]
    left = [(b, a) for a, b in right]
    across = [(d, d ^ 1) for d in range(devices)]
    order_at = jnp.array(order, jnp.int32)
    my_spot = jnp.array(spot, jnp.int32)[chip]

    def send(block, pairs_of):
        return lax.ppermute(block, "prow", pairs_of)

    per = rows // orbitals
    start = me * per
    occ_row = jnp.repeat(occupation, orbitals)
    occ_col = jnp.tile(occupation, orbitals)
    my_pattern = lax.dynamic_slice_in_dim(pattern, start, per, 0).astype(jnp.float32)
    my_hop = lax.dynamic_slice_in_dim(hopping, start, per, 0)
    firsts = start + jnp.arange(per, dtype=jnp.int32)
    second_ids = jnp.arange(pairs, dtype=jnp.int32) // orbitals
    facts = jnp.stack(
        [
            jnp.repeat(my_pattern, orbitals, axis=1) * (occ_row - occ_col)[None],
            jnp.tile(my_pattern, (1, orbitals)) * (1.0 - occ_col - occ_row)[None],
            jnp.repeat(my_hop, orbitals, axis=1),
            (firsts[:, None] == second_ids[None]).astype(jnp.float32),
        ],
        axis=1,
    )
    eye = jnp.tile(jnp.eye(orbitals, dtype=jnp.float32), (1, 4))
    hop = jnp.tile(hopping, (1, 4))
    mats = build_kernels(interaction, facts, eye, hop, orbitals, 2)

    own = (green_same, green_opp)
    partner = [send(block, across) for block in own]
    place = jnp.stack([core, chip]).astype(jnp.int32)
    sums = step(place, mats, [[[own[k], partner[k]] for k in range(2)]], (), (), orbitals)
    going = [own, own]
    half = chips // 2
    for hop_count in range(1, half):
        going = [
            [send(going[0][k], right) for k in range(2)],
            [send(going[1][k], left) for k in range(2)],
        ]
        shared = [[send(block, across) for block in side] for side in going]
        greens = [
            [[going[side][k], shared[side][k]] for k in range(2)] for side in range(2)
        ]
        behind = order_at[(my_spot - hop_count) % chips]
        before = order_at[(my_spot + hop_count) % chips]
        place = jnp.stack([core, behind, before]).astype(jnp.int32)
        sums = step(place, mats, greens, sums, (), orbitals)
    far = [send(going[0][0], right), send(going[1][1], left)]
    shared = [send(block, across) for block in far]
    place = jnp.stack([core, order_at[(my_spot + half) % chips]]).astype(jnp.int32)
    new_same, new_opp, next_same, next_opp, share = step(
        place,
        mats,
        [[[far[k], shared[k]] for k in range(2)]],
        sums,
        own,
        orbitals,
    )
    collision = lax.all_gather(share.reshape(per, width), "prow", axis=0, tiled=True)
    return (new_same, new_opp, next_same, next_opp, collision)


def per_device(green_same, green_opp, interaction, pattern, occupation, hopping):
    rows = green_same.shape[0]
    orbitals = hopping.shape[0]
    devices = orbitals * orbitals // rows
    fits = rows % (2 * orbitals) == 0 and rows % 64 == 0 and devices % 4 == 0 and devices >= 8
    form = ring_form if fits else plain_form
    return form(green_same, green_opp, interaction, pattern, occupation, hopping)


def solution(mesh):
    placed = (
        P(("groups", "prow"), None),
        P(("groups", "prow"), None),
        P(("groups", "prow"), None),
        P("groups", None),
        P("groups"),
        P("groups", None),
    )
    return jax.shard_map(
        per_device,
        mesh=mesh,
        in_specs=placed,
        out_specs=(
            P(("groups", "prow"), None),
            P(("groups", "prow"), None),
            P(("groups", "prow"), None),
            P(("groups", "prow"), None),
            P("groups", None),
        ),
        check_vma=False,
    )
```

```python
import functools
import math

import jax
import jax.numpy as jnp
from jax import lax
from jax.experimental import pallas as pl
from jax.experimental.pallas import tpu as pltpu
from jax.sharding import PartitionSpec as P

MIB = 1 << 20


def swap_orbitals(block, orbitals):
    count = block.shape[1]
    return (
        block.reshape(orbitals, orbitals, count)
        .transpose(1, 0, 2)
        .reshape(orbitals * orbitals, count)
    )


def product(left, right):
    return jnp.dot(left, right, preferred_element_type=jnp.float32)


def plain_form(green_same, green_opp, interaction, pattern, occupation, hopping):
    rows, width = green_same.shape
    orbitals = hopping.shape[0]
    pairs = orbitals * orbitals
    highest = lax.Precision.HIGHEST
    row_ids = lax.axis_index("prow") * rows + jnp.arange(rows, dtype=jnp.int32)
    orbit_ids = jnp.arange(orbitals, dtype=jnp.int32)
    first_hot = (row_ids[:, None] // orbitals == orbit_ids[None, :]).astype(jnp.float32)
    second_hot = (row_ids[:, None] % orbitals == orbit_ids[None, :]).astype(jnp.float32)
    linked = jnp.dot(first_hot, pattern.astype(jnp.float32), precision=highest)
    screened = (
        interaction.astype(jnp.float32).reshape(rows, orbitals, orbitals) * linked[:, :, None]
    )
    polar_factor = occupation[:, None] - occupation[None, :]
    ladder_factor = 1.0 - occupation[:, None] - occupation[None, :]
    polar_terms = screened * polar_factor[None]
    hop_first = jnp.dot(first_hot, hopping, precision=highest)
    hop_second = jnp.dot(second_hot, hopping, precision=highest)
    pair_hopping = (
        hop_first[:, :, None] * second_hot[:, None, :]
        + first_hot[:, :, None] * hop_second[:, None, :]
    )
    kernel_direct = (polar_terms + pair_hopping).astype(jnp.bfloat16).reshape(rows, pairs)
    kernel_polar = polar_terms.astype(jnp.bfloat16).reshape(rows, pairs)
    kernel_ladder = (screened * ladder_factor[None]).astype(jnp.bfloat16).reshape(rows, pairs)
    same_piece = lax.all_gather(green_same, "prow", axis=0, tiled=True)
    opp_piece = lax.all_gather(green_opp, "prow", axis=0, tiled=True)
    new_same = (
        product(kernel_direct, same_piece)
        + product(kernel_polar, opp_piece)
        + product(kernel_ladder, swap_orbitals(same_piece, orbitals))
    )
    new_opp = (
        product(kernel_direct, opp_piece)
        + product(kernel_polar, same_piece)
        + product(kernel_ladder, swap_orbitals(opp_piece, orbitals))
    )
    next_same = (green_same.astype(jnp.float32) + 0.5 * new_same).astype(jnp.bfloat16)
    next_opp = (green_opp.astype(jnp.float32) + 0.5 * new_opp).astype(jnp.bfloat16)
    share = jnp.dot(first_hot.T, new_same + new_opp, precision=highest) * (
        1.0 / math.sqrt(orbitals)
    )
    collision = lax.psum(share, "prow")
    return (new_same, new_opp, next_same, next_opp, collision)


def build_body(orbitals, low, high, pairs, *refs):
    place_ref, inter_ref, pat_ref, hop_ref, occ_ref, pat4_ref, hop4_ref, eye4_ref, occ4_ref = refs[:9]
    mixed_ref, polar_ref, turned_ref = refs[-3:]
    span = 4 * orbitals
    tiles = pairs // span
    start = place_ref[0]
    strips = range(0, high - low, 128)

    @pl.loop(0, tiles)
    def _(tile):
        cols = pl.ds(pl.multiple_of(tile * span, 128), span)
        for strip in strips:
            size = min(128, high - low - strip)
            piece = inter_ref[strip : strip + size, cols].T.astype(jnp.float32)
            at = strip // 128 * pairs + tile * span
            turned_ref[pl.ds(pl.multiple_of(at, 128), span), :size] = piece

    group = lax.broadcasted_iota(jnp.int32, (1, span), 1) // orbitals
    occ4 = occ4_ref[...]

    @pl.loop(0, tiles)
    def _(tile):
        cols = pl.ds(pl.multiple_of(tile * span, 128), span)

        def spread(values):
            row = jnp.where(group == 0, values[0], values[1])
            return jnp.where(group == 2, values[2], jnp.where(group == 3, values[3], row))

        inner = [4 * tile + m for m in range(4)]
        occ = spread([occ_ref[i] for i in inner])
        polar_factor = occ - occ4
        ladder_factor = (1.0 - occ4) - occ
        facts = {}
        for first in range(low // orbitals, -(-high // orbitals)):
            here = start + first
            linked = spread([pat_ref[here, i].astype(jnp.float32) for i in inner])
            hop_row = spread([hop_ref[here, i] for i in inner])
            unit = (group + 4 * tile == here).astype(jnp.float32)
            linked4 = pat4_ref[pl.ds(here, 1), :]
            facts[first] = (linked * polar_factor, linked4 * ladder_factor, hop_row, unit)
        for strip in strips:
            size = min(128, high - low - strip)
            pieces = [
                turned_ref[
                    pl.ds(strip // 128 * pairs + 4 * tile + m, orbitals, stride=orbitals), :
                ]
                for m in range(4)
            ]
            block = jnp.concatenate(pieces, axis=0).astype(jnp.bfloat16).T[:size]
            row = low + strip
            while row < low + strip + size:
                first, second = row // orbitals, row % orbitals
                count = min(orbitals - second, low + strip + size - row)
                there = slice(row - low, row - low + count)
                polar_row, ladder_row, hop_row, unit = facts[first]
                polar = inter_ref[there, cols].astype(jnp.float32) * polar_row
                hop = (
                    hop_row * eye4_ref[second : second + count]
                    + unit * hop4_ref[second : second + count]
                )
                part = block[row - low - strip : row - low - strip + count]
                ladder = (part.astype(jnp.float32) * ladder_row).astype(jnp.bfloat16)
                direct = (polar + hop).astype(jnp.bfloat16).astype(jnp.float32)
                held = polar.astype(jnp.bfloat16)
                polar_ref[there, cols] = held
                mixed_ref[there, cols] = (
                    direct - held.astype(jnp.float32) + ladder.astype(jnp.float32)
                ).astype(jnp.bfloat16)
                row += count


def build_rows(place, interaction, smalls, made, low, high):
    rows, pairs = interaction.shape
    pattern, hopping, occupation = smalls[:3]
    orbitals = hopping.shape[0]
    height = high - low
    block = low // height
    shape = jax.ShapeDtypeStruct((rows, pairs), jnp.bfloat16)
    wide = pl.BlockSpec((height, pairs), lambda g, p: (block, 0))
    smem = pl.BlockSpec(memory_space=pltpu.SMEM)
    row4 = pl.BlockSpec((1, 4 * orbitals), lambda g, p: (0, 0))
    small = pl.BlockSpec((orbitals, 4 * orbitals), lambda g, p: (0, 0))
    return pl.pallas_call(
        functools.partial(build_body, orbitals, low, high, pairs),
        grid_spec=pltpu.PrefetchScalarGridSpec(
            num_scalar_prefetch=1,
            grid=(1,),
            in_specs=[wide, smem, smem, smem, small, small, small, row4]
            + [pl.BlockSpec(memory_space=pl.ANY)] * len(made),
            out_specs=[wide] * 2,
            scratch_shapes=[pltpu.VMEM((-(-height // 128) * pairs, 128), jnp.float32)],
        ),
        out_shape=[shape] * 2,
        input_output_aliases={9 + n: n for n in range(len(made))},
        compiler_params=pltpu.CompilerParams(vmem_limit_bytes=44 * MIB),
        cost_estimate=pl.CostEstimate(
            flops=20 * height * pairs, bytes_accessed=6 * height * pairs, transcendentals=0
        ),
        name="build_rows",
    )(place, interaction, *smalls, *made)


def step_body(chips, opening, closing, orbitals, scale, *refs):
    place_ref = refs[0]
    refs = list(refs[1:])
    mixed_ref, polar_ref = refs.pop(0), refs.pop(0)
    greens = [[[refs.pop(0) for _ in range(2)] for _ in range(2)] for _ in range(chips)]
    sums = [] if opening else [refs.pop(0) for _ in range(3)]
    olds = [refs.pop(0) for _ in range(2)] if closing else []
    held = refs.pop()
    totals = [refs.pop() for _ in range(3)][::-1] if closing else refs[:3]
    core = place_ref[0]
    rows = greens[0][0][0].shape[0]
    now = pl.program_id(1)

    for chip in range(chips):

        @pl.when(now == chip)
        def _():
            for which in range(2):
                lane = core if which == 0 else 1 - core
                there = pl.ds(pl.multiple_of(lane * rows, 64), rows)
                same, opp = greens[chip][0][which][...], greens[chip][1][which][...]
                held[0, there, :] = same
                held[1, there, :] = opp
                both = same.astype(jnp.float32) + opp.astype(jnp.float32)
                held[2, there, :] = both.astype(jnp.bfloat16)

    @pl.when(now == 0)
    def _():
        for n in range(3):
            if opening:
                totals[n][...] = jnp.zeros_like(totals[n])
            else:
                totals[n][...] = sums[n][...]

    totals[0][...] += product(mixed_ref[...], held[0])
    totals[1][...] += product(mixed_ref[...], held[1])
    totals[2][...] += product(polar_ref[...], held[2])
    if closing:

        @pl.when(now == chips - 1)
        def _():
            for first in range(rows // orbitals):
                part = slice(first * orbitals, (first + 1) * orbitals)
                shared = totals[2][part, :]
                both = None
                for kind in range(2):
                    slope = totals[kind][part, :] + shared
                    old = olds[kind][part, :].astype(jnp.float32)
                    refs[kind][part, :] = slope
                    refs[2 + kind][part, :] = (old + 0.5 * slope).astype(jnp.bfloat16)
                    both = slope if both is None else both + slope
                refs[4][first : first + 1, :] = jnp.sum(both, axis=0, keepdims=True) * scale


def step(place, mats, greens, sums, olds, orbitals):
    chips = len(greens)
    opening, closing = not sums, bool(olds)
    rows, width = greens[0][0][0].shape
    wide = 2 * rows
    span = min(width, 256)
    tall = pl.BlockSpec((rows, span), lambda n, g, p: (0, n))
    mat = pl.BlockSpec((rows, wide), lambda n, g, p: (0, p[1 + g]))
    wide_sum = jax.ShapeDtypeStruct((rows, width), jnp.float32)
    scratch = [pltpu.VMEM((3, wide, span), jnp.bfloat16)]
    if closing:
        out_specs = [tall] * 4 + [pl.BlockSpec((rows // orbitals, span), lambda n, g, p: (0, n))]
        out_shape = [wide_sum] * 2 + [jax.ShapeDtypeStruct((rows, width), jnp.bfloat16)] * 2
        out_shape += [jax.ShapeDtypeStruct((rows // orbitals, width), jnp.float32)]
        scratch = [pltpu.VMEM((rows, span), jnp.float32)] * 3 + scratch
    else:
        out_specs, out_shape = [tall] * 3, [wide_sum] * 3
    operands = list(mats)
    operands += [greens[c][k][w] for c in range(chips) for k in range(2) for w in range(2)]
    in_specs = [mat] * 2 + [tall] * (4 * chips)
    aliases = {}
    if not opening:
        if not closing:
            aliases = {1 + len(operands) + n: n for n in range(3)}
        operands += list(sums)
        in_specs += [tall] * 3
    if closing:
        operands += list(olds)
        in_specs += [tall] * 2
    return pl.pallas_call(
        functools.partial(
            step_body, chips, opening, closing, orbitals, 1.0 / math.sqrt(orbitals)
        ),
        grid_spec=pltpu.PrefetchScalarGridSpec(
            num_scalar_prefetch=1,
            grid=(width // span, chips),
            in_specs=in_specs,
            out_specs=out_specs,
            scratch_shapes=scratch,
        ),
        out_shape=out_shape,
        input_output_aliases=aliases,
        compiler_params=pltpu.CompilerParams(vmem_limit_bytes=36 * MIB),
        cost_estimate=pl.CostEstimate(
            flops=6 * chips * rows * wide * width,
            bytes_accessed=8 * chips * rows * wide + 24 * rows * width,
            transcendentals=0,
        ),
        name="add_products",
    )(place, *operands)


def spread_blocks(block, index, stride, devices):
    blocks = [block]
    for other in range(1, 4):
        pairs_of = [(d, d ^ (other * stride)) for d in range(devices)]
        blocks.append(lax.ppermute(block, "prow", pairs_of))
    part = index // stride % 4
    low, high = part % 2 == 1, part // 2 == 1
    b = [jnp.where(low, blocks[n ^ 1], blocks[n]) for n in range(4)]
    b = [jnp.where(high, b[n ^ 2], b[n]) for n in range(4)]
    return jnp.concatenate(b, axis=0)


def after(value, *others):
    return lax.optimization_barrier((value, *others))[0]


def ring_form(green_same, green_opp, interaction, pattern, occupation, hopping):
    rows, width = green_same.shape
    orbitals = hopping.shape[0]
    pairs = orbitals * orbitals
    devices = pairs // rows
    chips = devices // 2
    me = lax.axis_index("prow")
    core, chip = me % 2, me // 2
    order = list(range(0, chips, 2)) + list(range(chips - 1, 0, -2))
    spot = [order.index(c) for c in range(chips)]
    ahead = [order[(spot[c] + 1) % chips] for c in range(chips)]
    right = [(2 * c + k, 2 * ahead[c] + k) for c in range(chips) for k in range(2)]
    left = [(b, a) for a, b in right]
    across = [(d, d ^ 1) for d in range(devices)]
    half = chips // 2
    table = []
    for c in range(chips):
        line = [c]
        for far in range(1, half + 1):
            line += [order[(spot[c] - far) % chips], order[(spot[c] + far) % chips]]
        table.append(line)
    line = lax.dynamic_index_in_dim(jnp.array(table, jnp.int32), chip, 0, keepdims=False)

    def send(block, pairs_of):
        return lax.ppermute(block, "prow", pairs_of)

    def both_ways(kind, blocks):
        return [send(blocks[0], right), send(blocks[1], left)]

    def share(blocks):
        return [(block, send(block, across)) for block in blocks]

    def place_of(low, high):
        return jnp.concatenate([core[None].astype(jnp.int32), line[low:high]])

    own = (green_same, green_opp)
    moving = [both_ways(kind, [own[kind]] * 2) for kind in range(2)]
    near = [share([own[kind]])[0] for kind in range(2)]

    start = (me * (rows // orbitals)).astype(jnp.int32)[None]
    smalls = (
        pattern,
        hopping,
        occupation,
        jnp.tile(pattern.astype(jnp.float32), (1, 4)),
        jnp.tile(hopping, (1, 4)),
        jnp.tile(jnp.eye(orbitals, dtype=jnp.float32), (1, 4)),
        jnp.tile(occupation, 4)[None],
    )
    big = rows // 9 * 4
    mats = build_rows(start, interaction, smalls, (), 0, big)

    got = [[], []]
    got[0] = [after(block, mats[0]) for block in moving[0]]
    moving[0] = both_ways(0, got[0])
    pair_same = share(got[0])
    mats = build_rows(after(start, got[0][0]), interaction, smalls, mats, big, 2 * big)

    got[1] = [after(block, mats[0]) for block in moving[1]]
    moving[1] = both_ways(1, got[1])
    pair_opp = share(got[1])
    mats = build_rows(after(start, got[1][0]), interaction, smalls, mats, 2 * big, rows)

    greens = [[near[0], near[1]]] + [[pair_same[n], pair_opp[n]] for n in range(2)]
    sums = ()
    for far in range(2, half):
        got[0] = [after(block, mats[0]) for block in moving[0]]
        last = far == half - 1
        if last:
            moving[0] = [send(got[0][0], right)]
        else:
            moving[0] = both_ways(0, got[0])
        pair_same = share(got[0])
        low = 0 if far == 2 else 2 * far - 3
        sums = step(
            after(place_of(low, 2 * far - 1), got[0][0]), mats, greens, sums, (), orbitals
        )
        got[1] = [after(block, sums[0]) for block in moving[1]]
        if last:
            moving[1] = [send(got[1][1], left)]
        else:
            moving[1] = both_ways(1, got[1])
        pair_opp = share(got[1])
        greens = [[pair_same[n], pair_opp[n]] for n in range(2)]
        mats = [after(mats[0], got[1][0]), mats[1]]
    low = 2 * half - 3
    sums = step(place_of(low, low + 2), mats, greens, sums, (), orbitals)
    far_same = share([after(moving[0][0], sums[0])])[0]
    far_opp = share([after(moving[1][0], sums[0])])[0]
    new_same, new_opp, next_same, next_opp, part = step(
        place_of(low + 2, low + 3), mats, [[far_same, far_opp]], sums, own, orbitals
    )
    if devices == 16:
        collision = spread_blocks(spread_blocks(part, me, 1, devices), me, 4, devices)
    else:
        collision = lax.all_gather(part, "prow", axis=0, tiled=True)
    return (new_same, new_opp, next_same, next_opp, collision)


def per_device(green_same, green_opp, interaction, pattern, occupation, hopping):
    rows = green_same.shape[0]
    orbitals = hopping.shape[0]
    devices = orbitals * orbitals // rows
    fits = rows % orbitals == 0 and rows % 576 == 0 and devices % 4 == 0 and devices >= 12
    form = ring_form if fits else plain_form
    return form(green_same, green_opp, interaction, pattern, occupation, hopping)


def solution(mesh):
    placed = (
        P(("groups", "prow"), None),
        P(("groups", "prow"), None),
        P(("groups", "prow"), None),
        P("groups", None),
        P("groups"),
        P("groups", None),
    )
    return jax.shard_map(
        per_device,
        mesh=mesh,
        in_specs=placed,
        out_specs=(
            P(("groups", "prow"), None),
            P(("groups", "prow"), None),
            P(("groups", "prow"), None),
            P(("groups", "prow"), None),
            P("groups", None),
        ),
        check_vma=False,
    )
```

```python
import functools
import math

import jax
import jax.numpy as jnp
from jax import lax
from jax.experimental import pallas as pl
from jax.experimental.pallas import tpu as pltpu
from jax.sharding import PartitionSpec as P

MIB = 1 << 20


def swap_orbitals(block, orbitals):
    count = block.shape[1]
    return (
        block.reshape(orbitals, orbitals, count)
        .transpose(1, 0, 2)
        .reshape(orbitals * orbitals, count)
    )


def product(left, right):
    return jnp.dot(left, right, preferred_element_type=jnp.float32)


def plain_form(green_same, green_opp, interaction, pattern, occupation, hopping):
    rows, width = green_same.shape
    orbitals = hopping.shape[0]
    pairs = orbitals * orbitals
    highest = lax.Precision.HIGHEST
    row_ids = lax.axis_index("prow") * rows + jnp.arange(rows, dtype=jnp.int32)
    orbit_ids = jnp.arange(orbitals, dtype=jnp.int32)
    first_hot = (row_ids[:, None] // orbitals == orbit_ids[None, :]).astype(jnp.float32)
    second_hot = (row_ids[:, None] % orbitals == orbit_ids[None, :]).astype(jnp.float32)
    linked = jnp.dot(first_hot, pattern.astype(jnp.float32), precision=highest)
    screened = (
        interaction.astype(jnp.float32).reshape(rows, orbitals, orbitals) * linked[:, :, None]
    )
    polar_factor = occupation[:, None] - occupation[None, :]
    ladder_factor = 1.0 - occupation[:, None] - occupation[None, :]
    polar_terms = screened * polar_factor[None]
    hop_first = jnp.dot(first_hot, hopping, precision=highest)
    hop_second = jnp.dot(second_hot, hopping, precision=highest)
    pair_hopping = (
        hop_first[:, :, None] * second_hot[:, None, :]
        + first_hot[:, :, None] * hop_second[:, None, :]
    )
    kernel_direct = (polar_terms + pair_hopping).astype(jnp.bfloat16).reshape(rows, pairs)
    kernel_polar = polar_terms.astype(jnp.bfloat16).reshape(rows, pairs)
    kernel_ladder = (screened * ladder_factor[None]).astype(jnp.bfloat16).reshape(rows, pairs)
    same_piece = lax.all_gather(green_same, "prow", axis=0, tiled=True)
    opp_piece = lax.all_gather(green_opp, "prow", axis=0, tiled=True)
    new_same = (
        product(kernel_direct, same_piece)
        + product(kernel_polar, opp_piece)
        + product(kernel_ladder, swap_orbitals(same_piece, orbitals))
    )
    new_opp = (
        product(kernel_direct, opp_piece)
        + product(kernel_polar, same_piece)
        + product(kernel_ladder, swap_orbitals(opp_piece, orbitals))
    )
    next_same = (green_same.astype(jnp.float32) + 0.5 * new_same).astype(jnp.bfloat16)
    next_opp = (green_opp.astype(jnp.float32) + 0.5 * new_opp).astype(jnp.bfloat16)
    share = jnp.dot(first_hot.T, new_same + new_opp, precision=highest) * (
        1.0 / math.sqrt(orbitals)
    )
    collision = lax.psum(share, "prow")
    return (new_same, new_opp, next_same, next_opp, collision)


def turn(unit, block):
    return lax.dot_general(
        unit, block, (((1,), (1,)), ((), ())), preferred_element_type=jnp.float32
    )


def build_body(orbitals, low, high, pairs, *refs):
    place_ref, inter_ref, pat_ref, hop_ref, occ_ref = refs[:5]
    pat4_ref, hop4_ref, eye4_ref, occ4_ref, unit_ref = refs[5:10]
    mixed_ref, polar_ref, turned_ref = refs[-3:]
    span = 4 * orbitals
    tiles = pairs // span
    start = place_ref[0]
    strips = range(0, high - low, 128)

    @pl.loop(0, tiles)
    def _(tile):
        cols = pl.ds(pl.multiple_of(tile * span, 128), span)
        turned = turn(unit_ref[...], inter_ref[:, cols])
        for strip in strips:
            size = min(128, high - low - strip)
            at = strip // 128 * pairs + tile * span
            turned_ref[pl.ds(pl.multiple_of(at, 128), span), :size] = turned[:, strip : strip + size]

    group = lax.broadcasted_iota(jnp.int32, (1, span), 1) // orbitals
    occ4 = occ4_ref[...]

    @pl.loop(0, tiles)
    def _(tile):
        cols = pl.ds(pl.multiple_of(tile * span, 128), span)

        def spread(values):
            row = jnp.where(group == 0, values[0], values[1])
            return jnp.where(group == 2, values[2], jnp.where(group == 3, values[3], row))

        inner = [4 * tile + m for m in range(4)]
        occ = spread([occ_ref[i] for i in inner])
        polar_factor = occ - occ4
        ladder_factor = (1.0 - occ4) - occ
        facts = {}
        for first in range(low // orbitals, -(-high // orbitals)):
            here = start + first
            linked = spread([pat_ref[here, i].astype(jnp.float32) for i in inner])
            hop_row = spread([hop_ref[here, i] for i in inner])
            unit = (group + 4 * tile == here).astype(jnp.float32)
            linked4 = pat4_ref[pl.ds(here, 1), :]
            facts[first] = (linked * polar_factor, linked4 * ladder_factor, hop_row, unit)
        sides = []
        for strip in strips:
            size = min(128, high - low - strip)
            pieces = [
                turned_ref[
                    pl.ds(strip // 128 * pairs + 4 * tile + m, orbitals, stride=orbitals), :
                ]
                for m in range(4)
            ]
            sides.append(jnp.concatenate(pieces, axis=0)[:, :size].astype(jnp.bfloat16))
        side = jnp.concatenate(sides, axis=1)
        block = turn(unit_ref[: high - low, : high - low], side)
        row = low
        while row < high:
            first, second = row // orbitals, row % orbitals
            count = min(orbitals - second, high - row)
            there = slice(row - low, row - low + count)
            polar_row, ladder_row, hop_row, unit = facts[first]
            polar = inter_ref[there, cols].astype(jnp.float32) * polar_row
            hop = (
                hop_row * eye4_ref[second : second + count]
                + unit * hop4_ref[second : second + count]
            )
            ladder = (block[there] * ladder_row).astype(jnp.bfloat16)
            direct = (polar + hop).astype(jnp.bfloat16).astype(jnp.float32)
            held = polar.astype(jnp.bfloat16)
            polar_ref[there, cols] = held
            mixed_ref[there, cols] = (
                direct - held.astype(jnp.float32) + ladder.astype(jnp.float32)
            ).astype(jnp.bfloat16)
            row += count


def build_rows(place, interaction, smalls, made, low, high):
    rows, pairs = interaction.shape
    pattern, hopping, occupation = smalls[:3]
    orbitals = hopping.shape[0]
    height = high - low
    block = low // height
    shape = jax.ShapeDtypeStruct((rows, pairs), jnp.bfloat16)
    wide = pl.BlockSpec((height, pairs), lambda g, p: (block, 0))
    smem = pl.BlockSpec(memory_space=pltpu.SMEM)
    row4 = pl.BlockSpec((1, 4 * orbitals), lambda g, p: (0, 0))
    small = pl.BlockSpec((orbitals, 4 * orbitals), lambda g, p: (0, 0))
    square = pl.BlockSpec((4 * orbitals, 4 * orbitals), lambda g, p: (0, 0))
    return pl.pallas_call(
        functools.partial(build_body, orbitals, low, high, pairs),
        grid_spec=pltpu.PrefetchScalarGridSpec(
            num_scalar_prefetch=1,
            grid=(1,),
            in_specs=[wide, smem, smem, smem, small, small, small, row4, square]
            + [pl.BlockSpec(memory_space=pl.ANY)] * len(made),
            out_specs=[wide] * 2,
            scratch_shapes=[pltpu.VMEM((-(-height // 128) * pairs, 128), jnp.float32)],
        ),
        out_shape=[shape] * 2,
        input_output_aliases={10 + n: n for n in range(len(made))},
        compiler_params=pltpu.CompilerParams(vmem_limit_bytes=44 * MIB),
        cost_estimate=pl.CostEstimate(flops=1024, bytes_accessed=1024, transcendentals=0),
        name="build_rows",
    )(place, interaction, *smalls, *made)


def step_body(parts, rows, opening, closing, orbitals, scale, *refs):
    place_ref = refs[0]
    refs = list(refs[1:])
    chips = len(parts)
    mixed_ref, polar_ref = refs.pop(0), refs.pop(0)
    greens = []
    for count in parts:
        pieces = [refs.pop(0) for _ in range(2 * count)]
        greens.append([pieces[:count], pieces[count:]])
    sums = [] if opening else [refs.pop(0) for _ in range(3)]
    olds = [refs.pop(0) for _ in range(2)] if closing else []
    held = refs.pop()
    totals = [refs.pop() for _ in range(3)][::-1] if closing else refs[:3]
    core = place_ref[0]
    span = greens[0][0][0].shape[1]
    now = pl.program_id(1)

    for chip in range(chips):

        @pl.when(now == chip)
        def _():
            for which in range(2):
                lane = core if which == 0 else 1 - core
                there = pl.ds(pl.multiple_of(lane * rows, 64), rows)
                pieces = greens[chip][which]
                same = pieces[0][:rows, :]
                opp = pieces[-1][pieces[-1].shape[0] - rows :, :]
                both = same.astype(jnp.float32) + opp.astype(jnp.float32)
                held[there, :span] = same
                held[there, span : 2 * span] = opp
                held[there, 2 * span :] = both.astype(jnp.bfloat16)

    @pl.when(now == 0)
    def _():
        for n in range(3):
            if opening:
                totals[n][...] = jnp.zeros_like(totals[n])
            else:
                totals[n][...] = sums[n][...]

    mixed = product(mixed_ref[...], held[:, : 2 * span])
    totals[0][...] += mixed[:, :span]
    totals[1][...] += mixed[:, span:]
    totals[2][...] += product(polar_ref[...], held[:, 2 * span :])
    if closing:

        @pl.when(now == chips - 1)
        def _():
            for first in range(rows // orbitals):
                part = slice(first * orbitals, (first + 1) * orbitals)
                shared = totals[2][part, :]
                both = None
                for kind in range(2):
                    slope = totals[kind][part, :] + shared
                    old = olds[kind][part, :].astype(jnp.float32)
                    refs[kind][part, :] = slope
                    refs[2 + kind][part, :] = (old + 0.5 * slope).astype(jnp.bfloat16)
                    both = slope if both is None else both + slope
                refs[4][first : first + 1, :] = jnp.sum(both, axis=0, keepdims=True) * scale


def step(place, low, mats, greens, sums, olds, orbitals):
    chips = len(greens)
    opening, closing = not sums, bool(olds)
    rows = mats[0].shape[0]
    width = greens[0][0][0].shape[1]
    parts = tuple(len(pair[0]) for pair in greens)
    wide = 2 * rows
    span = min(width, 256) if closing else width
    tall = pl.BlockSpec((rows, span), lambda n, g, p: (0, n))
    mat = pl.BlockSpec((rows, wide), lambda n, g, p: (0, p[1 + low + g]))
    wide_sum = jax.ShapeDtypeStruct((rows, width), jnp.float32)
    scratch = [pltpu.VMEM((wide, 3 * span), jnp.bfloat16)]
    if closing:
        out_specs = [tall] * 4 + [pl.BlockSpec((rows // orbitals, span), lambda n, g, p: (0, n))]
        out_shape = [wide_sum] * 2 + [jax.ShapeDtypeStruct((rows, width), jnp.bfloat16)] * 2
        out_shape += [jax.ShapeDtypeStruct((rows // orbitals, width), jnp.float32)]
        scratch = [pltpu.VMEM((rows, span), jnp.float32)] * 3 + scratch
    else:
        out_specs, out_shape = [tall] * 3, [wide_sum] * 3
    operands = list(mats)
    blocks = [block for pair in greens for side in pair for block in side]
    operands += blocks
    in_specs = [mat] * 2
    in_specs += [pl.BlockSpec((block.shape[0], span), lambda n, g, p: (0, n)) for block in blocks]
    aliases = {}
    if not opening:
        if not closing:
            aliases = {1 + len(operands) + n: n for n in range(3)}
        operands += list(sums)
        in_specs += [tall] * 3
    if closing:
        operands += list(olds)
        in_specs += [tall] * 2
    return pl.pallas_call(
        functools.partial(
            step_body, parts, rows, opening, closing, orbitals, 1.0 / math.sqrt(orbitals)
        ),
        grid_spec=pltpu.PrefetchScalarGridSpec(
            num_scalar_prefetch=1,
            grid=(width // span, chips),
            in_specs=in_specs,
            out_specs=out_specs,
            scratch_shapes=scratch,
        ),
        out_shape=out_shape,
        input_output_aliases=aliases,
        compiler_params=pltpu.CompilerParams(vmem_limit_bytes=48 * MIB),
        cost_estimate=pl.CostEstimate(flops=1024, bytes_accessed=1024, transcendentals=0),
        name="add_products",
    )(place, *operands)


def spread_blocks(block, index, stride, devices):
    blocks = [block]
    for other in range(1, 4):
        pairs_of = [(d, d ^ (other * stride)) for d in range(devices)]
        blocks.append(lax.ppermute(block, "prow", pairs_of))
    part = index // stride % 4
    low, high = part % 2 == 1, part // 2 == 1
    b = [jnp.where(low, blocks[n ^ 1], blocks[n]) for n in range(4)]
    b = [jnp.where(high, b[n ^ 2], b[n]) for n in range(4)]
    return jnp.concatenate(b, axis=0)


def after(value, *others):
    return lax.optimization_barrier((value, *others))[0]


def ring_form(green_same, green_opp, interaction, pattern, occupation, hopping):
    rows, width = green_same.shape
    orbitals = hopping.shape[0]
    pairs = orbitals * orbitals
    devices = pairs // rows
    chips = devices // 2
    me = lax.axis_index("prow")
    core, chip = me % 2, me // 2
    order = list(range(0, chips, 2)) + list(range(chips - 1, 0, -2))
    spot = [order.index(c) for c in range(chips)]
    ahead = [order[(spot[c] + 1) % chips] for c in range(chips)]
    right = [(2 * c + k, 2 * ahead[c] + k) for c in range(chips) for k in range(2)]
    left = [(b, a) for a, b in right]
    across = [(d, d ^ 1) for d in range(devices)]
    half = chips // 2
    table = []
    for c in range(chips):
        line = [c]
        for far in range(1, half + 1):
            line += [order[(spot[c] - far) % chips], order[(spot[c] + far) % chips]]
        table.append(line)
    line = lax.dynamic_index_in_dim(jnp.array(table, jnp.int32), chip, 0, keepdims=False)

    def send(block, pairs_of):
        return lax.ppermute(block, "prow", pairs_of)

    place = jnp.concatenate([core[None].astype(jnp.int32), line])
    own = jnp.concatenate([green_same, green_opp], axis=0)
    moving = [send(own, right), send(own, left)]
    near = send(own, across)

    start = (me * (rows // orbitals)).astype(jnp.int32)[None]
    smalls = (
        pattern,
        hopping,
        occupation,
        jnp.tile(pattern.astype(jnp.float32), (1, 4)),
        jnp.tile(hopping, (1, 4)),
        jnp.tile(jnp.eye(orbitals, dtype=jnp.float32), (1, 4)),
        jnp.tile(occupation, 4)[None],
        jnp.eye(4 * orbitals, dtype=jnp.bfloat16),
    )
    big = rows // 9 * 4
    mats = build_rows(start, interaction, smalls, (), 0, big)
    mats = build_rows(start, interaction, smalls, mats, big, 2 * big)

    greens, low, sums, done = [([own], [near])], 0, (), mats[0]
    for far in range(1, half):
        got = [after(block, done) for block in moving]
        if far < half - 1:
            moving = [send(got[0], right), send(got[1], left)]
        else:
            moving = [send(got[0][:rows], right), send(got[1][rows:], left)]
        passed = [([block], [send(block, across)]) for block in got]
        if far == 1:
            mats = build_rows(after(start, got[0]), interaction, smalls, mats, 2 * big, rows)
            greens += passed
        else:
            greens = passed
        sums = step(after(place, got[0]), low, mats, greens, sums, (), orbitals)
        low += len(greens)
        done = sums[0]
    last = [after(block, done) for block in moving]
    shared = [send(block, across) for block in last]
    new_same, new_opp, next_same, next_opp, part = step(
        place, low, mats, [(last, shared)], sums, (green_same, green_opp), orbitals
    )
    if devices == 16:
        collision = spread_blocks(spread_blocks(part, me, 1, devices), me, 4, devices)
    else:
        collision = lax.all_gather(part, "prow", axis=0, tiled=True)
    return (new_same, new_opp, next_same, next_opp, collision)


def per_device(green_same, green_opp, interaction, pattern, occupation, hopping):
    rows = green_same.shape[0]
    orbitals = hopping.shape[0]
    devices = orbitals * orbitals // rows
    fits = rows % orbitals == 0 and rows % 576 == 0 and devices % 4 == 0 and devices >= 12
    form = ring_form if fits else plain_form
    return form(green_same, green_opp, interaction, pattern, occupation, hopping)


def solution(mesh):
    placed = (
        P(("groups", "prow"), None),
        P(("groups", "prow"), None),
        P(("groups", "prow"), None),
        P("groups", None),
        P("groups"),
        P("groups", None),
    )
    return jax.shard_map(
        per_device,
        mesh=mesh,
        in_specs=placed,
        out_specs=(
            P(("groups", "prow"), None),
            P(("groups", "prow"), None),
            P(("groups", "prow"), None),
            P(("groups", "prow"), None),
            P("groups", None),
        ),
        check_vma=False,
    )
```

```python
import functools
import math

import jax
import jax.numpy as jnp
from jax import lax
from jax.experimental import pallas as pl
from jax.experimental.pallas import tpu as pltpu
from jax.sharding import PartitionSpec as P

MIB = 1 << 20


def swap_orbitals(block, orbitals):
    count = block.shape[1]
    return (
        block.reshape(orbitals, orbitals, count)
        .transpose(1, 0, 2)
        .reshape(orbitals * orbitals, count)
    )


def product(left, right):
    return jnp.dot(left, right, preferred_element_type=jnp.float32)


def plain_form(green_same, green_opp, interaction, pattern, occupation, hopping):
    rows, width = green_same.shape
    orbitals = hopping.shape[0]
    pairs = orbitals * orbitals
    highest = lax.Precision.HIGHEST
    row_ids = lax.axis_index("prow") * rows + jnp.arange(rows, dtype=jnp.int32)
    orbit_ids = jnp.arange(orbitals, dtype=jnp.int32)
    first_hot = (row_ids[:, None] // orbitals == orbit_ids[None, :]).astype(jnp.float32)
    second_hot = (row_ids[:, None] % orbitals == orbit_ids[None, :]).astype(jnp.float32)
    linked = jnp.dot(first_hot, pattern.astype(jnp.float32), precision=highest)
    screened = (
        interaction.astype(jnp.float32).reshape(rows, orbitals, orbitals) * linked[:, :, None]
    )
    polar_factor = occupation[:, None] - occupation[None, :]
    ladder_factor = 1.0 - occupation[:, None] - occupation[None, :]
    polar_terms = screened * polar_factor[None]
    hop_first = jnp.dot(first_hot, hopping, precision=highest)
    hop_second = jnp.dot(second_hot, hopping, precision=highest)
    pair_hopping = (
        hop_first[:, :, None] * second_hot[:, None, :]
        + first_hot[:, :, None] * hop_second[:, None, :]
    )
    kernel_direct = (polar_terms + pair_hopping).astype(jnp.bfloat16).reshape(rows, pairs)
    kernel_polar = polar_terms.astype(jnp.bfloat16).reshape(rows, pairs)
    kernel_ladder = (screened * ladder_factor[None]).astype(jnp.bfloat16).reshape(rows, pairs)
    same_piece = lax.all_gather(green_same, "prow", axis=0, tiled=True)
    opp_piece = lax.all_gather(green_opp, "prow", axis=0, tiled=True)
    new_same = (
        product(kernel_direct, same_piece)
        + product(kernel_polar, opp_piece)
        + product(kernel_ladder, swap_orbitals(same_piece, orbitals))
    )
    new_opp = (
        product(kernel_direct, opp_piece)
        + product(kernel_polar, same_piece)
        + product(kernel_ladder, swap_orbitals(opp_piece, orbitals))
    )
    next_same = (green_same.astype(jnp.float32) + 0.5 * new_same).astype(jnp.bfloat16)
    next_opp = (green_opp.astype(jnp.float32) + 0.5 * new_opp).astype(jnp.bfloat16)
    share = jnp.dot(first_hot.T, new_same + new_opp, precision=highest) * (
        1.0 / math.sqrt(orbitals)
    )
    collision = lax.psum(share, "prow")
    return (new_same, new_opp, next_same, next_opp, collision)


def build_body(orbitals, low, high, pairs, *refs):
    place_ref, inter_ref, pat_ref, hop_ref, occ_ref = refs[:5]
    pat4_ref, hop4_ref, eye4_ref, occ4_ref = refs[5:9]
    mixed_ref, polar_ref, turned_ref = refs[-3:]
    span = 4 * orbitals
    tiles = pairs // span
    start = place_ref[0]
    strips = range(0, high - low, 128)

    pitch = orbitals + 1
    room = orbitals * pitch

    @pl.loop(0, tiles // 2)
    def _(tile):
        cols = pl.ds(pl.multiple_of(tile * 2 * span, 128), 2 * span)
        for strip in strips:
            size = min(128, high - low - strip)
            turned = inter_ref[strip : strip + size, cols].astype(jnp.float32).T
            at = pl.multiple_of(strip // 128 * room + tile * 8 * pitch, 8)
            for m in range(8):
                there = pl.ds(at + m * pitch, orbitals)
                turned_ref[there, :size] = turned[m * orbitals : (m + 1) * orbitals]

    group = lax.broadcasted_iota(jnp.int32, (1, span), 1) // orbitals
    occ4 = occ4_ref[...]

    @pl.loop(0, tiles)
    def _(tile):
        cols = pl.ds(pl.multiple_of(tile * span, 128), span)

        def spread(values):
            row = jnp.where(group == 0, values[0], values[1])
            return jnp.where(group == 2, values[2], jnp.where(group == 3, values[3], row))

        inner = [4 * tile + m for m in range(4)]
        occ = spread([occ_ref[i] for i in inner])
        polar_factor = occ - occ4
        ladder_factor = (1.0 - occ4) - occ
        facts = {}
        for first in range(low // orbitals, -(-high // orbitals)):
            here = start + first
            linked = spread([pat_ref[here, i].astype(jnp.float32) for i in inner])
            hop_row = spread([hop_ref[here, i] for i in inner])
            unit = (group + 4 * tile == here).astype(jnp.float32)
            linked4 = pat4_ref[pl.ds(here, 1), :]
            facts[first] = (linked * polar_factor, linked4 * ladder_factor, hop_row, unit)
        blocks = []
        for strip in strips:
            size = min(128, high - low - strip)
            pieces = [
                turned_ref[
                    pl.ds(strip // 128 * room + 4 * tile + m, orbitals, stride=pitch), :
                ]
                for m in range(4)
            ]
            blocks.append(jnp.concatenate(pieces, axis=0).T[:size])
        block = jnp.concatenate(blocks, axis=0)
        row = low
        while row < high:
            first, second = row // orbitals, row % orbitals
            count = min(orbitals - second, high - row)
            there = slice(row - low, row - low + count)
            polar_row, ladder_row, hop_row, unit = facts[first]
            polar = inter_ref[there, cols].astype(jnp.float32) * polar_row
            hop = (
                hop_row * eye4_ref[second : second + count]
                + unit * hop4_ref[second : second + count]
            )
            ladder = (block[there] * ladder_row).astype(jnp.bfloat16)
            direct = (polar + hop).astype(jnp.bfloat16).astype(jnp.float32)
            held = polar.astype(jnp.bfloat16)
            polar_ref[there, cols] = held
            mixed_ref[there, cols] = (
                direct - held.astype(jnp.float32) + ladder.astype(jnp.float32)
            ).astype(jnp.bfloat16)
            row += count


def build_rows(place, interaction, smalls, made, low, high):
    rows, pairs = interaction.shape
    pattern, hopping, occupation = smalls[:3]
    orbitals = hopping.shape[0]
    height = high - low
    block = low // height
    shape = jax.ShapeDtypeStruct((rows, pairs), jnp.bfloat16)
    wide = pl.BlockSpec((height, pairs), lambda g, p: (block, 0))
    smem = pl.BlockSpec(memory_space=pltpu.SMEM)
    row4 = pl.BlockSpec((1, 4 * orbitals), lambda g, p: (0, 0))
    small = pl.BlockSpec((orbitals, 4 * orbitals), lambda g, p: (0, 0))
    return pl.pallas_call(
        functools.partial(build_body, orbitals, low, high, pairs),
        grid_spec=pltpu.PrefetchScalarGridSpec(
            num_scalar_prefetch=1,
            grid=(1,),
            in_specs=[wide, smem, smem, smem, small, small, small, row4]
            + [pl.BlockSpec(memory_space=pl.ANY)] * len(made),
            out_specs=[wide] * 2,
            scratch_shapes=[pltpu.VMEM((-(-height // 128) * orbitals * (orbitals + 1), 128), jnp.float32)],
        ),
        out_shape=[shape] * 2,
        input_output_aliases={9 + n: n for n in range(len(made))},
        compiler_params=pltpu.CompilerParams(vmem_limit_bytes=44 * MIB),
        cost_estimate=pl.CostEstimate(flops=1024, bytes_accessed=1024, transcendentals=0),
        name="build_rows",
    )(place, interaction, *smalls, *made)


def step_body(parts, rows, opening, closing, orbitals, scale, *refs):
    place_ref = refs[0]
    refs = list(refs[1:])
    chips = len(parts)
    mixed_ref, polar_ref = refs.pop(0), refs.pop(0)
    greens = []
    for count in parts:
        pieces = [refs.pop(0) for _ in range(2 * count)]
        greens.append([pieces[:count], pieces[count:]])
    sums = [] if opening else [refs.pop(0) for _ in range(3)]
    olds = [refs.pop(0) for _ in range(2)] if closing else []
    held = refs.pop()
    totals = [refs.pop() for _ in range(3)][::-1] if closing else refs[:3]
    core = place_ref[0]
    span = greens[0][0][0].shape[1]
    now = pl.program_id(1)

    for chip in range(chips):

        @pl.when(now == chip)
        def _():
            for which in range(2):
                lane = core if which == 0 else 1 - core
                there = pl.ds(pl.multiple_of(lane * rows, 64), rows)
                pieces = greens[chip][which]
                same = pieces[0][:rows, :]
                opp = pieces[-1][pieces[-1].shape[0] - rows :, :]
                both = same.astype(jnp.float32) + opp.astype(jnp.float32)
                held[there, :span] = same
                held[there, span : 2 * span] = opp
                held[there, 2 * span :] = both.astype(jnp.bfloat16)

    @pl.when(now == 0)
    def _():
        for n in range(3):
            if opening:
                totals[n][...] = jnp.zeros_like(totals[n])
            else:
                totals[n][...] = sums[n][...]

    mixed = product(mixed_ref[...], held[:, : 2 * span])
    totals[0][...] += mixed[:, :span]
    totals[1][...] += mixed[:, span:]
    totals[2][...] += product(polar_ref[...], held[:, 2 * span :])
    if closing:

        @pl.when(now == chips - 1)
        def _():
            for first in range(rows // orbitals):
                part = slice(first * orbitals, (first + 1) * orbitals)
                shared = totals[2][part, :]
                both = None
                for kind in range(2):
                    slope = totals[kind][part, :] + shared
                    old = olds[kind][part, :].astype(jnp.float32)
                    refs[kind][part, :] = slope
                    refs[2 + kind][part, :] = (old + 0.5 * slope).astype(jnp.bfloat16)
                    both = slope if both is None else both + slope
                refs[4][first : first + 1, :] = jnp.sum(both, axis=0, keepdims=True) * scale


def step(place, low, mats, greens, sums, olds, orbitals):
    chips = len(greens)
    opening, closing = not sums, bool(olds)
    rows = mats[0].shape[0]
    width = greens[0][0][0].shape[1]
    parts = tuple(len(pair[0]) for pair in greens)
    wide = 2 * rows
    span = min(width, 256) if closing else width
    tall = pl.BlockSpec((rows, span), lambda n, g, p: (0, n))
    mat = pl.BlockSpec((rows, wide), lambda n, g, p: (0, p[1 + low + g]))
    wide_sum = jax.ShapeDtypeStruct((rows, width), jnp.float32)
    scratch = [pltpu.VMEM((wide, 3 * span), jnp.bfloat16)]
    if closing:
        out_specs = [tall] * 4 + [pl.BlockSpec((rows // orbitals, span), lambda n, g, p: (0, n))]
        out_shape = [wide_sum] * 2 + [jax.ShapeDtypeStruct((rows, width), jnp.bfloat16)] * 2
        out_shape += [jax.ShapeDtypeStruct((rows // orbitals, width), jnp.float32)]
        scratch = [pltpu.VMEM((rows, span), jnp.float32)] * 3 + scratch
    else:
        out_specs, out_shape = [tall] * 3, [wide_sum] * 3
    operands = list(mats)
    blocks = [block for pair in greens for side in pair for block in side]
    operands += blocks
    in_specs = [mat] * 2
    in_specs += [pl.BlockSpec((block.shape[0], span), lambda n, g, p: (0, n)) for block in blocks]
    aliases = {}
    if not opening:
        if not closing:
            aliases = {1 + len(operands) + n: n for n in range(3)}
        operands += list(sums)
        in_specs += [tall] * 3
    if closing:
        operands += list(olds)
        in_specs += [tall] * 2
    return pl.pallas_call(
        functools.partial(
            step_body, parts, rows, opening, closing, orbitals, 1.0 / math.sqrt(orbitals)
        ),
        grid_spec=pltpu.PrefetchScalarGridSpec(
            num_scalar_prefetch=1,
            grid=(width // span, chips),
            in_specs=in_specs,
            out_specs=out_specs,
            scratch_shapes=scratch,
        ),
        out_shape=out_shape,
        input_output_aliases=aliases,
        compiler_params=pltpu.CompilerParams(vmem_limit_bytes=48 * MIB),
        cost_estimate=pl.CostEstimate(flops=1024, bytes_accessed=1024, transcendentals=0),
        name="add_products",
    )(place, *operands)


def spread_blocks(block, index, stride, devices):
    blocks = [block]
    for other in range(1, 4):
        pairs_of = [(d, d ^ (other * stride)) for d in range(devices)]
        blocks.append(lax.ppermute(block, "prow", pairs_of))
    part = index // stride % 4
    low, high = part % 2 == 1, part // 2 == 1
    b = [jnp.where(low, blocks[n ^ 1], blocks[n]) for n in range(4)]
    b = [jnp.where(high, b[n ^ 2], b[n]) for n in range(4)]
    return jnp.concatenate(b, axis=0)


def after(value, *others):
    return lax.optimization_barrier((value, *others))[0]


def ring_form(green_same, green_opp, interaction, pattern, occupation, hopping):
    rows, width = green_same.shape
    orbitals = hopping.shape[0]
    pairs = orbitals * orbitals
    devices = pairs // rows
    chips = devices // 2
    me = lax.axis_index("prow")
    core, chip = me % 2, me // 2
    order = list(range(0, chips, 2)) + list(range(chips - 1, 0, -2))
    spot = [order.index(c) for c in range(chips)]
    ahead = [order[(spot[c] + 1) % chips] for c in range(chips)]
    right = [(2 * c + k, 2 * ahead[c] + k) for c in range(chips) for k in range(2)]
    left = [(b, a) for a, b in right]
    across = [(d, d ^ 1) for d in range(devices)]
    half = chips // 2
    table = []
    for c in range(chips):
        line = [c]
        for far in range(1, half + 1):
            line += [order[(spot[c] - far) % chips], order[(spot[c] + far) % chips]]
        table.append(line)
    line = lax.dynamic_index_in_dim(jnp.array(table, jnp.int32), chip, 0, keepdims=False)

    def send(block, pairs_of):
        return lax.ppermute(block, "prow", pairs_of)

    place = jnp.concatenate([core[None].astype(jnp.int32), line])
    own = jnp.concatenate([green_same, green_opp], axis=0)
    moving = [send(own, right), send(own, left)]
    near = send(own, across)

    start = (me * (rows // orbitals)).astype(jnp.int32)[None]
    smalls = (
        pattern,
        hopping,
        occupation,
        jnp.tile(pattern.astype(jnp.float32), (1, 4)),
        jnp.tile(hopping, (1, 4)),
        jnp.tile(jnp.eye(orbitals, dtype=jnp.float32), (1, 4)),
        jnp.tile(occupation, 4)[None],
    )
    big = rows // 9 * 4
    mats = build_rows(start, interaction, smalls, (), 0, big)
    mats = build_rows(start, interaction, smalls, mats, big, 2 * big)

    greens, low, sums, done = [([own], [near])], 0, (), mats[0]
    for far in range(1, half):
        got = [after(block, done) for block in moving]
        if far < half - 1:
            moving = [send(got[0], right), send(got[1], left)]
        else:
            moving = [send(got[0][:rows], right), send(got[1][rows:], left)]
        passed = [([block], [send(block, across)]) for block in got]
        if far == 1:
            mats = build_rows(after(start, got[0]), interaction, smalls, mats, 2 * big, rows)
            greens += passed
        else:
            greens = passed
        sums = step(after(place, got[0]), low, mats, greens, sums, (), orbitals)
        low += len(greens)
        done = sums[0]
    last = [after(block, done) for block in moving]
    shared = [send(block, across) for block in last]
    new_same, new_opp, next_same, next_opp, part = step(
        place, low, mats, [(last, shared)], sums, (green_same, green_opp), orbitals
    )
    if devices == 16:
        collision = spread_blocks(spread_blocks(part, me, 1, devices), me, 4, devices)
    else:
        collision = lax.all_gather(part, "prow", axis=0, tiled=True)
    return (new_same, new_opp, next_same, next_opp, collision)


def per_device(green_same, green_opp, interaction, pattern, occupation, hopping):
    rows = green_same.shape[0]
    orbitals = hopping.shape[0]
    devices = orbitals * orbitals // rows
    fits = rows % orbitals == 0 and rows % 576 == 0 and devices % 4 == 0 and devices >= 12
    form = ring_form if fits else plain_form
    return form(green_same, green_opp, interaction, pattern, occupation, hopping)


def solution(mesh):
    placed = (
        P(("groups", "prow"), None),
        P(("groups", "prow"), None),
        P(("groups", "prow"), None),
        P("groups", None),
        P("groups"),
        P("groups", None),
    )
    return jax.shard_map(
        per_device,
        mesh=mesh,
        in_specs=placed,
        out_specs=(
            P(("groups", "prow"), None),
            P(("groups", "prow"), None),
            P(("groups", "prow"), None),
            P(("groups", "prow"), None),
            P("groups", None),
        ),
        check_vma=False,
    )
```

```python
import functools
import math

import jax
import jax.numpy as jnp
from jax import lax
from jax.experimental import pallas as pl
from jax.experimental.pallas import tpu as pltpu
from jax.sharding import PartitionSpec as P

MIB = 1 << 20


def swap_orbitals(block, orbitals):
    count = block.shape[1]
    return (
        block.reshape(orbitals, orbitals, count)
        .transpose(1, 0, 2)
        .reshape(orbitals * orbitals, count)
    )


def product(left, right):
    return jnp.dot(left, right, preferred_element_type=jnp.float32)


def plain_form(green_same, green_opp, interaction, pattern, occupation, hopping):
    rows, width = green_same.shape
    orbitals = hopping.shape[0]
    pairs = orbitals * orbitals
    highest = lax.Precision.HIGHEST
    row_ids = lax.axis_index("prow") * rows + jnp.arange(rows, dtype=jnp.int32)
    orbit_ids = jnp.arange(orbitals, dtype=jnp.int32)
    first_hot = (row_ids[:, None] // orbitals == orbit_ids[None, :]).astype(jnp.float32)
    second_hot = (row_ids[:, None] % orbitals == orbit_ids[None, :]).astype(jnp.float32)
    linked = jnp.dot(first_hot, pattern.astype(jnp.float32), precision=highest)
    screened = (
        interaction.astype(jnp.float32).reshape(rows, orbitals, orbitals) * linked[:, :, None]
    )
    polar_factor = occupation[:, None] - occupation[None, :]
    ladder_factor = 1.0 - occupation[:, None] - occupation[None, :]
    polar_terms = screened * polar_factor[None]
    hop_first = jnp.dot(first_hot, hopping, precision=highest)
    hop_second = jnp.dot(second_hot, hopping, precision=highest)
    pair_hopping = (
        hop_first[:, :, None] * second_hot[:, None, :]
        + first_hot[:, :, None] * hop_second[:, None, :]
    )
    kernel_direct = (polar_terms + pair_hopping).astype(jnp.bfloat16).reshape(rows, pairs)
    kernel_polar = polar_terms.astype(jnp.bfloat16).reshape(rows, pairs)
    kernel_ladder = (screened * ladder_factor[None]).astype(jnp.bfloat16).reshape(rows, pairs)
    same_piece = lax.all_gather(green_same, "prow", axis=0, tiled=True)
    opp_piece = lax.all_gather(green_opp, "prow", axis=0, tiled=True)
    new_same = (
        product(kernel_direct, same_piece)
        + product(kernel_polar, opp_piece)
        + product(kernel_ladder, swap_orbitals(same_piece, orbitals))
    )
    new_opp = (
        product(kernel_direct, opp_piece)
        + product(kernel_polar, same_piece)
        + product(kernel_ladder, swap_orbitals(opp_piece, orbitals))
    )
    next_same = (green_same.astype(jnp.float32) + 0.5 * new_same).astype(jnp.bfloat16)
    next_opp = (green_opp.astype(jnp.float32) + 0.5 * new_opp).astype(jnp.bfloat16)
    share = jnp.dot(first_hot.T, new_same + new_opp, precision=highest) * (
        1.0 / math.sqrt(orbitals)
    )
    collision = lax.psum(share, "prow")
    return (new_same, new_opp, next_same, next_opp, collision)


def build_body(orbitals, low, high, pairs, only, *refs):
    place_ref, inter_ref, pat_ref, hop_ref, occ_ref = refs[:5]
    pat4_ref, hop4_ref, eye4_ref, occ4_ref = refs[5:9]
    mixed_ref, polar_ref, turned_ref = refs[-3:]
    span = 4 * orbitals
    tiles = pairs // span
    start = place_ref[0]
    strips = range(0, high - low, 128)
    if only is not None:
        kept = refs[9:-3]

        @pl.when(place_ref[1] == only)
        def _():
            build_body(orbitals, low, high, pairs, None, *refs)

        if kept:

            @pl.when(place_ref[1] != only)
            def _():
                mixed_ref[...] = kept[0][...]
                polar_ref[...] = kept[1][...]

        return

    pitch = orbitals + 1
    room = orbitals * pitch

    @pl.loop(0, tiles // 2)
    def _(tile):
        cols = pl.ds(pl.multiple_of(tile * 2 * span, 128), 2 * span)
        for strip in strips:
            size = min(128, high - low - strip)
            turned = inter_ref[strip : strip + size, cols].astype(jnp.float32).T
            at = pl.multiple_of(strip // 128 * room + tile * 8 * pitch, 8)
            for m in range(8):
                there = pl.ds(at + m * pitch, orbitals)
                turned_ref[there, :size] = turned[m * orbitals : (m + 1) * orbitals]

    group = lax.broadcasted_iota(jnp.int32, (1, span), 1) // orbitals
    occ4 = occ4_ref[...]

    @pl.loop(0, tiles)
    def _(tile):
        cols = pl.ds(pl.multiple_of(tile * span, 128), span)

        def spread(values):
            row = jnp.where(group == 0, values[0], values[1])
            return jnp.where(group == 2, values[2], jnp.where(group == 3, values[3], row))

        inner = [4 * tile + m for m in range(4)]
        occ = spread([occ_ref[i] for i in inner])
        polar_factor = occ - occ4
        ladder_factor = (1.0 - occ4) - occ
        facts = {}
        for first in range(low // orbitals, -(-high // orbitals)):
            here = start + first
            linked = spread([pat_ref[here, i].astype(jnp.float32) for i in inner])
            hop_row = spread([hop_ref[here, i] for i in inner])
            unit = (group + 4 * tile == here).astype(jnp.float32)
            linked4 = pat4_ref[pl.ds(here, 1), :]
            facts[first] = (linked * polar_factor, linked4 * ladder_factor, hop_row, unit)
        blocks = []
        for strip in strips:
            size = min(128, high - low - strip)
            pieces = [
                turned_ref[
                    pl.ds(strip // 128 * room + 4 * tile + m, orbitals, stride=pitch), :
                ]
                for m in range(4)
            ]
            blocks.append(jnp.concatenate(pieces, axis=0).T[:size])
        block = jnp.concatenate(blocks, axis=0)
        row = low
        while row < high:
            first, second = row // orbitals, row % orbitals
            count = min(orbitals - second, high - row)
            there = slice(row - low, row - low + count)
            polar_row, ladder_row, hop_row, unit = facts[first]
            polar = inter_ref[there, cols].astype(jnp.float32) * polar_row
            hop = (
                hop_row * eye4_ref[second : second + count]
                + unit * hop4_ref[second : second + count]
            )
            ladder = (block[there] * ladder_row).astype(jnp.bfloat16)
            direct = (polar + hop).astype(jnp.bfloat16).astype(jnp.float32)
            held = polar.astype(jnp.bfloat16)
            polar_ref[there, cols] = held
            mixed_ref[there, cols] = (
                direct - held.astype(jnp.float32) + ladder.astype(jnp.float32)
            ).astype(jnp.bfloat16)
            row += count


def build_rows(place, interaction, smalls, made, low, high, only=None):
    rows, pairs = interaction.shape
    pattern, hopping, occupation = smalls[:3]
    orbitals = hopping.shape[0]
    height = high - low
    block = low // height
    shape = jax.ShapeDtypeStruct((rows, pairs), jnp.bfloat16)
    wide = pl.BlockSpec((height, pairs), lambda g, p: (block, 0))
    smem = pl.BlockSpec(memory_space=pltpu.SMEM)
    row4 = pl.BlockSpec((1, 4 * orbitals), lambda g, p: (0, 0))
    small = pl.BlockSpec((orbitals, 4 * orbitals), lambda g, p: (0, 0))
    return pl.pallas_call(
        functools.partial(build_body, orbitals, low, high, pairs, only),
        grid_spec=pltpu.PrefetchScalarGridSpec(
            num_scalar_prefetch=1,
            grid=(1,),
            in_specs=[wide, smem, smem, smem, small, small, small, row4]
            + [pl.BlockSpec(memory_space=pl.ANY) if only is None else wide] * len(made),
            out_specs=[wide] * 2,
            scratch_shapes=[pltpu.VMEM((-(-height // 128) * orbitals * (orbitals + 1), 128), jnp.float32)],
        ),
        out_shape=[shape] * 2,
        input_output_aliases={9 + n: n for n in range(len(made))},
        compiler_params=pltpu.CompilerParams(vmem_limit_bytes=44 * MIB),
        cost_estimate=pl.CostEstimate(flops=1024, bytes_accessed=1024, transcendentals=0),
        name="build_rows",
    )(place, interaction, *smalls, *made)


def step_body(parts, rows, opening, closing, orbitals, scale, *refs):
    place_ref = refs[0]
    refs = list(refs[1:])
    chips = len(parts)
    mixed_ref, polar_ref = refs.pop(0), refs.pop(0)
    greens = []
    for count in parts:
        pieces = [refs.pop(0) for _ in range(2 * count)]
        greens.append([pieces[:count], pieces[count:]])
    sums = [] if opening else [refs.pop(0) for _ in range(3)]
    olds = [refs.pop(0) for _ in range(2)] if closing else []
    held = refs.pop()
    totals = [refs.pop() for _ in range(3)][::-1] if closing else refs[:3]
    core = place_ref[0]
    span = greens[0][0][0].shape[1]
    now = pl.program_id(1)

    for chip in range(chips):

        @pl.when(now == chip)
        def _():
            for which in range(2):
                lane = core if which == 0 else 1 - core
                there = pl.ds(pl.multiple_of(lane * rows, 64), rows)
                pieces = greens[chip][which]
                same = pieces[0][:rows, :]
                opp = pieces[-1][pieces[-1].shape[0] - rows :, :]
                both = same.astype(jnp.float32) + opp.astype(jnp.float32)
                held[there, :span] = same
                held[there, span : 2 * span] = opp
                held[there, 2 * span :] = both.astype(jnp.bfloat16)

    @pl.when(now == 0)
    def _():
        for n in range(3):
            if opening:
                totals[n][...] = jnp.zeros_like(totals[n])
            else:
                totals[n][...] = sums[n][...]

    mixed = product(mixed_ref[...], held[:, : 2 * span])
    totals[0][...] += mixed[:, :span]
    totals[1][...] += mixed[:, span:]
    totals[2][...] += product(polar_ref[...], held[:, 2 * span :])
    if closing:

        @pl.when(now == chips - 1)
        def _():
            for first in range(rows // orbitals):
                part = slice(first * orbitals, (first + 1) * orbitals)
                shared = totals[2][part, :]
                both = None
                for kind in range(2):
                    slope = totals[kind][part, :] + shared
                    old = olds[kind][part, :].astype(jnp.float32)
                    refs[kind][part, :] = slope
                    refs[2 + kind][part, :] = (old + 0.5 * slope).astype(jnp.bfloat16)
                    both = slope if both is None else both + slope
                refs[4][first : first + 1, :] = jnp.sum(both, axis=0, keepdims=True) * scale


def step(place, low, mats, greens, sums, olds, orbitals):
    chips = len(greens)
    opening, closing = not sums, bool(olds)
    rows = mats[0].shape[0]
    width = greens[0][0][0].shape[1]
    parts = tuple(len(pair[0]) for pair in greens)
    wide = 2 * rows
    span = min(width, 256) if closing else width
    tall = pl.BlockSpec((rows, span), lambda n, g, p: (0, n))
    mat = pl.BlockSpec((rows, wide), lambda n, g, p: (0, p[1 + low + g]))
    wide_sum = jax.ShapeDtypeStruct((rows, width), jnp.float32)
    scratch = [pltpu.VMEM((wide, 3 * span), jnp.bfloat16)]
    if closing:
        out_specs = [tall] * 4 + [pl.BlockSpec((rows // orbitals, span), lambda n, g, p: (0, n))]
        out_shape = [wide_sum] * 2 + [jax.ShapeDtypeStruct((rows, width), jnp.bfloat16)] * 2
        out_shape += [jax.ShapeDtypeStruct((rows // orbitals, width), jnp.float32)]
        scratch = [pltpu.VMEM((rows, span), jnp.float32)] * 3 + scratch
    else:
        out_specs, out_shape = [tall] * 3, [wide_sum] * 3
    operands = list(mats)
    blocks = [block for pair in greens for side in pair for block in side]
    operands += blocks
    in_specs = [mat] * 2
    in_specs += [pl.BlockSpec((block.shape[0], span), lambda n, g, p: (0, n)) for block in blocks]
    aliases = {}
    if not opening:
        if not closing:
            aliases = {1 + len(operands) + n: n for n in range(3)}
        operands += list(sums)
        in_specs += [tall] * 3
    if closing:
        operands += list(olds)
        in_specs += [tall] * 2
    return pl.pallas_call(
        functools.partial(
            step_body, parts, rows, opening, closing, orbitals, 1.0 / math.sqrt(orbitals)
        ),
        grid_spec=pltpu.PrefetchScalarGridSpec(
            num_scalar_prefetch=1,
            grid=(width // span, chips),
            in_specs=in_specs,
            out_specs=out_specs,
            scratch_shapes=scratch,
        ),
        out_shape=out_shape,
        input_output_aliases=aliases,
        compiler_params=pltpu.CompilerParams(vmem_limit_bytes=48 * MIB),
        cost_estimate=pl.CostEstimate(flops=1024, bytes_accessed=1024, transcendentals=0),
        name="add_products",
    )(place, *operands)


def spread_blocks(block, index, stride, devices):
    blocks = [block]
    for other in range(1, 4):
        pairs_of = [(d, d ^ (other * stride)) for d in range(devices)]
        blocks.append(lax.ppermute(block, "prow", pairs_of))
    part = index // stride % 4
    low, high = part % 2 == 1, part // 2 == 1
    b = [jnp.where(low, blocks[n ^ 1], blocks[n]) for n in range(4)]
    b = [jnp.where(high, b[n ^ 2], b[n]) for n in range(4)]
    return jnp.concatenate(b, axis=0)


def after(value, *others):
    return lax.optimization_barrier((value, *others))[0]


def ring_form(green_same, green_opp, interaction, pattern, occupation, hopping):
    rows, width = green_same.shape
    orbitals = hopping.shape[0]
    pairs = orbitals * orbitals
    devices = pairs // rows
    chips = devices // 2
    me = lax.axis_index("prow")
    core, chip = me % 2, me // 2
    order = list(range(0, chips, 2)) + list(range(chips - 1, 0, -2))
    spot = [order.index(c) for c in range(chips)]
    ahead = [order[(spot[c] + 1) % chips] for c in range(chips)]
    right = [(2 * c + k, 2 * ahead[c] + k) for c in range(chips) for k in range(2)]
    left = [(b, a) for a, b in right]
    across = [(d, d ^ 1) for d in range(devices)]
    half = chips // 2
    table = []
    for c in range(chips):
        line = [c]
        for far in range(1, half + 1):
            line += [order[(spot[c] - far) % chips], order[(spot[c] + far) % chips]]
        table.append(line)
    line = lax.dynamic_index_in_dim(jnp.array(table, jnp.int32), chip, 0, keepdims=False)

    def send(block, pairs_of):
        return lax.ppermute(block, "prow", pairs_of)

    place = jnp.concatenate([core[None].astype(jnp.int32), line])
    start = jnp.stack([me * (rows // orbitals), core]).astype(jnp.int32)
    smalls = (
        pattern,
        hopping,
        occupation,
        jnp.tile(pattern.astype(jnp.float32), (1, 4)),
        jnp.tile(hopping, (1, 4)),
        jnp.tile(jnp.eye(orbitals, dtype=jnp.float32), (1, 4)),
        jnp.tile(occupation, 4)[None],
    )
    big = rows // 9 * 4
    mats = build_rows(start, interaction, smalls, (), 2 * big, rows, only=1)
    own = after(jnp.concatenate([green_same, green_opp], axis=0), mats[0])
    moving = [send(own, right), send(own, left)]
    near = send(own, across)
    mats = build_rows(after(start, own), interaction, smalls, mats, 0, big)

    chips_in, low, sums, done = [([own], [near])], 0, (), mats[0]
    for far in range(1, half):
        got = [after(block, done) for block in moving]
        if far < half - 1:
            moving = [send(got[0], right), send(got[1], left)]
        else:
            moving = [send(got[0][:rows], right), send(got[1][rows:], left)]
        passed = [([block], [send(block, across)]) for block in got]
        if far == 1:
            mats = build_rows(after(start, got[0]), interaction, smalls, mats, big, 2 * big)
            mats = build_rows(start, interaction, smalls, mats, 2 * big, rows, only=0)
            chips_in += passed
            done = mats[0]
            continue
        if far == 2:
            sums = step(after(place, got[0]), low, mats, chips_in, sums, (), orbitals)
            low += len(chips_in)
        sums = step(after(place, got[0]), low, mats, passed, sums, (), orbitals)
        low += len(passed)
        done = sums[0]
    last = [after(block, done) for block in moving]
    shared = [send(block, across) for block in last]
    new_same, new_opp, next_same, next_opp, part = step(
        place, low, mats, [(last, shared)], sums, (green_same, green_opp), orbitals
    )
    if devices == 16:
        collision = spread_blocks(spread_blocks(part, me, 1, devices), me, 4, devices)
    else:
        collision = lax.all_gather(part, "prow", axis=0, tiled=True)
    return (new_same, new_opp, next_same, next_opp, collision)


def per_device(green_same, green_opp, interaction, pattern, occupation, hopping):
    rows = green_same.shape[0]
    orbitals = hopping.shape[0]
    devices = orbitals * orbitals // rows
    fits = rows % orbitals == 0 and rows % 576 == 0 and devices % 4 == 0 and devices >= 12
    form = ring_form if fits else plain_form
    return form(green_same, green_opp, interaction, pattern, occupation, hopping)


def solution(mesh):
    placed = (
        P(("groups", "prow"), None),
        P(("groups", "prow"), None),
        P(("groups", "prow"), None),
        P("groups", None),
        P("groups"),
        P("groups", None),
    )
    return jax.shard_map(
        per_device,
        mesh=mesh,
        in_specs=placed,
        out_specs=(
            P(("groups", "prow"), None),
            P(("groups", "prow"), None),
            P(("groups", "prow"), None),
            P(("groups", "prow"), None),
            P("groups", None),
        ),
        check_vma=False,
    )
```

```python
import functools
import math

import jax
import jax.numpy as jnp
from jax import lax
from jax.experimental import pallas as pl
from jax.experimental.pallas import tpu as pltpu
from jax.sharding import PartitionSpec as P

MIB = 1 << 20


def swap_orbitals(block, orbitals):
    count = block.shape[1]
    return (
        block.reshape(orbitals, orbitals, count)
        .transpose(1, 0, 2)
        .reshape(orbitals * orbitals, count)
    )


def product(left, right):
    return jnp.dot(left, right, preferred_element_type=jnp.float32)


def plain_form(green_same, green_opp, interaction, pattern, occupation, hopping):
    rows, width = green_same.shape
    orbitals = hopping.shape[0]
    pairs = orbitals * orbitals
    highest = lax.Precision.HIGHEST
    row_ids = lax.axis_index("prow") * rows + jnp.arange(rows, dtype=jnp.int32)
    orbit_ids = jnp.arange(orbitals, dtype=jnp.int32)
    first_hot = (row_ids[:, None] // orbitals == orbit_ids[None, :]).astype(jnp.float32)
    second_hot = (row_ids[:, None] % orbitals == orbit_ids[None, :]).astype(jnp.float32)
    linked = jnp.dot(first_hot, pattern.astype(jnp.float32), precision=highest)
    screened = (
        interaction.astype(jnp.float32).reshape(rows, orbitals, orbitals) * linked[:, :, None]
    )
    polar_factor = occupation[:, None] - occupation[None, :]
    ladder_factor = 1.0 - occupation[:, None] - occupation[None, :]
    polar_terms = screened * polar_factor[None]
    hop_first = jnp.dot(first_hot, hopping, precision=highest)
    hop_second = jnp.dot(second_hot, hopping, precision=highest)
    pair_hopping = (
        hop_first[:, :, None] * second_hot[:, None, :]
        + first_hot[:, :, None] * hop_second[:, None, :]
    )
    kernel_direct = (polar_terms + pair_hopping).astype(jnp.bfloat16).reshape(rows, pairs)
    kernel_polar = polar_terms.astype(jnp.bfloat16).reshape(rows, pairs)
    kernel_ladder = (screened * ladder_factor[None]).astype(jnp.bfloat16).reshape(rows, pairs)
    same_piece = lax.all_gather(green_same, "prow", axis=0, tiled=True)
    opp_piece = lax.all_gather(green_opp, "prow", axis=0, tiled=True)
    new_same = (
        product(kernel_direct, same_piece)
        + product(kernel_polar, opp_piece)
        + product(kernel_ladder, swap_orbitals(same_piece, orbitals))
    )
    new_opp = (
        product(kernel_direct, opp_piece)
        + product(kernel_polar, same_piece)
        + product(kernel_ladder, swap_orbitals(opp_piece, orbitals))
    )
    next_same = (green_same.astype(jnp.float32) + 0.5 * new_same).astype(jnp.bfloat16)
    next_opp = (green_opp.astype(jnp.float32) + 0.5 * new_opp).astype(jnp.bfloat16)
    share = jnp.dot(first_hot.T, new_same + new_opp, precision=highest) * (
        1.0 / math.sqrt(orbitals)
    )
    collision = lax.psum(share, "prow")
    return (new_same, new_opp, next_same, next_opp, collision)


def build_body(orbitals, low, high, pairs, *refs):
    place_ref, inter_ref, pat_ref, hop_ref, occ_ref = refs[:5]
    pat4_ref, hop4_ref, eye4_ref, occ4_ref = refs[5:9]
    mixed_ref, polar_ref, turned_ref = refs[-3:]
    span = 4 * orbitals
    tiles = pairs // span
    start = place_ref[0]
    strips = range(0, high - low, 128)

    pitch = orbitals + 1
    room = orbitals * pitch

    @pl.loop(0, tiles // 2)
    def _(tile):
        cols = pl.ds(pl.multiple_of(tile * 2 * span, 128), 2 * span)
        for strip in strips:
            size = min(128, high - low - strip)
            turned = inter_ref[strip : strip + size, cols].astype(jnp.float32).T
            at = pl.multiple_of(strip // 128 * room + tile * 8 * pitch, 8)
            for m in range(8):
                there = pl.ds(at + m * pitch, orbitals)
                turned_ref[there, :size] = turned[m * orbitals : (m + 1) * orbitals]

    group = lax.broadcasted_iota(jnp.int32, (1, span), 1) // orbitals
    occ4 = occ4_ref[...]

    @pl.loop(0, tiles)
    def _(tile):
        cols = pl.ds(pl.multiple_of(tile * span, 128), span)

        def spread(values):
            row = jnp.where(group == 0, values[0], values[1])
            return jnp.where(group == 2, values[2], jnp.where(group == 3, values[3], row))

        inner = [4 * tile + m for m in range(4)]
        occ = spread([occ_ref[i] for i in inner])
        polar_factor = occ - occ4
        ladder_factor = (1.0 - occ4) - occ
        facts = {}
        for first in range(low // orbitals, -(-high // orbitals)):
            here = start + first
            linked = spread([pat_ref[here, i].astype(jnp.float32) for i in inner])
            hop_row = spread([hop_ref[here, i] for i in inner])
            unit = (group + 4 * tile == here).astype(jnp.float32)
            linked4 = pat4_ref[pl.ds(here, 1), :]
            facts[first] = (linked * polar_factor, linked4 * ladder_factor, hop_row, unit)
        blocks = []
        for strip in strips:
            size = min(128, high - low - strip)
            pieces = [
                turned_ref[
                    pl.ds(strip // 128 * room + 4 * tile + m, orbitals, stride=pitch), :
                ]
                for m in range(4)
            ]
            blocks.append(jnp.concatenate(pieces, axis=0).T[:size])
        block = jnp.concatenate(blocks, axis=0)
        row = low
        while row < high:
            first, second = row // orbitals, row % orbitals
            count = min(orbitals - second, high - row)
            there = slice(row - low, row - low + count)
            polar_row, ladder_row, hop_row, unit = facts[first]
            polar = inter_ref[there, cols].astype(jnp.float32) * polar_row
            hop = (
                hop_row * eye4_ref[second : second + count]
                + unit * hop4_ref[second : second + count]
            )
            ladder = (block[there] * ladder_row).astype(jnp.bfloat16)
            direct = (polar + hop).astype(jnp.bfloat16).astype(jnp.float32)
            held = polar.astype(jnp.bfloat16)
            polar_ref[there, cols] = held
            mixed_ref[there, cols] = (
                direct - held.astype(jnp.float32) + ladder.astype(jnp.float32)
            ).astype(jnp.bfloat16)
            row += count


def build_rows(place, interaction, smalls, made, low, high):
    rows, pairs = interaction.shape
    pattern, hopping, occupation = smalls[:3]
    orbitals = hopping.shape[0]
    height = high - low
    block = low // height
    assert low % height == 0
    shape = jax.ShapeDtypeStruct((rows, pairs), jnp.bfloat16)
    wide = pl.BlockSpec((height, pairs), lambda g, p: (block, 0))
    smem = pl.BlockSpec(memory_space=pltpu.SMEM)
    row4 = pl.BlockSpec((1, 4 * orbitals), lambda g, p: (0, 0))
    small = pl.BlockSpec((orbitals, 4 * orbitals), lambda g, p: (0, 0))
    return pl.pallas_call(
        functools.partial(build_body, orbitals, low, high, pairs),
        grid_spec=pltpu.PrefetchScalarGridSpec(
            num_scalar_prefetch=1,
            grid=(1,),
            in_specs=[wide, smem, smem, smem, small, small, small, row4]
            + [pl.BlockSpec(memory_space=pl.ANY)] * len(made),
            out_specs=[wide] * 2,
            scratch_shapes=[pltpu.VMEM((-(-height // 128) * orbitals * (orbitals + 1), 128), jnp.float32)],
        ),
        out_shape=[shape] * 2,
        input_output_aliases={9 + n: n for n in range(len(made))},
        compiler_params=pltpu.CompilerParams(vmem_limit_bytes=44 * MIB),
        cost_estimate=pl.CostEstimate(flops=1024, bytes_accessed=1024, transcendentals=0),
        name="build_rows",
    )(place, interaction, *smalls, *made)


def step_body(parts, rows, opening, closing, orbitals, scale, *refs):
    place_ref = refs[0]
    refs = list(refs[1:])
    chips = len(parts)
    mixed_ref, polar_ref = refs.pop(0), refs.pop(0)
    greens = []
    for count in parts:
        pieces = [refs.pop(0) for _ in range(2 * count)]
        greens.append([pieces[:count], pieces[count:]])
    sums = [] if opening else [refs.pop(0) for _ in range(3)]
    olds = [refs.pop(0) for _ in range(2)] if closing else []
    held = refs.pop()
    totals = [refs.pop() for _ in range(3)][::-1] if closing else refs[:3]
    core = place_ref[0]
    span = greens[0][0][0].shape[1]
    now = pl.program_id(1)

    for chip in range(chips):

        @pl.when(now == chip)
        def _():
            for which in range(2):
                lane = core if which == 0 else 1 - core
                there = pl.ds(pl.multiple_of(lane * rows, 64), rows)
                pieces = greens[chip][which]
                same = pieces[0][:rows, :]
                opp = pieces[-1][pieces[-1].shape[0] - rows :, :]
                both = same.astype(jnp.float32) + opp.astype(jnp.float32)
                held[there, :span] = same
                held[there, span : 2 * span] = opp
                held[there, 2 * span :] = both.astype(jnp.bfloat16)

    @pl.when(now == 0)
    def _():
        for n in range(3):
            if opening:
                totals[n][...] = jnp.zeros_like(totals[n])
            else:
                totals[n][...] = sums[n][...]

    mixed = product(mixed_ref[...], held[:, : 2 * span])
    totals[0][...] += mixed[:, :span]
    totals[1][...] += mixed[:, span:]
    totals[2][...] += product(polar_ref[...], held[:, 2 * span :])
    if closing:

        @pl.when(now == chips - 1)
        def _():
            for first in range(rows // orbitals):
                part = slice(first * orbitals, (first + 1) * orbitals)
                shared = totals[2][part, :]
                both = None
                for kind in range(2):
                    slope = totals[kind][part, :] + shared
                    old = olds[kind][part, :].astype(jnp.float32)
                    refs[kind][part, :] = slope
                    refs[2 + kind][part, :] = (old + 0.5 * slope).astype(jnp.bfloat16)
                    both = slope if both is None else both + slope
                summed = jnp.sum(both, axis=0, keepdims=True) * scale
                for copy in range(first, refs[4].shape[0], rows // orbitals):
                    refs[4][copy : copy + 1, :] = summed


def step(place, low, mats, greens, sums, olds, orbitals):
    chips = len(greens)
    opening, closing = not sums, bool(olds)
    rows = mats[0].shape[0]
    width = greens[0][0][0].shape[1]
    parts = tuple(len(pair[0]) for pair in greens)
    wide = 2 * rows
    span = min(width, 256) if closing else width
    tall = pl.BlockSpec((rows, span), lambda n, g, p: (0, n))
    mat = pl.BlockSpec((rows, wide), lambda n, g, p: (0, p[1 + low + g]))
    wide_sum = jax.ShapeDtypeStruct((rows, width), jnp.float32)
    scratch = [pltpu.VMEM((wide, 3 * span), jnp.bfloat16)]
    if closing:
        out_specs = [tall] * 4 + [pl.BlockSpec((orbitals, span), lambda n, g, p: (0, n))]
        out_shape = [wide_sum] * 2 + [jax.ShapeDtypeStruct((rows, width), jnp.bfloat16)] * 2
        out_shape += [jax.ShapeDtypeStruct((orbitals, width), jnp.float32)]
        scratch = [pltpu.VMEM((rows, span), jnp.float32)] * 3 + scratch
    else:
        out_specs, out_shape = [tall] * 3, [wide_sum] * 3
    operands = list(mats)
    blocks = [block for pair in greens for side in pair for block in side]
    operands += blocks
    in_specs = [mat] * 2
    in_specs += [pl.BlockSpec((block.shape[0], span), lambda n, g, p: (0, n)) for block in blocks]
    aliases = {}
    if not opening:
        if not closing:
            aliases = {1 + len(operands) + n: n for n in range(3)}
        operands += list(sums)
        in_specs += [tall] * 3
    if closing:
        operands += list(olds)
        in_specs += [tall] * 2
    return pl.pallas_call(
        functools.partial(
            step_body, parts, rows, opening, closing, orbitals, 1.0 / math.sqrt(orbitals)
        ),
        grid_spec=pltpu.PrefetchScalarGridSpec(
            num_scalar_prefetch=1,
            grid=(width // span, chips),
            in_specs=in_specs,
            out_specs=out_specs,
            scratch_shapes=scratch,
        ),
        out_shape=out_shape,
        input_output_aliases=aliases,
        compiler_params=pltpu.CompilerParams(vmem_limit_bytes=48 * MIB),
        cost_estimate=pl.CostEstimate(flops=1024, bytes_accessed=1024, transcendentals=0),
        name="add_products",
    )(place, *operands)


def after(value, *others):
    return lax.optimization_barrier((value, *others))[0]


def ring_form(green_same, green_opp, interaction, pattern, occupation, hopping):
    rows, width = green_same.shape
    orbitals = hopping.shape[0]
    pairs = orbitals * orbitals
    devices = pairs // rows
    chips = devices // 2
    me = lax.axis_index("prow")
    core = me % 2
    order = list(range(0, chips, 2)) + list(range(chips - 1, 0, -2))
    spot = [order.index(c) for c in range(chips)]
    half = chips // 2

    def away(device, far):
        way = 1 if device % 2 == 0 else -1
        return order[(spot[device // 2] - way * far) % chips]

    first_way = [(2 * away(d, 1) + d % 2, d) for d in range(devices)]
    second_way = [(b, a) for a, b in first_way]
    across = [(d, d ^ 1) for d in range(devices)]
    table = []
    for d in range(devices):
        line = [d % 2, d // 2]
        for far in range(1, half + 1):
            line += [away(d, far), away(d, -far)]
        table.append(line)
    place = lax.dynamic_index_in_dim(jnp.array(table, jnp.int32), me, 0, keepdims=False)

    def send(block, pairs_of):
        return lax.ppermute(block, "prow", pairs_of)

    start = (me * (rows // orbitals)).astype(jnp.int32)[None]
    smalls = (
        pattern,
        hopping,
        occupation,
        jnp.tile(pattern.astype(jnp.float32), (1, 4)),
        jnp.tile(hopping, (1, 4)),
        jnp.tile(jnp.eye(orbitals, dtype=jnp.float32), (1, 4)),
        jnp.tile(occupation, 4)[None],
    )

    def build(when, made, strip):
        low = 128 * strip
        return build_rows(when, interaction, smalls, made, low, min(low + 128, rows))

    strips = -(-rows // 128)
    own = jnp.concatenate([green_same, green_opp], axis=0)
    moving = [send(own, first_way), None]
    mats = build(start, (), 0)
    own_later = after(own, mats[0])
    moving[1] = send(own_later, second_way)
    near = send(own_later, across)
    mats = build(start, mats, 1)

    chips_in, low, sums, done, made = [([own], [near])], 0, (), mats[0], 2
    for far in range(1, half):
        got, passed = [], []
        for turn in range(2):
            block = after(moving[turn], done)
            onward = block if far < half - 1 else block[turn * rows : (turn + 1) * rows]
            moving[turn] = send(onward, second_way if turn else first_way)
            got.append(block)
            passed.append(send(block, across))
            if made < strips:
                mats = build(after(start, block), mats, made)
                made += 1
                done = mats[0]
            if far > 1 and turn == (far == 2) and made == strips:
                sums = step(after(place, block), low, mats, chips_in, sums, (), orbitals)
                low += len(chips_in)
                chips_in, done = [], sums[0]
        chips_in = chips_in + [([got[0]], [passed[1]]), ([got[1]], [passed[0]])]
    sums = step(place, low, mats, chips_in, sums, (), orbitals)
    low += len(chips_in)
    last = [after(block, sums[0]) for block in moving]
    shared = [send(block, across) for block in last]
    new_same, new_opp, next_same, next_opp, part = step(
        place, low, mats, [(last, shared)], sums, (green_same, green_opp), orbitals
    )
    collision = lax.all_to_all(part, "prow", split_axis=0, concat_axis=0, tiled=True)
    return (new_same, new_opp, next_same, next_opp, collision)


def per_device(green_same, green_opp, interaction, pattern, occupation, hopping):
    rows = green_same.shape[0]
    orbitals = hopping.shape[0]
    devices = orbitals * orbitals // rows
    fits = rows % orbitals == 0 and rows % 576 == 0 and devices % 4 == 0 and devices >= 12
    form = ring_form if fits else plain_form
    return form(green_same, green_opp, interaction, pattern, occupation, hopping)


def solution(mesh):
    placed = (
        P(("groups", "prow"), None),
        P(("groups", "prow"), None),
        P(("groups", "prow"), None),
        P("groups", None),
        P("groups"),
        P("groups", None),
    )
    return jax.shard_map(
        per_device,
        mesh=mesh,
        in_specs=placed,
        out_specs=(
            P(("groups", "prow"), None),
            P(("groups", "prow"), None),
            P(("groups", "prow"), None),
            P(("groups", "prow"), None),
            P("groups", None),
        ),
        check_vma=False,
    )
```

```python
import functools
import math

import jax
import jax.numpy as jnp
from jax import lax
from jax.experimental import pallas as pl
from jax.experimental.pallas import tpu as pltpu
from jax.sharding import PartitionSpec as P

MIB = 1 << 20


def swap_orbitals(block, orbitals):
    count = block.shape[1]
    return (
        block.reshape(orbitals, orbitals, count)
        .transpose(1, 0, 2)
        .reshape(orbitals * orbitals, count)
    )


def product(left, right):
    return jnp.dot(left, right, preferred_element_type=jnp.float32)


def plain_form(green_same, green_opp, interaction, pattern, occupation, hopping):
    rows, width = green_same.shape
    orbitals = hopping.shape[0]
    pairs = orbitals * orbitals
    highest = lax.Precision.HIGHEST
    row_ids = lax.axis_index("prow") * rows + jnp.arange(rows, dtype=jnp.int32)
    orbit_ids = jnp.arange(orbitals, dtype=jnp.int32)
    first_hot = (row_ids[:, None] // orbitals == orbit_ids[None, :]).astype(jnp.float32)
    second_hot = (row_ids[:, None] % orbitals == orbit_ids[None, :]).astype(jnp.float32)
    linked = jnp.dot(first_hot, pattern.astype(jnp.float32), precision=highest)
    screened = (
        interaction.astype(jnp.float32).reshape(rows, orbitals, orbitals) * linked[:, :, None]
    )
    polar_factor = occupation[:, None] - occupation[None, :]
    ladder_factor = 1.0 - occupation[:, None] - occupation[None, :]
    polar_terms = screened * polar_factor[None]
    hop_first = jnp.dot(first_hot, hopping, precision=highest)
    hop_second = jnp.dot(second_hot, hopping, precision=highest)
    pair_hopping = (
        hop_first[:, :, None] * second_hot[:, None, :]
        + first_hot[:, :, None] * hop_second[:, None, :]
    )
    kernel_direct = (polar_terms + pair_hopping).astype(jnp.bfloat16).reshape(rows, pairs)
    kernel_polar = polar_terms.astype(jnp.bfloat16).reshape(rows, pairs)
    kernel_ladder = (screened * ladder_factor[None]).astype(jnp.bfloat16).reshape(rows, pairs)
    same_piece = lax.all_gather(green_same, "prow", axis=0, tiled=True)
    opp_piece = lax.all_gather(green_opp, "prow", axis=0, tiled=True)
    new_same = (
        product(kernel_direct, same_piece)
        + product(kernel_polar, opp_piece)
        + product(kernel_ladder, swap_orbitals(same_piece, orbitals))
    )
    new_opp = (
        product(kernel_direct, opp_piece)
        + product(kernel_polar, same_piece)
        + product(kernel_ladder, swap_orbitals(opp_piece, orbitals))
    )
    next_same = (green_same.astype(jnp.float32) + 0.5 * new_same).astype(jnp.bfloat16)
    next_opp = (green_opp.astype(jnp.float32) + 0.5 * new_opp).astype(jnp.bfloat16)
    share = jnp.dot(first_hot.T, new_same + new_opp, precision=highest) * (
        1.0 / math.sqrt(orbitals)
    )
    collision = lax.psum(share, "prow")
    return (new_same, new_opp, next_same, next_opp, collision)


def build_body(orbitals, low, high, pairs, *refs):
    place_ref, inter_ref, pat_ref, hop_ref, occ_ref = refs[:5]
    pat4_ref, hop4_ref, eye4_ref, occ4_ref = refs[5:9]
    mixed_ref, polar_ref, turned_ref = refs[-3:]
    span = 4 * orbitals
    tiles = pairs // span
    start = place_ref[0]
    strips = range(0, high - low, 128)

    pitch = orbitals + 1
    room = orbitals * pitch

    @pl.when(pl.program_id(0) == 0)
    def _():
        @pl.loop(0, tiles // 2)
        def _(tile):
            cols = pl.ds(pl.multiple_of(tile * 2 * span, 128), 2 * span)
            for strip in strips:
                size = min(128, high - low - strip)
                turned = inter_ref[strip : strip + size, cols].astype(jnp.float32).T
                at = pl.multiple_of(strip // 128 * room + tile * 8 * pitch, 8)
                for m in range(8):
                    there = pl.ds(at + m * pitch, orbitals)
                    turned_ref[there, :size] = turned[m * orbitals : (m + 1) * orbitals]

    group = lax.broadcasted_iota(jnp.int32, (1, span), 1) // orbitals
    occ4 = occ4_ref[...]

    per_chunk = mixed_ref.shape[1] // span

    @pl.loop(0, per_chunk, unroll=2)
    def _(step):
        tile = pl.program_id(0) * per_chunk + step
        cols = pl.ds(pl.multiple_of(tile * span, 128), span)
        out_cols = pl.ds(pl.multiple_of(step * span, 128), span)

        def spread(values):
            row = jnp.where(group == 0, values[0], values[1])
            return jnp.where(group == 2, values[2], jnp.where(group == 3, values[3], row))

        inner = [4 * tile + m for m in range(4)]
        occ = spread([occ_ref[i] for i in inner])
        polar_factor = occ - occ4
        ladder_factor = (1.0 - occ4) - occ
        facts = {}
        for first in range(low // orbitals, -(-high // orbitals)):
            here = start + first
            linked = spread([pat_ref[here, i].astype(jnp.float32) for i in inner])
            hop_row = spread([hop_ref[here, i] for i in inner])
            unit = (group + 4 * tile == here).astype(jnp.float32)
            linked4 = pat4_ref[pl.ds(here, 1), :]
            facts[first] = (linked * polar_factor, linked4 * ladder_factor, hop_row, unit)
        blocks = []
        for strip in strips:
            size = min(128, high - low - strip)
            pieces = [
                turned_ref[
                    pl.ds(strip // 128 * room + 4 * tile + m, orbitals, stride=pitch), :
                ]
                for m in range(4)
            ]
            blocks.append(jnp.concatenate(pieces, axis=0).T[:size])
        block = jnp.concatenate(blocks, axis=0)
        row = low
        while row < high:
            first, second = row // orbitals, row % orbitals
            count = min(orbitals - second, high - row)
            there = slice(row - low, row - low + count)
            polar_row, ladder_row, hop_row, unit = facts[first]
            polar = inter_ref[there, cols].astype(jnp.float32) * polar_row
            hop = (
                hop_row * eye4_ref[second : second + count]
                + unit * hop4_ref[second : second + count]
            )
            ladder = (block[there] * ladder_row).astype(jnp.bfloat16)
            direct = (polar + hop).astype(jnp.bfloat16).astype(jnp.float32)
            held = polar.astype(jnp.bfloat16)
            polar_ref[there, out_cols] = held
            mixed_ref[there, out_cols] = (
                direct - held.astype(jnp.float32) + ladder.astype(jnp.float32)
            ).astype(jnp.bfloat16)
            row += count


def build_rows(place, interaction, smalls, made, low, high):
    rows, pairs = interaction.shape
    pattern, hopping, occupation = smalls[:3]
    orbitals = hopping.shape[0]
    height = high - low
    block = low // height
    assert low % height == 0
    shape = pltpu.HBM((rows, pairs), jnp.bfloat16)
    chunks = 4
    once = pl.Buffered(1)
    wide = pl.BlockSpec((height, pairs), lambda g, p: (block, 0), pipeline_mode=once)
    chunk = pl.BlockSpec((height, pairs // chunks), lambda g, p: (block, g))
    smem = pl.BlockSpec(memory_space=pltpu.SMEM)
    row4 = pl.BlockSpec((1, 4 * orbitals), lambda g, p: (0, 0))
    small = pl.BlockSpec((orbitals, 4 * orbitals), lambda g, p: (0, 0))
    return pl.pallas_call(
        functools.partial(build_body, orbitals, low, high, pairs),
        grid_spec=pltpu.PrefetchScalarGridSpec(
            num_scalar_prefetch=1,
            grid=(chunks,),
            in_specs=[wide, smem, smem, smem, small, small, small, row4]
            + [pl.BlockSpec(memory_space=pl.ANY)] * len(made),
            out_specs=[chunk] * 2,
            scratch_shapes=[pltpu.VMEM((-(-height // 128) * orbitals * (orbitals + 1), 128), jnp.float32)],
        ),
        out_shape=[shape] * 2,
        input_output_aliases={9 + n: n for n in range(len(made))},
        compiler_params=pltpu.CompilerParams(vmem_limit_bytes=28 * MIB),
        cost_estimate=pl.CostEstimate(flops=1024, bytes_accessed=1024, transcendentals=0),
        name="build_rows",
    )(place, interaction, *smalls, *made)


def step_body(parts, rows, opening, closing, orbitals, scale, *refs):
    place_ref = refs[0]
    refs = list(refs[1:])
    chips = len(parts)
    mixed_ref, polar_ref = refs.pop(0), refs.pop(0)
    greens = []
    for count in parts:
        pieces = [refs.pop(0) for _ in range(2 * count)]
        greens.append([pieces[:count], pieces[count:]])
    sums = [] if opening else [refs.pop(0) for _ in range(3)]
    olds = [refs.pop(0) for _ in range(2)] if closing else []
    held = refs.pop()
    totals = [refs.pop() for _ in range(3)][::-1] if closing else refs[:3]
    core = place_ref[0]
    span = greens[0][0][0].shape[1]
    now = pl.program_id(1)

    for chip in range(chips):

        @pl.when(now == chip)
        def _():
            for which in range(2):
                lane = core if which == 0 else 1 - core
                there = pl.ds(pl.multiple_of(lane * rows, 64), rows)
                pieces = greens[chip][which]
                same = pieces[0][:rows, :]
                opp = pieces[-1][pieces[-1].shape[0] - rows :, :]
                both = same.astype(jnp.float32) + opp.astype(jnp.float32)
                held[there, :span] = same
                held[there, span : 2 * span] = opp
                held[there, 2 * span :] = both.astype(jnp.bfloat16)

    @pl.when(now == 0)
    def _():
        for n in range(3):
            if opening:
                totals[n][...] = jnp.zeros_like(totals[n])
            else:
                totals[n][...] = sums[n][...]

    mixed = product(mixed_ref[...], held[:, : 2 * span])
    totals[0][...] += mixed[:, :span]
    totals[1][...] += mixed[:, span:]
    totals[2][...] += product(polar_ref[...], held[:, 2 * span :])
    if closing:

        @pl.when(now == chips - 1)
        def _():
            for first in range(rows // orbitals):
                part = slice(first * orbitals, (first + 1) * orbitals)
                shared = totals[2][part, :]
                both = None
                for kind in range(2):
                    slope = totals[kind][part, :] + shared
                    old = olds[kind][part, :].astype(jnp.float32)
                    refs[kind][part, :] = slope
                    refs[2 + kind][part, :] = (old + 0.5 * slope).astype(jnp.bfloat16)
                    both = slope if both is None else both + slope
                refs[4][first : first + 1, :] = jnp.sum(both, axis=0, keepdims=True) * scale


def step(place, low, mats, greens, sums, olds, orbitals):
    chips = len(greens)
    opening, closing = not sums, bool(olds)
    rows = mats[0].shape[0]
    width = greens[0][0][0].shape[1]
    parts = tuple(len(pair[0]) for pair in greens)
    wide = 2 * rows
    span = min(width, 256) if closing else width
    tall = pl.BlockSpec((rows, span), lambda n, g, p: (0, n))
    mat = pl.BlockSpec((rows, wide), lambda n, g, p: (0, p[1 + low + g]))
    wide_sum = jax.ShapeDtypeStruct((rows, width), jnp.float32)
    scratch = [pltpu.VMEM((wide, 3 * span), jnp.bfloat16)]
    if closing:
        out_specs = [tall] * 4 + [pl.BlockSpec((rows // orbitals, span), lambda n, g, p: (0, n))]
        out_shape = [wide_sum] * 2 + [jax.ShapeDtypeStruct((rows, width), jnp.bfloat16)] * 2
        out_shape += [jax.ShapeDtypeStruct((rows // orbitals, width), jnp.float32)]
        scratch = [pltpu.VMEM((rows, span), jnp.float32)] * 3 + scratch
    else:
        out_specs, out_shape = [tall] * 3, [wide_sum] * 3
    operands = [pltpu.with_memory_space_constraint(mat_, pltpu.HBM) for mat_ in mats]
    blocks = [block for pair in greens for side in pair for block in side]
    operands += blocks
    in_specs = [mat] * 2
    mode = pl.Buffered(1 if span == width else 2)
    in_specs += [
        pl.BlockSpec((block.shape[0], span), lambda n, g, p: (0, n), pipeline_mode=mode)
        for block in blocks
    ]
    aliases = {}
    if not opening:
        if not closing:
            aliases = {1 + len(operands) + n: n for n in range(3)}
        operands += list(sums)
        in_specs += [pl.BlockSpec((rows, span), lambda n, g, p: (0, n), pipeline_mode=mode)] * 3
    if closing:
        operands += list(olds)
        in_specs += [tall] * 2
    return pl.pallas_call(
        functools.partial(
            step_body, parts, rows, opening, closing, orbitals, 1.0 / math.sqrt(orbitals)
        ),
        grid_spec=pltpu.PrefetchScalarGridSpec(
            num_scalar_prefetch=1,
            grid=(width // span, chips),
            in_specs=in_specs,
            out_specs=out_specs,
            scratch_shapes=scratch,
        ),
        out_shape=out_shape,
        input_output_aliases=aliases,
        compiler_params=pltpu.CompilerParams(vmem_limit_bytes=36 * MIB),
        cost_estimate=pl.CostEstimate(flops=1024, bytes_accessed=1024, transcendentals=0),
        name="add_products",
    )(place, *operands)


def spread_blocks(block, index, stride, devices):
    blocks = [block]
    for other in range(1, 4):
        pairs_of = [(d, d ^ (other * stride)) for d in range(devices)]
        blocks.append(lax.ppermute(block, "prow", pairs_of))
    part = index // stride % 4
    low, high = part % 2 == 1, part // 2 == 1
    b = [jnp.where(low, blocks[n ^ 1], blocks[n]) for n in range(4)]
    b = [jnp.where(high, b[n ^ 2], b[n]) for n in range(4)]
    return jnp.concatenate(b, axis=0)


def after(value, *others):
    return lax.optimization_barrier((value, *others))[0]


def ring_form(green_same, green_opp, interaction, pattern, occupation, hopping):
    rows, width = green_same.shape
    orbitals = hopping.shape[0]
    pairs = orbitals * orbitals
    devices = pairs // rows
    chips = devices // 2
    me = lax.axis_index("prow")
    core = me % 2
    order = list(range(0, chips, 2)) + list(range(chips - 1, 0, -2))
    spot = [order.index(c) for c in range(chips)]
    half = chips // 2

    def away(device, far):
        way = 1 if device % 2 == 0 else -1
        return order[(spot[device // 2] - way * far) % chips]

    first_way = [(2 * away(d, 1) + d % 2, d) for d in range(devices)]
    second_way = [(b, a) for a, b in first_way]
    across = [(d, d ^ 1) for d in range(devices)]
    table = []
    for d in range(devices):
        line = [d % 2, d // 2]
        for far in range(1, half + 1):
            line += [away(d, -far), away(d, far)]
        table.append(line)
    place = lax.dynamic_index_in_dim(jnp.array(table, jnp.int32), me, 0, keepdims=False)

    def send(block, pairs_of):
        return lax.ppermute(block, "prow", pairs_of)

    interaction = pltpu.with_memory_space_constraint(interaction, pltpu.HBM)
    start = (me * (rows // orbitals)).astype(jnp.int32)[None]
    smalls = (
        pattern,
        hopping,
        occupation,
        jnp.tile(pattern.astype(jnp.float32), (1, 4)),
        jnp.tile(hopping, (1, 4)),
        jnp.tile(jnp.eye(orbitals, dtype=jnp.float32), (1, 4)),
        jnp.tile(occupation, 4)[None],
    )

    big = rows // 9 * 4
    cuts = [(0, big), (big, 2 * big), (2 * big, rows)]

    def build(when, made, part):
        return build_rows(when, interaction, smalls, made, *cuts[part])

    own = jnp.concatenate([green_same, green_opp], axis=0)
    moving = [send(own, first_way), None]
    mats = build(start, (), 0)
    own_later = after(own, mats[0])
    moving[1] = send(own_later, second_way)
    near = send(own_later, across)
    mats = build(start, mats, 1)

    low, sums, done = 0, (), mats[0]
    waiting = [([own], [near])]
    for far in range(1, half):
        got, passed = [], []
        for turn in range(2):
            block = after(moving[turn], done)
            onward = block if far < half - 1 else block[turn * rows : (turn + 1) * rows]
            moving[turn] = send(onward, second_way if turn else first_way)
            got.append(block)
            passed.append(send(block, across))
            if far == 1 and turn == 0:
                mats = build(after(start, block), mats, 2)
                done = mats[0]
                continue
            later = []
            if turn == 1:
                came = [([got[1]], [passed[0]]), ([got[0]], [passed[1]])]
                split = 0 if far == 1 else 1
                waiting, later = waiting + came[:split], came[split:]
            sums = step(after(place, block), low, mats, waiting, sums, (), orbitals)
            low += len(waiting)
            waiting, done = later, sums[0]
    sums = step(place, low, mats, waiting, sums, (), orbitals)
    low += len(waiting)
    last = [after(block, sums[0]) for block in moving]
    shared = [send(block, across) for block in last]
    new_same, new_opp, next_same, next_opp, part = step(
        place, low, mats, [(last, shared)], sums, (green_same, green_opp), orbitals
    )
    if devices == 16:
        collision = spread_blocks(spread_blocks(part, me, 1, devices), me, 4, devices)
    else:
        collision = lax.all_gather(part, "prow", axis=0, tiled=True)
    return (new_same, new_opp, next_same, next_opp, collision)


def per_device(green_same, green_opp, interaction, pattern, occupation, hopping):
    rows = green_same.shape[0]
    orbitals = hopping.shape[0]
    devices = orbitals * orbitals // rows
    fits = rows % orbitals == 0 and rows % 576 == 0 and devices % 4 == 0 and devices >= 12
    form = ring_form if fits else plain_form
    return form(green_same, green_opp, interaction, pattern, occupation, hopping)


def solution(mesh):
    placed = (
        P(("groups", "prow"), None),
        P(("groups", "prow"), None),
        P(("groups", "prow"), None),
        P("groups", None),
        P("groups"),
        P("groups", None),
    )
    return jax.shard_map(
        per_device,
        mesh=mesh,
        in_specs=placed,
        out_specs=(
            P(("groups", "prow"), None),
            P(("groups", "prow"), None),
            P(("groups", "prow"), None),
            P(("groups", "prow"), None),
            P("groups", None),
        ),
        check_vma=False,
    )
```

```python
import functools
import math

import jax
import jax.numpy as jnp
import numpy as np
from jax import lax
from jax.experimental import pallas as pl
from jax.experimental.pallas import tpu as pltpu
from jax.sharding import PartitionSpec as P

MIB = 1 << 20


def swap_orbitals(block, orbitals):
    count = block.shape[1]
    return (
        block.reshape(orbitals, orbitals, count)
        .transpose(1, 0, 2)
        .reshape(orbitals * orbitals, count)
    )


def product(left, right):
    return jnp.dot(left, right, preferred_element_type=jnp.float32)


def plain_form(green_same, green_opp, interaction, pattern, occupation, hopping):
    rows, width = green_same.shape
    orbitals = hopping.shape[0]
    pairs = orbitals * orbitals
    highest = lax.Precision.HIGHEST
    row_ids = lax.axis_index("prow") * rows + jnp.arange(rows, dtype=jnp.int32)
    orbit_ids = jnp.arange(orbitals, dtype=jnp.int32)
    first_hot = (row_ids[:, None] // orbitals == orbit_ids[None, :]).astype(jnp.float32)
    second_hot = (row_ids[:, None] % orbitals == orbit_ids[None, :]).astype(jnp.float32)
    linked = jnp.dot(first_hot, pattern.astype(jnp.float32), precision=highest)
    screened = (
        interaction.astype(jnp.float32).reshape(rows, orbitals, orbitals) * linked[:, :, None]
    )
    polar_factor = occupation[:, None] - occupation[None, :]
    ladder_factor = 1.0 - occupation[:, None] - occupation[None, :]
    polar_terms = screened * polar_factor[None]
    hop_first = jnp.dot(first_hot, hopping, precision=highest)
    hop_second = jnp.dot(second_hot, hopping, precision=highest)
    pair_hopping = (
        hop_first[:, :, None] * second_hot[:, None, :]
        + first_hot[:, :, None] * hop_second[:, None, :]
    )
    kernel_direct = (polar_terms + pair_hopping).astype(jnp.bfloat16).reshape(rows, pairs)
    kernel_polar = polar_terms.astype(jnp.bfloat16).reshape(rows, pairs)
    kernel_ladder = (screened * ladder_factor[None]).astype(jnp.bfloat16).reshape(rows, pairs)
    same_piece = lax.all_gather(green_same, "prow", axis=0, tiled=True)
    opp_piece = lax.all_gather(green_opp, "prow", axis=0, tiled=True)
    new_same = (
        product(kernel_direct, same_piece)
        + product(kernel_polar, opp_piece)
        + product(kernel_ladder, swap_orbitals(same_piece, orbitals))
    )
    new_opp = (
        product(kernel_direct, opp_piece)
        + product(kernel_polar, same_piece)
        + product(kernel_ladder, swap_orbitals(opp_piece, orbitals))
    )
    next_same = (green_same.astype(jnp.float32) + 0.5 * new_same).astype(jnp.bfloat16)
    next_opp = (green_opp.astype(jnp.float32) + 0.5 * new_opp).astype(jnp.bfloat16)
    share = jnp.dot(first_hot.T, new_same + new_opp, precision=highest) * (
        1.0 / math.sqrt(orbitals)
    )
    collision = lax.psum(share, "prow")
    return (new_same, new_opp, next_same, next_opp, collision)


def build_body(orbitals, low, high, pairs, *refs):
    place_ref, inter_ref, pat_ref, hop_ref, occ_ref = refs[:5]
    both4_ref, eye4_ref, occ4_ref = refs[5:8]
    mixed_ref, polar_ref, turned_ref = refs[-3:]
    span = 4 * orbitals
    tiles = pairs // span
    start = place_ref[0]
    strips = range(0, high - low, 128)

    pitch = orbitals + 1
    room = orbitals * pitch

    @pl.when(pl.program_id(0) == 0)
    def _():
        @pl.loop(0, tiles // 2)
        def _(tile):
            cols = pl.ds(pl.multiple_of(tile * 2 * span, 128), 2 * span)
            for strip in strips:
                size = min(128, high - low - strip)
                turned = inter_ref[strip : strip + size, cols].astype(jnp.float32).T
                at = pl.multiple_of(strip // 128 * room + tile * 8 * pitch, 8)
                for m in range(8):
                    there = pl.ds(at + m * pitch, orbitals)
                    turned_ref[there, :size] = turned[m * orbitals : (m + 1) * orbitals]

    group = lax.broadcasted_iota(jnp.int32, (1, span), 1) // orbitals
    occ4 = occ4_ref[...]

    per_chunk = mixed_ref.shape[1] // span

    @pl.loop(0, per_chunk, unroll=2)
    def _(step):
        tile = pl.program_id(0) * per_chunk + step
        cols = pl.ds(pl.multiple_of(tile * span, 128), span)
        out_cols = pl.ds(pl.multiple_of(step * span, 128), span)

        def spread(values):
            row = jnp.where(group == 0, values[0], values[1])
            return jnp.where(group == 2, values[2], jnp.where(group == 3, values[3], row))

        inner = [4 * tile + m for m in range(4)]
        occ = spread([occ_ref[i] for i in inner])
        polar_factor = occ - occ4
        ladder_factor = (1.0 - occ4) - occ
        facts = {}
        for first in range(low // orbitals, -(-high // orbitals)):
            here = start + first
            linked = spread([pat_ref[here, i].astype(jnp.float32) for i in inner])
            hop_row = spread([hop_ref[here, i] for i in inner])
            unit = (group + 4 * tile == here).astype(jnp.float32)
            linked4 = both4_ref[pl.ds(here, 1), :]
            facts[first] = (linked * polar_factor, linked4 * ladder_factor, hop_row, unit)
        blocks = []
        for strip in strips:
            size = min(128, high - low - strip)
            pieces = [
                turned_ref[
                    pl.ds(strip // 128 * room + 4 * tile + m, orbitals, stride=pitch), :
                ]
                for m in range(4)
            ]
            blocks.append(jnp.concatenate(pieces, axis=0).T[:size])
        block = jnp.concatenate(blocks, axis=0)
        row = low
        while row < high:
            first, second = row // orbitals, row % orbitals
            count = min(orbitals - second, high - row)
            there = slice(row - low, row - low + count)
            polar_row, ladder_row, hop_row, unit = facts[first]
            polar = inter_ref[there, cols].astype(jnp.float32) * polar_row
            hop = (
                hop_row * eye4_ref[second : second + count]
                + unit * both4_ref[orbitals + second : orbitals + second + count]
            )
            ladder = (block[there] * ladder_row).astype(jnp.bfloat16)
            direct = (polar + hop).astype(jnp.bfloat16).astype(jnp.float32)
            held = polar.astype(jnp.bfloat16)
            polar_ref[there, out_cols] = held
            mixed_ref[there, out_cols] = (
                direct - held.astype(jnp.float32) + ladder.astype(jnp.float32)
            ).astype(jnp.bfloat16)
            row += count


def build_rows(place, interaction, smalls, made, low, high):
    rows, pairs = interaction.shape
    pattern, hopping, occupation = smalls[:3]
    orbitals = hopping.shape[0]
    height = high - low
    block = low // height
    assert low % height == 0
    shape = pltpu.HBM((rows, pairs), jnp.bfloat16)
    chunks = 4
    once = pl.Buffered(1)
    wide = pl.BlockSpec((height, pairs), lambda g, p: (block, 0), pipeline_mode=once)
    chunk = pl.BlockSpec((height, pairs // chunks), lambda g, p: (block, g))
    smem = pl.BlockSpec(memory_space=pltpu.SMEM)
    row4 = pl.BlockSpec((1, 4 * orbitals), lambda g, p: (0, 0))
    small = pl.BlockSpec((orbitals, 4 * orbitals), lambda g, p: (0, 0))
    twice = pl.BlockSpec((2 * orbitals, 4 * orbitals), lambda g, p: (0, 0))
    return pl.pallas_call(
        functools.partial(build_body, orbitals, low, high, pairs),
        grid_spec=pltpu.PrefetchScalarGridSpec(
            num_scalar_prefetch=1,
            grid=(chunks,),
            in_specs=[wide, smem, smem, smem, twice, small, row4]
            + [pl.BlockSpec(memory_space=pl.ANY)] * len(made),
            out_specs=[chunk] * 2,
            scratch_shapes=[pltpu.VMEM((-(-height // 128) * orbitals * (orbitals + 1), 128), jnp.float32)],
        ),
        out_shape=[shape] * 2,
        input_output_aliases={8 + n: n for n in range(len(made))},
        compiler_params=pltpu.CompilerParams(vmem_limit_bytes=28 * MIB),
        cost_estimate=pl.CostEstimate(flops=1024, bytes_accessed=1024, transcendentals=0),
        name="build_rows",
    )(place, interaction, *smalls, *made)


def step_body(parts, rows, opening, closing, orbitals, scale, *refs):
    place_ref = refs[0]
    refs = list(refs[1:])
    chips = len(parts)
    mixed_ref, polar_ref = refs.pop(0), refs.pop(0)
    greens = []
    for count in parts:
        pieces = [refs.pop(0) for _ in range(2 * count)]
        greens.append([pieces[:count], pieces[count:]])
    sums = [] if opening else [refs.pop(0) for _ in range(3)]
    olds = [refs.pop(0) for _ in range(2)] if closing else []
    held = refs.pop()
    totals = [refs.pop() for _ in range(3)][::-1] if closing else refs[:3]
    core = place_ref[0]
    span = greens[0][0][0].shape[1]
    now = pl.program_id(1)

    for chip in range(chips):

        @pl.when(now == chip)
        def _():
            for which in range(2):
                lane = core if which == 0 else 1 - core
                there = pl.ds(pl.multiple_of(lane * rows, 64), rows)
                pieces = greens[chip][which]
                same = pieces[0][:rows, :]
                opp = pieces[-1][pieces[-1].shape[0] - rows :, :]
                both = same.astype(jnp.float32) + opp.astype(jnp.float32)
                held[there, :span] = same
                held[there, span : 2 * span] = opp
                held[there, 2 * span :] = both.astype(jnp.bfloat16)

    @pl.when(now == 0)
    def _():
        for n in range(3):
            if opening:
                totals[n][...] = jnp.zeros_like(totals[n])
            else:
                totals[n][...] = sums[n][...]

    mixed = product(mixed_ref[...], held[:, : 2 * span])
    totals[0][...] += mixed[:, :span]
    totals[1][...] += mixed[:, span:]
    totals[2][...] += product(polar_ref[...], held[:, 2 * span :])
    if closing:

        @pl.when(now == chips - 1)
        def _():
            for first in range(rows // orbitals):
                part = slice(first * orbitals, (first + 1) * orbitals)
                shared = totals[2][part, :]
                both = None
                for kind in range(2):
                    slope = totals[kind][part, :] + shared
                    old = olds[kind][part, :].astype(jnp.float32)
                    refs[kind][part, :] = slope
                    refs[2 + kind][part, :] = (old + 0.5 * slope).astype(jnp.bfloat16)
                    both = slope if both is None else both + slope
                refs[4][first : first + 1, :] = jnp.sum(both, axis=0, keepdims=True) * scale


def step(place, low, mats, greens, sums, olds, orbitals):
    chips = len(greens)
    opening, closing = not sums, bool(olds)
    rows = mats[0].shape[0]
    width = greens[0][0][0].shape[1]
    parts = tuple(len(pair[0]) for pair in greens)
    wide = 2 * rows
    span = min(width, 256) if closing else width
    tall = pl.BlockSpec((rows, span), lambda n, g, p: (0, n))
    mat = pl.BlockSpec((rows, wide), lambda n, g, p: (0, p[1 + low + g]))
    wide_sum = jax.ShapeDtypeStruct((rows, width), jnp.float32)
    scratch = [pltpu.VMEM((wide, 3 * span), jnp.bfloat16)]
    if closing:
        out_specs = [tall] * 4 + [pl.BlockSpec((rows // orbitals, span), lambda n, g, p: (0, n))]
        out_shape = [wide_sum] * 2 + [jax.ShapeDtypeStruct((rows, width), jnp.bfloat16)] * 2
        out_shape += [jax.ShapeDtypeStruct((rows // orbitals, width), jnp.float32)]
        scratch = [pltpu.VMEM((rows, span), jnp.float32)] * 3 + scratch
    else:
        out_specs, out_shape = [tall] * 3, [wide_sum] * 3
    operands = [pltpu.with_memory_space_constraint(mat_, pltpu.HBM) for mat_ in mats]
    blocks = [block for pair in greens for side in pair for block in side]
    operands += blocks
    in_specs = [mat] * 2
    mode = pl.Buffered(1 if span == width else 2)
    in_specs += [
        pl.BlockSpec((block.shape[0], span), lambda n, g, p: (0, n), pipeline_mode=mode)
        for block in blocks
    ]
    aliases = {}
    if not opening:
        if not closing:
            aliases = {1 + len(operands) + n: n for n in range(3)}
        operands += list(sums)
        in_specs += [pl.BlockSpec((rows, span), lambda n, g, p: (0, n), pipeline_mode=mode)] * 3
    if closing:
        operands += list(olds)
        in_specs += [tall] * 2
    return pl.pallas_call(
        functools.partial(
            step_body, parts, rows, opening, closing, orbitals, 1.0 / math.sqrt(orbitals)
        ),
        grid_spec=pltpu.PrefetchScalarGridSpec(
            num_scalar_prefetch=1,
            grid=(width // span, chips),
            in_specs=in_specs,
            out_specs=out_specs,
            scratch_shapes=scratch,
        ),
        out_shape=out_shape,
        input_output_aliases=aliases,
        compiler_params=pltpu.CompilerParams(vmem_limit_bytes=36 * MIB),
        cost_estimate=pl.CostEstimate(flops=1024, bytes_accessed=1024, transcendentals=0),
        name="add_products",
    )(place, *operands)


def spread_blocks(block, index, stride, devices):
    blocks = [block]
    for other in range(1, 4):
        pairs_of = [(d, d ^ (other * stride)) for d in range(devices)]
        blocks.append(lax.ppermute(block, "prow", pairs_of))
    part = index // stride % 4
    low, high = part % 2 == 1, part // 2 == 1
    b = [jnp.where(low, blocks[n ^ 1], blocks[n]) for n in range(4)]
    b = [jnp.where(high, b[n ^ 2], b[n]) for n in range(4)]
    return jnp.concatenate(b, axis=0)


def after(value, *others):
    return lax.optimization_barrier((value, *others))[0]


def ring_form(green_same, green_opp, interaction, pattern, occupation, hopping):
    rows, width = green_same.shape
    orbitals = hopping.shape[0]
    pairs = orbitals * orbitals
    devices = pairs // rows
    chips = devices // 2
    me = lax.axis_index("prow")
    core = me % 2
    order = list(range(0, chips, 2)) + list(range(chips - 1, 0, -2))
    spot = [order.index(c) for c in range(chips)]
    half = chips // 2

    def away(device, far):
        way = 1 if device % 2 == 0 else -1
        return order[(spot[device // 2] - way * far) % chips]

    first_way = [(2 * away(d, 1) + d % 2, d) for d in range(devices)]
    second_way = [(b, a) for a, b in first_way]
    across = [(d, d ^ 1) for d in range(devices)]
    table = []
    for d in range(devices):
        line = [d % 2, d // 2]
        for far in range(1, half + 1):
            line += [away(d, -far), away(d, far)]
        table.append(line)
    place = lax.dynamic_index_in_dim(jnp.array(table, jnp.int32), me, 0, keepdims=False)

    def send(block, pairs_of):
        return lax.ppermute(block, "prow", pairs_of)

    interaction = pltpu.with_memory_space_constraint(interaction, pltpu.HBM)
    start = (me * (rows // orbitals)).astype(jnp.int32)[None]
    smalls = (
        pattern,
        hopping,
        occupation,
        jnp.concatenate([jnp.concatenate([pattern.astype(jnp.float32), hopping], axis=0)] * 4, axis=1),
        jnp.array(np.tile(np.eye(orbitals, dtype=np.float32), (1, 4))),
        jnp.concatenate([occupation] * 4)[None],
    )

    big = rows // 9 * 4
    cuts = [(2 * big, rows), (0, big), (big, 2 * big)]

    def build(when, made, part):
        return build_rows(when, interaction, smalls, made, *cuts[part])

    own = jnp.concatenate([green_same, green_opp], axis=0)
    moving = [send(own, first_way), None]
    mats = build(start, (), 0)
    own_later = after(own, mats[0])
    moving[1] = send(own_later, second_way)
    near = send(own_later, across)
    mats = build(start, mats, 1)

    low, sums, done = 0, (), mats[0]
    waiting = [([own], [near])]
    for far in range(1, half):
        got, passed = [], []
        for turn in range(2):
            block = after(moving[turn], done)
            onward = block if far < half - 1 else block[turn * rows : (turn + 1) * rows]
            moving[turn] = send(onward, second_way if turn else first_way)
            got.append(block)
            passed.append(send(block, across))
            if far == 1 and turn == 0:
                mats = build(after(start, block), mats, 2)
                done = mats[0]
                continue
            later = []
            if turn == 1:
                came = [([got[1]], [passed[0]]), ([got[0]], [passed[1]])]
                split = 0 if far == 1 else 1
                waiting, later = waiting + came[:split], came[split:]
            sums = step(after(place, block), low, mats, waiting, sums, (), orbitals)
            low += len(waiting)
            waiting, done = later, sums[0]
    sums = step(place, low, mats, waiting, sums, (), orbitals)
    low += len(waiting)
    last = [after(block, sums[0]) for block in moving]
    shared = [send(block, across) for block in last]
    new_same, new_opp, next_same, next_opp, part = step(
        place, low, mats, [(last, shared)], sums, (green_same, green_opp), orbitals
    )
    if devices == 16:
        collision = spread_blocks(spread_blocks(part, me, 1, devices), me, 4, devices)
    else:
        collision = lax.all_gather(part, "prow", axis=0, tiled=True)
    return (new_same, new_opp, next_same, next_opp, collision)


def per_device(green_same, green_opp, interaction, pattern, occupation, hopping):
    rows = green_same.shape[0]
    orbitals = hopping.shape[0]
    devices = orbitals * orbitals // rows
    fits = rows % orbitals == 0 and rows % 576 == 0 and devices % 4 == 0 and devices >= 12
    form = ring_form if fits else plain_form
    return form(green_same, green_opp, interaction, pattern, occupation, hopping)


def solution(mesh):
    placed = (
        P(("groups", "prow"), None),
        P(("groups", "prow"), None),
        P(("groups", "prow"), None),
        P("groups", None),
        P("groups"),
        P("groups", None),
    )
    return jax.shard_map(
        per_device,
        mesh=mesh,
        in_specs=placed,
        out_specs=(
            P(("groups", "prow"), None),
            P(("groups", "prow"), None),
            P(("groups", "prow"), None),
            P(("groups", "prow"), None),
            P("groups", None),
        ),
        check_vma=False,
    )
```

```python
import functools
import math

import jax
import jax.numpy as jnp
import numpy as np
from jax import lax
from jax.experimental import pallas as pl
from jax.experimental.pallas import tpu as pltpu
from jax.sharding import PartitionSpec as P

MIB = 1 << 20


def swap_orbitals(block, orbitals):
    count = block.shape[1]
    return (
        block.reshape(orbitals, orbitals, count)
        .transpose(1, 0, 2)
        .reshape(orbitals * orbitals, count)
    )


def product(left, right):
    return jnp.dot(left, right, preferred_element_type=jnp.float32)


def plain_form(green_same, green_opp, interaction, pattern, occupation, hopping):
    rows, width = green_same.shape
    orbitals = hopping.shape[0]
    pairs = orbitals * orbitals
    highest = lax.Precision.HIGHEST
    row_ids = lax.axis_index("prow") * rows + jnp.arange(rows, dtype=jnp.int32)
    orbit_ids = jnp.arange(orbitals, dtype=jnp.int32)
    first_hot = (row_ids[:, None] // orbitals == orbit_ids[None, :]).astype(jnp.float32)
    second_hot = (row_ids[:, None] % orbitals == orbit_ids[None, :]).astype(jnp.float32)
    linked = jnp.dot(first_hot, pattern.astype(jnp.float32), precision=highest)
    screened = (
        interaction.astype(jnp.float32).reshape(rows, orbitals, orbitals) * linked[:, :, None]
    )
    polar_factor = occupation[:, None] - occupation[None, :]
    ladder_factor = 1.0 - occupation[:, None] - occupation[None, :]
    polar_terms = screened * polar_factor[None]
    hop_first = jnp.dot(first_hot, hopping, precision=highest)
    hop_second = jnp.dot(second_hot, hopping, precision=highest)
    pair_hopping = (
        hop_first[:, :, None] * second_hot[:, None, :]
        + first_hot[:, :, None] * hop_second[:, None, :]
    )
    kernel_direct = (polar_terms + pair_hopping).astype(jnp.bfloat16).reshape(rows, pairs)
    kernel_polar = polar_terms.astype(jnp.bfloat16).reshape(rows, pairs)
    kernel_ladder = (screened * ladder_factor[None]).astype(jnp.bfloat16).reshape(rows, pairs)
    same_piece = lax.all_gather(green_same, "prow", axis=0, tiled=True)
    opp_piece = lax.all_gather(green_opp, "prow", axis=0, tiled=True)
    new_same = (
        product(kernel_direct, same_piece)
        + product(kernel_polar, opp_piece)
        + product(kernel_ladder, swap_orbitals(same_piece, orbitals))
    )
    new_opp = (
        product(kernel_direct, opp_piece)
        + product(kernel_polar, same_piece)
        + product(kernel_ladder, swap_orbitals(opp_piece, orbitals))
    )
    next_same = (green_same.astype(jnp.float32) + 0.5 * new_same).astype(jnp.bfloat16)
    next_opp = (green_opp.astype(jnp.float32) + 0.5 * new_opp).astype(jnp.bfloat16)
    share = jnp.dot(first_hot.T, new_same + new_opp, precision=highest) * (
        1.0 / math.sqrt(orbitals)
    )
    collision = lax.psum(share, "prow")
    return (new_same, new_opp, next_same, next_opp, collision)


def build_body(orbitals, low, high, pairs, *refs):
    place_ref, inter_ref, pat_ref, hop_ref, occ_ref = refs[:5]
    both4_ref, eye4_ref, occ4_ref = refs[5:8]
    mixed_ref, polar_ref, turned_ref = refs[-3:]
    span = 4 * orbitals
    tiles = pairs // span
    start = place_ref[0]
    strips = range(0, high - low, 128)

    pitch = orbitals + 1
    room = orbitals * pitch

    @pl.when(pl.program_id(0) == 0)
    def _():
        @pl.loop(0, tiles // 2)
        def _(tile):
            cols = pl.ds(pl.multiple_of(tile * 2 * span, 128), 2 * span)
            for strip in strips:
                size = min(128, high - low - strip)
                turned = inter_ref[strip : strip + size, cols].astype(jnp.float32).T
                at = pl.multiple_of(strip // 128 * room + tile * 8 * pitch, 8)
                for m in range(8):
                    there = pl.ds(at + m * pitch, orbitals)
                    turned_ref[there, :size] = turned[m * orbitals : (m + 1) * orbitals]

    group = lax.broadcasted_iota(jnp.int32, (1, span), 1) // orbitals
    occ4 = occ4_ref[...]

    per_chunk = mixed_ref.shape[1] // span

    @pl.loop(0, per_chunk, unroll=2)
    def _(step):
        tile = pl.program_id(0) * per_chunk + step
        cols = pl.ds(pl.multiple_of(tile * span, 128), span)
        out_cols = pl.ds(pl.multiple_of(step * span, 128), span)

        def spread(values):
            row = jnp.where(group == 0, values[0], values[1])
            return jnp.where(group == 2, values[2], jnp.where(group == 3, values[3], row))

        inner = [4 * tile + m for m in range(4)]
        occ = spread([occ_ref[i] for i in inner])
        polar_factor = occ - occ4
        ladder_factor = (1.0 - occ4) - occ
        facts = {}
        for first in range(low // orbitals, -(-high // orbitals)):
            here = start + first
            linked = spread([pat_ref[here, i].astype(jnp.float32) for i in inner])
            hop_row = spread([hop_ref[here, i] for i in inner])
            unit = (group + 4 * tile == here).astype(jnp.float32)
            linked4 = both4_ref[pl.ds(here, 1), :]
            facts[first] = (linked * polar_factor, linked4 * ladder_factor, hop_row, unit)
        blocks = []
        for strip in strips:
            size = min(128, high - low - strip)
            pieces = [
                turned_ref[
                    pl.ds(strip // 128 * room + 4 * tile + m, orbitals, stride=pitch), :
                ]
                for m in range(4)
            ]
            blocks.append(jnp.concatenate(pieces, axis=0).T[:size])
        block = jnp.concatenate(blocks, axis=0)
        row = low
        while row < high:
            first, second = row // orbitals, row % orbitals
            count = min(orbitals - second, high - row)
            there = slice(row - low, row - low + count)
            polar_row, ladder_row, hop_row, unit = facts[first]
            polar = inter_ref[there, cols].astype(jnp.float32) * polar_row
            hop = (
                hop_row * eye4_ref[second : second + count]
                + unit * both4_ref[orbitals + second : orbitals + second + count]
            )
            ladder = (block[there] * ladder_row).astype(jnp.bfloat16)
            direct = (polar + hop).astype(jnp.bfloat16).astype(jnp.float32)
            held = polar.astype(jnp.bfloat16)
            polar_ref[there, out_cols] = held
            mixed_ref[there, out_cols] = (
                direct - held.astype(jnp.float32) + ladder.astype(jnp.float32)
            ).astype(jnp.bfloat16)
            row += count


def build_rows(place, interaction, smalls, made, low, high):
    rows, pairs = interaction.shape
    pattern, hopping, occupation = smalls[:3]
    orbitals = hopping.shape[0]
    height = high - low
    block = low // height
    assert low % height == 0
    shape = pltpu.HBM((rows, pairs), jnp.bfloat16)
    chunks = 4
    once = pl.Buffered(1)
    wide = pl.BlockSpec((height, pairs), lambda g, p: (block, 0), pipeline_mode=once)
    chunk = pl.BlockSpec((height, pairs // chunks), lambda g, p: (block, g))
    smem = pl.BlockSpec(memory_space=pltpu.SMEM)
    row4 = pl.BlockSpec((1, 4 * orbitals), lambda g, p: (0, 0))
    small = pl.BlockSpec((orbitals, 4 * orbitals), lambda g, p: (0, 0))
    twice = pl.BlockSpec((2 * orbitals, 4 * orbitals), lambda g, p: (0, 0))
    return pl.pallas_call(
        functools.partial(build_body, orbitals, low, high, pairs),
        grid_spec=pltpu.PrefetchScalarGridSpec(
            num_scalar_prefetch=1,
            grid=(chunks,),
            in_specs=[wide, smem, smem, smem, twice, small, row4]
            + [pl.BlockSpec(memory_space=pl.ANY)] * len(made),
            out_specs=[chunk] * 2,
            scratch_shapes=[pltpu.VMEM((-(-height // 128) * orbitals * (orbitals + 1), 128), jnp.float32)],
        ),
        out_shape=[shape] * 2,
        input_output_aliases={8 + n: n for n in range(len(made))},
        compiler_params=pltpu.CompilerParams(vmem_limit_bytes=28 * MIB),
        cost_estimate=pl.CostEstimate(flops=1024, bytes_accessed=1024, transcendentals=0),
        name="build_rows",
    )(place, interaction, *smalls, *made)


def step_body(parts, rows, opening, closing, summing, before, orbitals, *refs):
    place_ref = refs[0]
    refs = list(refs[1:])
    chips = len(parts)
    mixed_ref, polar_ref = refs.pop(0), refs.pop(0)
    greens = []
    for count in parts:
        pieces = [refs.pop(0) for _ in range(2 * count)]
        greens.append([pieces[:count], pieces[count:]])
    sums = [] if opening else [refs.pop(0) for _ in range(3)]
    olds = [refs.pop(0) for _ in range(2)] if closing else []
    del refs[:before]
    held = refs.pop()
    totals = [refs.pop() for _ in range(3)][::-1] if closing else refs[:3]
    core = place_ref[0]
    span = greens[0][0][0].shape[1]
    now = pl.program_id(1)

    for chip in range(chips):

        @pl.when(now == chip)
        def _():
            for which in range(2):
                lane = core if which == 0 else 1 - core
                there = pl.ds(pl.multiple_of(lane * rows, 64), rows)
                pieces = greens[chip][which]
                same = pieces[0][:rows, :]
                opp = pieces[-1][pieces[-1].shape[0] - rows :, :]
                both = same.astype(jnp.float32) + opp.astype(jnp.float32)
                held[there, :span] = same
                held[there, span : 2 * span] = opp
                held[there, 2 * span :] = both.astype(jnp.bfloat16)

    @pl.when(now == 0)
    def _():
        for n in range(3):
            if opening:
                totals[n][...] = jnp.zeros_like(totals[n])
            else:
                totals[n][...] = sums[n][...]

    mixed = product(mixed_ref[...], held[:, : 2 * span])
    totals[0][...] += mixed[:, :span]
    totals[1][...] += mixed[:, span:]
    totals[2][...] += product(polar_ref[...], held[:, 2 * span :])
    if closing:

        @pl.when(now == chips - 1)
        def _():
            for first in range(rows // orbitals):
                part = slice(first * orbitals, (first + 1) * orbitals)
                shared = totals[2][part, :]
                for kind in range(2):
                    slope = totals[kind][part, :] + shared
                    old = olds[kind][part, :].astype(jnp.float32)
                    refs[kind][part, :] = slope
                    refs[2 + kind][part, :] = (old + 0.5 * slope).astype(jnp.bfloat16)

    if summing:

        @pl.when(now == chips - 1)
        def _():
            for first in range(rows // orbitals):
                part = slice(first * orbitals, (first + 1) * orbitals)
                both = totals[0][part, :] + totals[1][part, :] + 2.0 * totals[2][part, :]
                refs[3][first : first + 1, :] = jnp.sum(both, axis=0, keepdims=True)


def step(place, low, mats, greens, sums, olds, orbitals, summing=False, at=0, before=()):
    chips = len(greens)
    opening, closing = not sums, bool(olds)
    rows = mats[0].shape[0]
    width = greens[0][0][0].shape[1]
    parts = tuple(len(pair[0]) for pair in greens)
    wide = 2 * rows
    span = min(width, 256) if closing else width
    tall = pl.BlockSpec((rows, span), lambda n, g, p: (0, n + at))
    mat = pl.BlockSpec((rows, wide), lambda n, g, p: (0, p[1 + low + g]))
    wide_sum = jax.ShapeDtypeStruct((rows, width), jnp.float32)
    scratch = [pltpu.VMEM((wide, 3 * span), jnp.bfloat16)]
    if closing:
        out_specs = [tall] * 4
        out_shape = [wide_sum] * 2 + [jax.ShapeDtypeStruct((rows, width), jnp.bfloat16)] * 2
        scratch = [pltpu.VMEM((rows, span), jnp.float32)] * 3 + scratch
    else:
        out_specs, out_shape = [tall] * 3, [wide_sum] * 3
        if summing:
            out_specs = out_specs + [pl.BlockSpec((rows // orbitals, span), lambda n, g, p: (0, n))]
            out_shape = out_shape + [jax.ShapeDtypeStruct((rows // orbitals, width), jnp.float32)]
    operands = [pltpu.with_memory_space_constraint(mat_, pltpu.HBM) for mat_ in mats]
    blocks = [block for pair in greens for side in pair for block in side]
    operands += blocks
    in_specs = [mat] * 2
    mode = pl.Buffered(1 if span == width else 2)
    in_specs += [
        pl.BlockSpec((block.shape[0], span), lambda n, g, p: (0, n + at), pipeline_mode=mode)
        for block in blocks
    ]
    aliases = {}
    if not opening:
        if not closing:
            aliases = {1 + len(operands) + n: n for n in range(3)}
        operands += list(sums)
        in_specs += [pl.BlockSpec((rows, span), lambda n, g, p: (0, n + at), pipeline_mode=mode)] * 3
    if closing:
        operands += list(olds)
        in_specs += [tall] * 2
        aliases = {1 + len(operands) + n: n for n in range(len(before))}
        operands += list(before)
        in_specs += [pl.BlockSpec(memory_space=pl.ANY)] * len(before)
    return pl.pallas_call(
        functools.partial(
            step_body, parts, rows, opening, closing, summing, len(before), orbitals
        ),
        grid_spec=pltpu.PrefetchScalarGridSpec(
            num_scalar_prefetch=1,
            grid=(1, chips),
            in_specs=in_specs,
            out_specs=out_specs,
            scratch_shapes=scratch,
        ),
        out_shape=out_shape,
        input_output_aliases=aliases,
        compiler_params=pltpu.CompilerParams(vmem_limit_bytes=36 * MIB),
        cost_estimate=pl.CostEstimate(flops=1024, bytes_accessed=1024, transcendentals=0),
        name="add_products",
    )(place, *operands)


def sums_body(orbitals, place_ref, mixed_ref, polar_ref, out_ref):
    rows, wide = mixed_ref.shape
    out_ref[...] = jnp.zeros_like(out_ref)
    for kind, ref in enumerate((mixed_ref, polar_ref)):
        lines = [
            jnp.sum(ref[low : low + orbitals, :].astype(jnp.float32), axis=0, keepdims=True)
            for low in range(0, rows, orbitals)
        ]
        lines += [jnp.zeros((8 - len(lines), wide), jnp.float32)] if len(lines) < 8 else []
        total = jnp.concatenate(lines, axis=0)
        high = total.astype(jnp.bfloat16).astype(jnp.float32)
        pair = jnp.concatenate([high, total - high], axis=0)
        out_ref[16 * kind : 16 * (kind + 1), :] = pair.astype(jnp.bfloat16)


def row_sums(place, spot, mats, orbitals):
    rows, pairs = mats[0].shape
    mat = pl.BlockSpec((rows, 2 * rows), lambda g, p: (0, p[1 + spot]))
    return pl.pallas_call(
        functools.partial(sums_body, orbitals),
        grid_spec=pltpu.PrefetchScalarGridSpec(
            num_scalar_prefetch=1,
            grid=(1,),
            in_specs=[mat, mat],
            out_specs=pl.BlockSpec((32, 2 * rows), lambda g, p: (0, 0)),
        ),
        out_shape=jax.ShapeDtypeStruct((32, 2 * rows), jnp.bfloat16),
        compiler_params=pltpu.CompilerParams(vmem_limit_bytes=20 * MIB),
        cost_estimate=pl.CostEstimate(flops=1024, bytes_accessed=1024, transcendentals=0),
        name="row_sums",
    )(place, *[pltpu.with_memory_space_constraint(mat_, pltpu.HBM) for mat_ in mats])


def share_body(scale, place_ref, own_ref, other_ref, same_ref, opp_ref, part_ref, out_ref, held):
    core = place_ref[0]
    rows, width = same_ref.shape
    there = pl.ds(pl.multiple_of(core * rows, 64), rows)
    rest = pl.ds(pl.multiple_of((1 - core) * rows, 64), rows)
    same, opp = same_ref[...], opp_ref[...]
    both = same.astype(jnp.float32) + opp.astype(jnp.float32)
    held[rest, :] = jnp.zeros((rows, 3 * width), jnp.bfloat16)
    held[there, :width] = same
    held[there, width : 2 * width] = opp
    held[there, 2 * width :] = both.astype(jnp.bfloat16)
    lines = jnp.concatenate([own_ref[...], other_ref[...]], axis=0)
    all_terms = product(lines, held[...])
    ends = []
    for low in (0, 32):
        terms = all_terms[low : low + 32]
        mixed = terms[0:8] + terms[8:16]
        polar = terms[16:24] + terms[24:32]
        ends.append(
            mixed[:, :width] + mixed[:, width : 2 * width] + 2.0 * polar[:, 2 * width :]
        )
    count = part_ref.shape[0]
    mine = (ends[0][:count] + part_ref[...]) * scale
    theirs = ends[1][:count] * scale
    first = core == 0
    out_ref[:count, :] = jnp.where(first, mine, theirs)
    out_ref[count:, :] = jnp.where(first, theirs, mine)


def chip_share(place, own_lines, other_lines, far, part, orbitals):
    rows, width = far[0].shape
    whole = lambda array: pl.BlockSpec(array.shape, lambda g, p: (0, 0))
    operands = [own_lines, other_lines, *far, part]
    return pl.pallas_call(
        functools.partial(share_body, 1.0 / math.sqrt(orbitals)),
        grid_spec=pltpu.PrefetchScalarGridSpec(
            num_scalar_prefetch=1,
            grid=(1,),
            in_specs=[whole(array) for array in operands],
            out_specs=pl.BlockSpec((2 * part.shape[0], width), lambda g, p: (0, 0)),
            scratch_shapes=[pltpu.VMEM((2 * rows, 3 * width), jnp.bfloat16)],
        ),
        out_shape=jax.ShapeDtypeStruct((2 * part.shape[0], width), jnp.float32),
        compiler_params=pltpu.CompilerParams(vmem_limit_bytes=20 * MIB),
        cost_estimate=pl.CostEstimate(flops=1024, bytes_accessed=1024, transcendentals=0),
        name="chip_share",
    )(place, *operands)


def spread_blocks(block, index, stride, devices):
    blocks = [block]
    for other in range(1, 4):
        pairs_of = [(d, d ^ (other * stride)) for d in range(devices)]
        blocks.append(lax.ppermute(block, "prow", pairs_of))
    part = index // stride % 4
    low, high = part % 2 == 1, part // 2 == 1
    b = [jnp.where(low, blocks[n ^ 1], blocks[n]) for n in range(4)]
    b = [jnp.where(high, b[n ^ 2], b[n]) for n in range(4)]
    return jnp.concatenate(b, axis=0)


def after(value, *others):
    return lax.optimization_barrier((value, *others))[0]


def ring_form(green_same, green_opp, interaction, pattern, occupation, hopping):
    rows, width = green_same.shape
    orbitals = hopping.shape[0]
    pairs = orbitals * orbitals
    devices = pairs // rows
    chips = devices // 2
    me = lax.axis_index("prow")
    core = me % 2
    order = list(range(0, chips, 2)) + list(range(chips - 1, 0, -2))
    spot = [order.index(c) for c in range(chips)]
    half = chips // 2

    def away(device, far):
        way = 1 if device % 2 == 0 else -1
        return order[(spot[device // 2] - way * far) % chips]

    first_way = [(2 * away(d, 1) + d % 2, d) for d in range(devices)]
    second_way = [(b, a) for a, b in first_way]
    across = [(d, d ^ 1) for d in range(devices)]
    table = []
    for d in range(devices):
        line = [d % 2, d // 2]
        for far in range(1, half + 1):
            line += [away(d, -far), away(d, far)]
        table.append(line)
    place = lax.dynamic_index_in_dim(jnp.array(table, jnp.int32), me, 0, keepdims=False)

    def send(block, pairs_of):
        return lax.ppermute(block, "prow", pairs_of)

    interaction = pltpu.with_memory_space_constraint(interaction, pltpu.HBM)
    start = (me * (rows // orbitals)).astype(jnp.int32)[None]
    smalls = (
        pattern,
        hopping,
        occupation,
        jnp.concatenate([jnp.concatenate([pattern.astype(jnp.float32), hopping], axis=0)] * 4, axis=1),
        jnp.array(np.tile(np.eye(orbitals, dtype=np.float32), (1, 4))),
        jnp.concatenate([occupation] * 4)[None],
    )

    big = rows // 9 * 4
    cuts = [(2 * big, rows), (0, big), (big, 2 * big)]

    def build(when, made, part):
        return build_rows(when, interaction, smalls, made, *cuts[part])

    own = jnp.concatenate([green_same, green_opp], axis=0)
    moving = [send(own, first_way), None]
    mats = build(start, (), 0)
    own_later = after(own, mats[0])
    moving[1] = send(own_later, second_way)
    near = send(own_later, across)
    mats = build(start, mats, 1)

    low, sums, done = 0, (), mats[0]
    waiting = [([own], [near])]
    for far in range(1, half):
        got, passed = [], []
        for turn in range(2):
            block = after(moving[turn], done)
            onward = block if far < half - 1 else block[turn * rows : (turn + 1) * rows]
            moving[turn] = send(onward, second_way if turn else first_way)
            got.append(block)
            passed.append(send(block, across))
            if far == 1 and turn == 0:
                mats = build(after(start, block), mats, 2)
                done = mats[0]
                continue
            later = []
            if turn == 1:
                came = [([got[1]], [passed[0]]), ([got[0]], [passed[1]])]
                split = 0 if far == 1 else 1
                waiting, later = waiting + came[:split], came[split:]
            when = after(place, block)
            if far == 2 and turn == 0:
                lines = row_sums(when, chips - 1, mats, orbitals)
                when = after(when, lines)
            if far == half - 1 and turn == 0:
                when = after(when, other_lines)
            sums = step(when, low, mats, waiting, sums, (), orbitals)
            low += len(waiting)
            waiting, done = later, sums[0]
            if far == 2 and turn == 0:
                other_lines = send(after(lines, done), across)
    *sums, part = step(place, low, mats, waiting, sums, (), orbitals, summing=True)
    low += len(waiting)
    last = [after(block, sums[0]) for block in moving]
    shared = [send(block, across) for block in last]

    mine = chip_share(place, lines, other_lines, last, part, orbitals)
    quad = [mine]
    for other in range(1, 4):
        quad.append(lax.ppermute(mine, "prow", [(d, d ^ other) for d in range(devices)]))
    olds = (green_same, green_opp)
    outs = step(after(place, mine), low, mats, [(last, shared)], sums, olds, orbitals)
    quad = lax.optimization_barrier((*quad, outs[0]))
    here, there = quad[0] + quad[1], quad[2] + quad[3]
    lower = me // 2 % 2 == 0
    rows_four = jnp.concatenate(
        [jnp.where(lower, here, there), jnp.where(lower, there, here)], axis=0
    )
    collision = spread_blocks(rows_four, me, 4, devices)
    outs = step(place, low, mats, [(last, shared)], sums, olds, orbitals, at=1, before=outs)
    return (*outs, collision)


def per_device(green_same, green_opp, interaction, pattern, occupation, hopping):
    rows = green_same.shape[0]
    orbitals = hopping.shape[0]
    devices = orbitals * orbitals // rows
    fits = rows % orbitals == 0 and rows % 576 == 0 and devices == 16 and rows // orbitals <= 8
    fits = fits and green_same.shape[1] == 512
    form = ring_form if fits else plain_form
    return form(green_same, green_opp, interaction, pattern, occupation, hopping)


def solution(mesh):
    placed = (
        P(("groups", "prow"), None),
        P(("groups", "prow"), None),
        P(("groups", "prow"), None),
        P("groups", None),
        P("groups"),
        P("groups", None),
    )
    return jax.shard_map(
        per_device,
        mesh=mesh,
        in_specs=placed,
        out_specs=(
            P(("groups", "prow"), None),
            P(("groups", "prow"), None),
            P(("groups", "prow"), None),
            P(("groups", "prow"), None),
            P("groups", None),
        ),
        check_vma=False,
    )
```

```python
import functools
import math

import jax
import jax.numpy as jnp
import numpy as np
from jax import lax
from jax.experimental import pallas as pl
from jax.experimental.pallas import tpu as pltpu
from jax.sharding import PartitionSpec as P

MIB = 1 << 20


def swap_orbitals(block, orbitals):
    count = block.shape[1]
    return (
        block.reshape(orbitals, orbitals, count)
        .transpose(1, 0, 2)
        .reshape(orbitals * orbitals, count)
    )


def product(left, right):
    return jnp.dot(left, right, preferred_element_type=jnp.float32)


def plain_form(green_same, green_opp, interaction, pattern, occupation, hopping):
    rows, width = green_same.shape
    orbitals = hopping.shape[0]
    pairs = orbitals * orbitals
    highest = lax.Precision.HIGHEST
    row_ids = lax.axis_index("prow") * rows + jnp.arange(rows, dtype=jnp.int32)
    orbit_ids = jnp.arange(orbitals, dtype=jnp.int32)
    first_hot = (row_ids[:, None] // orbitals == orbit_ids[None, :]).astype(jnp.float32)
    second_hot = (row_ids[:, None] % orbitals == orbit_ids[None, :]).astype(jnp.float32)
    linked = jnp.dot(first_hot, pattern.astype(jnp.float32), precision=highest)
    screened = (
        interaction.astype(jnp.float32).reshape(rows, orbitals, orbitals) * linked[:, :, None]
    )
    polar_factor = occupation[:, None] - occupation[None, :]
    ladder_factor = 1.0 - occupation[:, None] - occupation[None, :]
    polar_terms = screened * polar_factor[None]
    hop_first = jnp.dot(first_hot, hopping, precision=highest)
    hop_second = jnp.dot(second_hot, hopping, precision=highest)
    pair_hopping = (
        hop_first[:, :, None] * second_hot[:, None, :]
        + first_hot[:, :, None] * hop_second[:, None, :]
    )
    kernel_direct = (polar_terms + pair_hopping).astype(jnp.bfloat16).reshape(rows, pairs)
    kernel_polar = polar_terms.astype(jnp.bfloat16).reshape(rows, pairs)
    kernel_ladder = (screened * ladder_factor[None]).astype(jnp.bfloat16).reshape(rows, pairs)
    same_piece = lax.all_gather(green_same, "prow", axis=0, tiled=True)
    opp_piece = lax.all_gather(green_opp, "prow", axis=0, tiled=True)
    new_same = (
        product(kernel_direct, same_piece)
        + product(kernel_polar, opp_piece)
        + product(kernel_ladder, swap_orbitals(same_piece, orbitals))
    )
    new_opp = (
        product(kernel_direct, opp_piece)
        + product(kernel_polar, same_piece)
        + product(kernel_ladder, swap_orbitals(opp_piece, orbitals))
    )
    next_same = (green_same.astype(jnp.float32) + 0.5 * new_same).astype(jnp.bfloat16)
    next_opp = (green_opp.astype(jnp.float32) + 0.5 * new_opp).astype(jnp.bfloat16)
    share = jnp.dot(first_hot.T, new_same + new_opp, precision=highest) * (
        1.0 / math.sqrt(orbitals)
    )
    collision = lax.psum(share, "prow")
    return (new_same, new_opp, next_same, next_opp, collision)


def build_body(orbitals, low, high, pairs, *refs):
    place_ref, inter_ref, pat_ref, hop_ref, occ_ref = refs[:5]
    both4_ref, eye4_ref, occ4_ref = refs[5:8]
    mixed_ref, polar_ref, turned_ref = refs[-3:]
    span = 4 * orbitals
    tiles = pairs // span
    start = place_ref[0]
    strips = range(0, high - low, 128)

    pitch = orbitals + 1
    room = orbitals * pitch

    @pl.when(pl.program_id(0) == 0)
    def _():
        @pl.loop(0, tiles // 2)
        def _(tile):
            cols = pl.ds(pl.multiple_of(tile * 2 * span, 128), 2 * span)
            for strip in strips:
                size = min(128, high - low - strip)
                turned = inter_ref[strip : strip + size, cols].astype(jnp.float32).T
                at = pl.multiple_of(strip // 128 * room + tile * 8 * pitch, 8)
                for m in range(8):
                    there = pl.ds(at + m * pitch, orbitals)
                    turned_ref[there, :size] = turned[m * orbitals : (m + 1) * orbitals]

    group = lax.broadcasted_iota(jnp.int32, (1, span), 1) // orbitals
    occ4 = occ4_ref[...]

    per_chunk = mixed_ref.shape[1] // span

    @pl.loop(0, per_chunk, unroll=2)
    def _(step):
        tile = pl.program_id(0) * per_chunk + step
        cols = pl.ds(pl.multiple_of(tile * span, 128), span)
        out_cols = pl.ds(pl.multiple_of(step * span, 128), span)

        def spread(values):
            row = jnp.where(group == 0, values[0], values[1])
            return jnp.where(group == 2, values[2], jnp.where(group == 3, values[3], row))

        inner = [4 * tile + m for m in range(4)]
        occ = spread([occ_ref[i] for i in inner])
        polar_factor = occ - occ4
        ladder_factor = (1.0 - occ4) - occ
        facts = {}
        for first in range(low // orbitals, -(-high // orbitals)):
            here = start + first
            linked = spread([pat_ref[here, i].astype(jnp.float32) for i in inner])
            hop_row = spread([hop_ref[here, i] for i in inner])
            unit = (group + 4 * tile == here).astype(jnp.float32)
            linked4 = both4_ref[pl.ds(here, 1), :]
            facts[first] = (linked * polar_factor, linked4 * ladder_factor, hop_row, unit)
        blocks = []
        for strip in strips:
            size = min(128, high - low - strip)
            pieces = [
                turned_ref[
                    pl.ds(strip // 128 * room + 4 * tile + m, orbitals, stride=pitch), :
                ]
                for m in range(4)
            ]
            blocks.append(jnp.concatenate(pieces, axis=0).T[:size])
        block = jnp.concatenate(blocks, axis=0)
        row = low
        while row < high:
            first, second = row // orbitals, row % orbitals
            count = min(orbitals - second, high - row)
            there = slice(row - low, row - low + count)
            polar_row, ladder_row, hop_row, unit = facts[first]
            polar = inter_ref[there, cols].astype(jnp.float32) * polar_row
            hop = (
                hop_row * eye4_ref[second : second + count]
                + unit * both4_ref[orbitals + second : orbitals + second + count]
            )
            ladder = (block[there] * ladder_row).astype(jnp.bfloat16)
            direct = (polar + hop).astype(jnp.bfloat16).astype(jnp.float32)
            held = polar.astype(jnp.bfloat16)
            polar_ref[there, out_cols] = held
            mixed_ref[there, out_cols] = (
                direct - held.astype(jnp.float32) + ladder.astype(jnp.float32)
            ).astype(jnp.bfloat16)
            row += count


def build_rows(place, interaction, smalls, made, low, high):
    rows, pairs = interaction.shape
    pattern, hopping, occupation = smalls[:3]
    orbitals = hopping.shape[0]
    height = high - low
    block = low // height
    assert low % height == 0
    shape = pltpu.HBM((rows, pairs), jnp.bfloat16)
    chunks = 4
    once = pl.Buffered(1)
    wide = pl.BlockSpec((height, pairs), lambda g, p: (block, 0), pipeline_mode=once)
    chunk = pl.BlockSpec((height, pairs // chunks), lambda g, p: (block, g))
    smem = pl.BlockSpec(memory_space=pltpu.SMEM)
    row4 = pl.BlockSpec((1, 4 * orbitals), lambda g, p: (0, 0))
    small = pl.BlockSpec((orbitals, 4 * orbitals), lambda g, p: (0, 0))
    twice = pl.BlockSpec((2 * orbitals, 4 * orbitals), lambda g, p: (0, 0))
    return pl.pallas_call(
        functools.partial(build_body, orbitals, low, high, pairs),
        grid_spec=pltpu.PrefetchScalarGridSpec(
            num_scalar_prefetch=1,
            grid=(chunks,),
            in_specs=[wide, smem, smem, smem, twice, small, row4]
            + [pl.BlockSpec(memory_space=pl.ANY)] * len(made),
            out_specs=[chunk] * 2,
            scratch_shapes=[pltpu.VMEM((-(-height // 128) * orbitals * (orbitals + 1), 128), jnp.float32)],
        ),
        out_shape=[shape] * 2,
        input_output_aliases={8 + n: n for n in range(len(made))},
        compiler_params=pltpu.CompilerParams(vmem_limit_bytes=28 * MIB),
        cost_estimate=pl.CostEstimate(flops=1024, bytes_accessed=1024, transcendentals=0),
        name="build_rows",
    )(place, interaction, *smalls, *made)


def step_body(parts, rows, opening, closing, orbitals, scale, *refs):
    place_ref = refs[0]
    refs = list(refs[1:])
    chips = len(parts)
    mixed_ref, polar_ref = refs.pop(0), refs.pop(0)
    greens = []
    for count in parts:
        pieces = [refs.pop(0) for _ in range(2 * count)]
        greens.append([pieces[:count], pieces[count:]])
    sums = [] if opening else [refs.pop(0) for _ in range(3)]
    olds = [refs.pop(0) for _ in range(2)] if closing else []
    held = refs.pop()
    totals = [refs.pop() for _ in range(3)][::-1] if closing else refs[:3]
    core = place_ref[0]
    span = greens[0][0][0].shape[1]
    now = pl.program_id(1)

    for chip in range(chips):

        @pl.when(now == chip)
        def _():
            for which in range(2):
                lane = core if which == 0 else 1 - core
                there = pl.ds(pl.multiple_of(lane * rows, 64), rows)
                pieces = greens[chip][which]
                same = pieces[0][:rows, :]
                opp = pieces[-1][pieces[-1].shape[0] - rows :, :]
                both = same.astype(jnp.float32) + opp.astype(jnp.float32)
                held[there, :span] = same
                held[there, span : 2 * span] = opp
                held[there, 2 * span :] = both.astype(jnp.bfloat16)

    @pl.when(now == 0)
    def _():
        for n in range(3):
            if opening:
                totals[n][...] = jnp.zeros_like(totals[n])
            else:
                totals[n][...] = sums[n][...]

    mixed = product(mixed_ref[...], held[:, : 2 * span])
    totals[0][...] += mixed[:, :span]
    totals[1][...] += mixed[:, span:]
    totals[2][...] += product(polar_ref[...], held[:, 2 * span :])
    if closing:

        @pl.when(now == chips - 1)
        def _():
            for first in range(rows // orbitals):
                part = slice(first * orbitals, (first + 1) * orbitals)
                shared = totals[2][part, :]
                both = None
                for kind in range(2):
                    slope = totals[kind][part, :] + shared
                    old = olds[kind][part, :].astype(jnp.float32)
                    refs[kind][part, :] = slope
                    refs[2 + kind][part, :] = (old + 0.5 * slope).astype(jnp.bfloat16)
                    both = slope if both is None else both + slope
                refs[4][first : first + 1, :] = jnp.sum(both, axis=0, keepdims=True) * scale


def step(place, low, mats, greens, sums, olds, orbitals):
    chips = len(greens)
    opening, closing = not sums, bool(olds)
    rows = mats[0].shape[0]
    width = greens[0][0][0].shape[1]
    parts = tuple(len(pair[0]) for pair in greens)
    wide = 2 * rows
    span = min(width, 128) if closing else width
    tall = pl.BlockSpec((rows, span), lambda n, g, p: (0, n))
    mat = pl.BlockSpec((rows, wide), lambda n, g, p: (0, p[1 + low + g]))
    wide_sum = jax.ShapeDtypeStruct((rows, width), jnp.float32)
    scratch = [pltpu.VMEM((wide, 3 * span), jnp.bfloat16)]
    if closing:
        out_specs = [tall] * 4 + [pl.BlockSpec((rows // orbitals, span), lambda n, g, p: (0, n))]
        out_shape = [wide_sum] * 2 + [jax.ShapeDtypeStruct((rows, width), jnp.bfloat16)] * 2
        out_shape += [jax.ShapeDtypeStruct((rows // orbitals, width), jnp.float32)]
        scratch = [pltpu.VMEM((rows, span), jnp.float32)] * 3 + scratch
    else:
        out_specs, out_shape = [tall] * 3, [wide_sum] * 3
    operands = [pltpu.with_memory_space_constraint(mat_, pltpu.HBM) for mat_ in mats]
    blocks = [block for pair in greens for side in pair for block in side]
    operands += blocks
    in_specs = [mat] * 2
    mode = pl.Buffered(1 if span == width else 2)
    in_specs += [
        pl.BlockSpec((block.shape[0], span), lambda n, g, p: (0, n), pipeline_mode=mode)
        for block in blocks
    ]
    aliases = {}
    if not opening:
        if not closing:
            aliases = {1 + len(operands) + n: n for n in range(3)}
        operands += list(sums)
        in_specs += [pl.BlockSpec((rows, span), lambda n, g, p: (0, n), pipeline_mode=mode)] * 3
    if closing:
        operands += list(olds)
        in_specs += [tall] * 2
    return pl.pallas_call(
        functools.partial(
            step_body, parts, rows, opening, closing, orbitals, 1.0 / math.sqrt(orbitals)
        ),
        grid_spec=pltpu.PrefetchScalarGridSpec(
            num_scalar_prefetch=1,
            grid=(width // span, chips),
            in_specs=in_specs,
            out_specs=out_specs,
            scratch_shapes=scratch,
        ),
        out_shape=out_shape,
        input_output_aliases=aliases,
        compiler_params=pltpu.CompilerParams(vmem_limit_bytes=36 * MIB),
        cost_estimate=pl.CostEstimate(flops=1024, bytes_accessed=1024, transcendentals=0),
        name="add_products",
    )(place, *operands)


def spread_blocks(block, index, stride, devices):
    blocks = [block]
    for other in range(1, 4):
        pairs_of = [(d, d ^ (other * stride)) for d in range(devices)]
        blocks.append(lax.ppermute(block, "prow", pairs_of))
    part = index // stride % 4
    low, high = part % 2 == 1, part // 2 == 1
    b = [jnp.where(low, blocks[n ^ 1], blocks[n]) for n in range(4)]
    b = [jnp.where(high, b[n ^ 2], b[n]) for n in range(4)]
    return jnp.concatenate(b, axis=0)


def after(value, *others):
    return lax.optimization_barrier((value, *others))[0]


def ring_form(green_same, green_opp, interaction, pattern, occupation, hopping):
    rows, width = green_same.shape
    orbitals = hopping.shape[0]
    pairs = orbitals * orbitals
    devices = pairs // rows
    chips = devices // 2
    me = lax.axis_index("prow")
    core = me % 2
    order = list(range(0, chips, 2)) + list(range(chips - 1, 0, -2))
    spot = [order.index(c) for c in range(chips)]
    half = chips // 2

    def away(device, far):
        way = 1 if device % 2 == 0 else -1
        return order[(spot[device // 2] - way * far) % chips]

    first_way = [(2 * away(d, 1) + d % 2, d) for d in range(devices)]
    second_way = [(b, a) for a, b in first_way]
    across = [(d, d ^ 1) for d in range(devices)]
    table = []
    for d in range(devices):
        line = [d % 2, d // 2]
        for far in range(1, half + 1):
            line += [away(d, -far), away(d, far)]
        table.append(line)
    place = lax.dynamic_index_in_dim(jnp.array(table, jnp.int32), me, 0, keepdims=False)

    def send(block, pairs_of):
        return lax.ppermute(block, "prow", pairs_of)

    interaction = pltpu.with_memory_space_constraint(interaction, pltpu.HBM)
    start = (me * (rows // orbitals)).astype(jnp.int32)[None]
    smalls = (
        pattern,
        hopping,
        occupation,
        jnp.concatenate([jnp.concatenate([pattern.astype(jnp.float32), hopping], axis=0)] * 4, axis=1),
        jnp.array(np.tile(np.eye(orbitals, dtype=np.float32), (1, 4))),
        jnp.concatenate([occupation] * 4)[None],
    )

    big = rows // 9 * 4
    cuts = [(2 * big, rows), (0, big), (big, 2 * big)]

    def build(when, made, part):
        return build_rows(when, interaction, smalls, made, *cuts[part])

    own = jnp.concatenate([green_same, green_opp], axis=0)
    moving = [send(own, first_way), None]
    mats = build(start, (), 0)
    own_later = after(own, mats[0])
    moving[1] = send(own_later, second_way)
    near = send(own_later, across)
    mats = build(start, mats, 1)

    low, sums, done = 0, (), mats[0]
    waiting = [([own], [near])]
    for far in range(1, half):
        got, passed = [], []
        for turn in range(2):
            block = after(moving[turn], done)
            onward = block if far < half - 1 else block[turn * rows : (turn + 1) * rows]
            moving[turn] = send(onward, second_way if turn else first_way)
            got.append(block)
            passed.append(send(block, across))
            if far == 1 and turn == 0:
                mats = build(after(start, block), mats, 2)
                done = mats[0]
                continue
            later = []
            if turn == 1:
                came = [([got[1]], [passed[0]]), ([got[0]], [passed[1]])]
                split = 0 if far == 1 else 1
                waiting, later = waiting + came[:split], came[split:]
            when = after(place, block, onward) if turn == 0 else after(place, block)
            sums = step(when, low, mats, waiting, sums, (), orbitals)
            low += len(waiting)
            waiting, done = later, sums[0]
    sums = step(place, low, mats, waiting, sums, (), orbitals)
    low += len(waiting)
    last = [after(block, sums[0]) for block in moving]
    shared = [send(block, across) for block in last]
    new_same, new_opp, next_same, next_opp, part = step(
        place, low, mats, [(last, shared)], sums, (green_same, green_opp), orbitals
    )
    if devices == 16:
        collision = spread_blocks(spread_blocks(part, me, 1, devices), me, 4, devices)
    else:
        collision = lax.all_gather(part, "prow", axis=0, tiled=True)
    return (new_same, new_opp, next_same, next_opp, collision)


def per_device(green_same, green_opp, interaction, pattern, occupation, hopping):
    rows = green_same.shape[0]
    orbitals = hopping.shape[0]
    devices = orbitals * orbitals // rows
    fits = rows % orbitals == 0 and rows % 576 == 0 and devices % 4 == 0 and devices >= 12
    form = ring_form if fits else plain_form
    return form(green_same, green_opp, interaction, pattern, occupation, hopping)


def solution(mesh):
    placed = (
        P(("groups", "prow"), None),
        P(("groups", "prow"), None),
        P(("groups", "prow"), None),
        P("groups", None),
        P("groups"),
        P("groups", None),
    )
    return jax.shard_map(
        per_device,
        mesh=mesh,
        in_specs=placed,
        out_specs=(
            P(("groups", "prow"), None),
            P(("groups", "prow"), None),
            P(("groups", "prow"), None),
            P(("groups", "prow"), None),
            P("groups", None),
        ),
        check_vma=False,
    )
```

```python
import functools
import math

import jax
import jax.numpy as jnp
import numpy as np
from jax import lax
from jax.experimental import pallas as pl
from jax.experimental.pallas import tpu as pltpu
from jax.sharding import PartitionSpec as P

MIB = 1 << 20


def swap_orbitals(block, orbitals):
    count = block.shape[1]
    return (
        block.reshape(orbitals, orbitals, count)
        .transpose(1, 0, 2)
        .reshape(orbitals * orbitals, count)
    )


def product(left, right):
    return jnp.dot(left, right, preferred_element_type=jnp.float32)


def plain_form(green_same, green_opp, interaction, pattern, occupation, hopping):
    rows, width = green_same.shape
    orbitals = hopping.shape[0]
    pairs = orbitals * orbitals
    highest = lax.Precision.HIGHEST
    row_ids = lax.axis_index("prow") * rows + jnp.arange(rows, dtype=jnp.int32)
    orbit_ids = jnp.arange(orbitals, dtype=jnp.int32)
    first_hot = (row_ids[:, None] // orbitals == orbit_ids[None, :]).astype(jnp.float32)
    second_hot = (row_ids[:, None] % orbitals == orbit_ids[None, :]).astype(jnp.float32)
    linked = jnp.dot(first_hot, pattern.astype(jnp.float32), precision=highest)
    screened = (
        interaction.astype(jnp.float32).reshape(rows, orbitals, orbitals) * linked[:, :, None]
    )
    polar_factor = occupation[:, None] - occupation[None, :]
    ladder_factor = 1.0 - occupation[:, None] - occupation[None, :]
    polar_terms = screened * polar_factor[None]
    hop_first = jnp.dot(first_hot, hopping, precision=highest)
    hop_second = jnp.dot(second_hot, hopping, precision=highest)
    pair_hopping = (
        hop_first[:, :, None] * second_hot[:, None, :]
        + first_hot[:, :, None] * hop_second[:, None, :]
    )
    kernel_direct = (polar_terms + pair_hopping).astype(jnp.bfloat16).reshape(rows, pairs)
    kernel_polar = polar_terms.astype(jnp.bfloat16).reshape(rows, pairs)
    kernel_ladder = (screened * ladder_factor[None]).astype(jnp.bfloat16).reshape(rows, pairs)
    same_piece = lax.all_gather(green_same, "prow", axis=0, tiled=True)
    opp_piece = lax.all_gather(green_opp, "prow", axis=0, tiled=True)
    new_same = (
        product(kernel_direct, same_piece)
        + product(kernel_polar, opp_piece)
        + product(kernel_ladder, swap_orbitals(same_piece, orbitals))
    )
    new_opp = (
        product(kernel_direct, opp_piece)
        + product(kernel_polar, same_piece)
        + product(kernel_ladder, swap_orbitals(opp_piece, orbitals))
    )
    next_same = (green_same.astype(jnp.float32) + 0.5 * new_same).astype(jnp.bfloat16)
    next_opp = (green_opp.astype(jnp.float32) + 0.5 * new_opp).astype(jnp.bfloat16)
    share = jnp.dot(first_hot.T, new_same + new_opp, precision=highest) * (
        1.0 / math.sqrt(orbitals)
    )
    collision = lax.psum(share, "prow")
    return (new_same, new_opp, next_same, next_opp, collision)


def build_body(orbitals, low, high, pairs, *refs):
    place_ref, inter_ref, pat_ref, hop_ref, occ_ref = refs[:5]
    both4_ref, eye4_ref, occ4_ref = refs[5:8]
    mixed_ref, polar_ref, turned_ref = refs[-3:]
    span = 4 * orbitals
    tiles = pairs // span
    start = place_ref[0]
    strips = range(0, high - low, 128)

    pitch = orbitals + 1
    room = orbitals * pitch

    @pl.when(pl.program_id(0) == 0)
    def _():
        @pl.loop(0, tiles // 2)
        def _(tile):
            cols = pl.ds(pl.multiple_of(tile * 2 * span, 128), 2 * span)
            for strip in strips:
                size = min(128, high - low - strip)
                turned = inter_ref[strip : strip + size, cols].astype(jnp.float32).T
                at = pl.multiple_of(strip // 128 * room + tile * 8 * pitch, 8)
                for m in range(8):
                    there = pl.ds(at + m * pitch, orbitals)
                    turned_ref[there, :size] = turned[m * orbitals : (m + 1) * orbitals]

    group = lax.broadcasted_iota(jnp.int32, (1, span), 1) // orbitals
    occ4 = occ4_ref[...]

    per_chunk = mixed_ref.shape[1] // span

    @pl.loop(0, per_chunk, unroll=2)
    def _(step):
        tile = pl.program_id(0) * per_chunk + step
        cols = pl.ds(pl.multiple_of(tile * span, 128), span)
        out_cols = pl.ds(pl.multiple_of(step * span, 128), span)

        def spread(values):
            row = jnp.where(group == 0, values[0], values[1])
            return jnp.where(group == 2, values[2], jnp.where(group == 3, values[3], row))

        inner = [4 * tile + m for m in range(4)]
        occ = spread([occ_ref[i] for i in inner])
        polar_factor = occ - occ4
        ladder_factor = (1.0 - occ4) - occ
        facts = {}
        for first in range(low // orbitals, -(-high // orbitals)):
            here = start + first
            linked = spread([pat_ref[here, i].astype(jnp.float32) for i in inner])
            hop_row = spread([hop_ref[here, i] for i in inner])
            unit = (group + 4 * tile == here).astype(jnp.float32)
            linked4 = both4_ref[pl.ds(here, 1), :]
            facts[first] = (linked * polar_factor, linked4 * ladder_factor, hop_row, unit)
        blocks = []
        for strip in strips:
            size = min(128, high - low - strip)
            pieces = [
                turned_ref[
                    pl.ds(strip // 128 * room + 4 * tile + m, orbitals, stride=pitch), :
                ]
                for m in range(4)
            ]
            blocks.append(jnp.concatenate(pieces, axis=0).T[:size])
        block = jnp.concatenate(blocks, axis=0)
        row = low
        while row < high:
            first, second = row // orbitals, row % orbitals
            count = min(orbitals - second, high - row)
            there = slice(row - low, row - low + count)
            polar_row, ladder_row, hop_row, unit = facts[first]
            polar = inter_ref[there, cols].astype(jnp.float32) * polar_row
            hop = (
                hop_row * eye4_ref[second : second + count]
                + unit * both4_ref[orbitals + second : orbitals + second + count]
            )
            ladder = (block[there] * ladder_row).astype(jnp.bfloat16)
            direct = (polar + hop).astype(jnp.bfloat16).astype(jnp.float32)
            held = polar.astype(jnp.bfloat16)
            polar_ref[there, out_cols] = held
            mixed_ref[there, out_cols] = (
                direct - held.astype(jnp.float32) + ladder.astype(jnp.float32)
            ).astype(jnp.bfloat16)
            row += count


def build_rows(place, interaction, smalls, made, low, high):
    rows, pairs = interaction.shape
    pattern, hopping, occupation = smalls[:3]
    orbitals = hopping.shape[0]
    height = high - low
    block = low // height
    assert low % height == 0
    shape = pltpu.HBM((rows, pairs), jnp.bfloat16)
    chunks = 4
    once = pl.Buffered(1)
    wide = pl.BlockSpec((height, pairs), lambda g, p: (block, 0), pipeline_mode=once)
    chunk = pl.BlockSpec((height, pairs // chunks), lambda g, p: (block, g))
    smem = pl.BlockSpec(memory_space=pltpu.SMEM)
    row4 = pl.BlockSpec((1, 4 * orbitals), lambda g, p: (0, 0))
    small = pl.BlockSpec((orbitals, 4 * orbitals), lambda g, p: (0, 0))
    twice = pl.BlockSpec((2 * orbitals, 4 * orbitals), lambda g, p: (0, 0))
    return pl.pallas_call(
        functools.partial(build_body, orbitals, low, high, pairs),
        grid_spec=pltpu.PrefetchScalarGridSpec(
            num_scalar_prefetch=1,
            grid=(chunks,),
            in_specs=[wide, smem, smem, smem, twice, small, row4]
            + [pl.BlockSpec(memory_space=pl.ANY)] * len(made),
            out_specs=[chunk] * 2,
            scratch_shapes=[pltpu.VMEM((-(-height // 128) * orbitals * (orbitals + 1), 128), jnp.float32)],
        ),
        out_shape=[shape] * 2,
        input_output_aliases={8 + n: n for n in range(len(made))},
        compiler_params=pltpu.CompilerParams(vmem_limit_bytes=28 * MIB),
        cost_estimate=pl.CostEstimate(flops=1024, bytes_accessed=1024, transcendentals=0),
        name="build_rows",
    )(place, interaction, *smalls, *made)


def step_body(parts, rows, opening, closing, orbitals, scale, *refs):
    place_ref = refs[0]
    refs = list(refs[1:])
    chips = len(parts)
    mixed_ref, polar_ref = refs.pop(0), refs.pop(0)
    greens = []
    for count in parts:
        pieces = [refs.pop(0) for _ in range(2 * count)]
        greens.append([pieces[:count], pieces[count:]])
    sums = [] if opening else [refs.pop(0) for _ in range(3)]
    olds = [refs.pop(0) for _ in range(2)] if closing else []
    held = refs.pop()
    totals = [refs.pop() for _ in range(3)][::-1] if closing else refs[:3]
    core = place_ref[0]
    span = greens[0][0][0].shape[1]
    now = pl.program_id(1)

    for chip in range(chips):

        @pl.when(now == chip)
        def _():
            for which in range(2):
                lane = core if which == 0 else 1 - core
                there = pl.ds(pl.multiple_of(lane * rows, 64), rows)
                pieces = greens[chip][which]
                same = pieces[0][:rows, :]
                opp = pieces[-1][pieces[-1].shape[0] - rows :, :]
                both = same.astype(jnp.float32) + opp.astype(jnp.float32)
                held[there, :span] = same
                held[there, span : 2 * span] = opp
                held[there, 2 * span :] = both.astype(jnp.bfloat16)

    @pl.when(now == 0)
    def _():
        for n in range(3):
            if opening:
                totals[n][...] = jnp.zeros_like(totals[n])
            else:
                totals[n][...] = sums[n][...]

    mixed = product(mixed_ref[...], held[:, : 2 * span])
    totals[0][...] += mixed[:, :span]
    totals[1][...] += mixed[:, span:]
    totals[2][...] += product(polar_ref[...], held[:, 2 * span :])
    if closing:

        @pl.when(now == chips - 1)
        def _():
            for first in range(rows // orbitals):
                part = slice(first * orbitals, (first + 1) * orbitals)
                shared = totals[2][part, :]
                both = None
                for kind in range(2):
                    slope = totals[kind][part, :] + shared
                    old = olds[kind][part, :].astype(jnp.float32)
                    refs[kind][part, :] = slope
                    refs[2 + kind][part, :] = (old + 0.5 * slope).astype(jnp.bfloat16)
                    both = slope if both is None else both + slope
                refs[4][first : first + 1, :] = jnp.sum(both, axis=0, keepdims=True) * scale


def step(place, low, mats, greens, sums, olds, orbitals):
    chips = len(greens)
    opening, closing = not sums, bool(olds)
    rows = mats[0].shape[0]
    width = greens[0][0][0].shape[1]
    parts = tuple(len(pair[0]) for pair in greens)
    wide = 2 * rows
    span = width
    tall = pl.BlockSpec((rows, span), lambda n, g, p: (0, n))
    mat = pl.BlockSpec((rows, wide), lambda n, g, p: (0, p[1 + low + g]))
    wide_sum = jax.ShapeDtypeStruct((rows, width), jnp.float32)
    scratch = [pltpu.VMEM((wide, 3 * span), jnp.bfloat16)]
    if closing:
        out_specs = [tall] * 4 + [pl.BlockSpec((rows // orbitals, span), lambda n, g, p: (0, n))]
        out_shape = [wide_sum] * 2 + [jax.ShapeDtypeStruct((rows, width), jnp.bfloat16)] * 2
        out_shape += [jax.ShapeDtypeStruct((rows // orbitals, width), jnp.float32)]
        scratch = [pltpu.VMEM((rows, span), jnp.float32)] * 3 + scratch
    else:
        out_specs, out_shape = [tall] * 3, [wide_sum] * 3
    operands = [pltpu.with_memory_space_constraint(mat_, pltpu.HBM) for mat_ in mats]
    blocks = [block for pair in greens for side in pair for block in side]
    operands += blocks
    in_specs = [mat] * 2
    mode = pl.Buffered(1 if span == width else 2)
    in_specs += [
        pl.BlockSpec((block.shape[0], span), lambda n, g, p: (0, n), pipeline_mode=mode)
        for block in blocks
    ]
    aliases = {}
    if not opening:
        if not closing:
            aliases = {1 + len(operands) + n: n for n in range(3)}
        operands += list(sums)
        in_specs += [pl.BlockSpec((rows, span), lambda n, g, p: (0, n), pipeline_mode=mode)] * 3
    if closing:
        operands += list(olds)
        in_specs += [tall] * 2
    return pl.pallas_call(
        functools.partial(
            step_body, parts, rows, opening, closing, orbitals, 1.0 / math.sqrt(orbitals)
        ),
        grid_spec=pltpu.PrefetchScalarGridSpec(
            num_scalar_prefetch=1,
            grid=(width // span, chips),
            in_specs=in_specs,
            out_specs=out_specs,
            scratch_shapes=scratch,
        ),
        out_shape=out_shape,
        input_output_aliases=aliases,
        compiler_params=pltpu.CompilerParams(vmem_limit_bytes=36 * MIB),
        cost_estimate=pl.CostEstimate(flops=1024, bytes_accessed=1024, transcendentals=0),
        name="add_products",
    )(place, *operands)


def spread_blocks(block, index, stride, devices):
    blocks = [block]
    for other in range(1, 4):
        pairs_of = [(d, d ^ (other * stride)) for d in range(devices)]
        blocks.append(lax.ppermute(block, "prow", pairs_of))
    part = index // stride % 4
    low, high = part % 2 == 1, part // 2 == 1
    b = [jnp.where(low, blocks[n ^ 1], blocks[n]) for n in range(4)]
    b = [jnp.where(high, b[n ^ 2], b[n]) for n in range(4)]
    return jnp.concatenate(b, axis=0)


def after(value, *others):
    return lax.optimization_barrier((value, *others))[0]


def ring_form(green_same, green_opp, interaction, pattern, occupation, hopping):
    rows, width = green_same.shape
    orbitals = hopping.shape[0]
    pairs = orbitals * orbitals
    devices = pairs // rows
    chips = devices // 2
    me = lax.axis_index("prow")
    core = me % 2
    order = list(range(0, chips, 2)) + list(range(chips - 1, 0, -2))
    spot = [order.index(c) for c in range(chips)]
    half = chips // 2

    def away(device, far):
        way = 1 if device % 2 == 0 else -1
        return order[(spot[device // 2] - way * far) % chips]

    first_way = [(2 * away(d, 1) + d % 2, d) for d in range(devices)]
    second_way = [(b, a) for a, b in first_way]
    across = [(d, d ^ 1) for d in range(devices)]
    table = []
    for d in range(devices):
        line = [d % 2, d // 2]
        for far in range(1, half + 1):
            line += [away(d, -far), away(d, far)]
        table.append(line)
    place = lax.dynamic_index_in_dim(jnp.array(table, jnp.int32), me, 0, keepdims=False)

    def send(block, pairs_of):
        return lax.ppermute(block, "prow", pairs_of)

    interaction = pltpu.with_memory_space_constraint(interaction, pltpu.HBM)
    start = (me * (rows // orbitals)).astype(jnp.int32)[None]
    smalls = (
        pattern,
        hopping,
        occupation,
        jnp.concatenate([jnp.concatenate([pattern.astype(jnp.float32), hopping], axis=0)] * 4, axis=1),
        jnp.array(np.tile(np.eye(orbitals, dtype=np.float32), (1, 4))),
        jnp.concatenate([occupation] * 4)[None],
    )

    big = rows // 9 * 4
    cuts = [(2 * big, rows), (0, big), (big, 2 * big)]

    def build(when, made, part):
        return build_rows(when, interaction, smalls, made, *cuts[part])

    own = jnp.concatenate([green_same, green_opp], axis=0)
    moving = [send(own, first_way), None]
    mats = build(start, (), 0)
    own_later = after(own, mats[0])
    moving[1] = send(own_later, second_way)
    near = send(own_later, across)
    mats = build(start, mats, 1)

    low, sums, done = 0, (), mats[0]
    waiting = [([own], [near])]
    for far in range(1, half):
        got, passed = [], []
        for turn in range(2):
            block = after(moving[turn], done)
            onward = block if far < half - 1 else block[turn * rows : (turn + 1) * rows]
            moving[turn] = send(onward, second_way if turn else first_way)
            got.append(block)
            passed.append(send(block, across))
            if far == 1 and turn == 0:
                mats = build(after(start, block), mats, 2)
                done = mats[0]
                continue
            later = []
            if turn == 1:
                came = [([got[1]], [passed[0]]), ([got[0]], [passed[1]])]
                split = 0 if far == 1 else 1
                waiting, later = waiting + came[:split], came[split:]
            sums = step(after(place, block), low, mats, waiting, sums, (), orbitals)
            low += len(waiting)
            waiting, done = later, sums[0]
    sums = step(place, low, mats, waiting, sums, (), orbitals)
    low += len(waiting)
    last = [after(block, sums[0]) for block in moving]
    shared = [send(block, across) for block in last]
    new_same, new_opp, next_same, next_opp, part = step(
        place, low, mats, [(last, shared)], sums, (green_same, green_opp), orbitals
    )
    if devices == 16:
        collision = spread_blocks(spread_blocks(part, me, 1, devices), me, 4, devices)
    else:
        collision = lax.all_gather(part, "prow", axis=0, tiled=True)
    return (new_same, new_opp, next_same, next_opp, collision)


def per_device(green_same, green_opp, interaction, pattern, occupation, hopping):
    rows = green_same.shape[0]
    orbitals = hopping.shape[0]
    devices = orbitals * orbitals // rows
    fits = rows % orbitals == 0 and rows % 576 == 0 and devices % 4 == 0 and devices >= 12
    form = ring_form if fits else plain_form
    return form(green_same, green_opp, interaction, pattern, occupation, hopping)


def solution(mesh):
    placed = (
        P(("groups", "prow"), None),
        P(("groups", "prow"), None),
        P(("groups", "prow"), None),
        P("groups", None),
        P("groups"),
        P("groups", None),
    )
    return jax.shard_map(
        per_device,
        mesh=mesh,
        in_specs=placed,
        out_specs=(
            P(("groups", "prow"), None),
            P(("groups", "prow"), None),
            P(("groups", "prow"), None),
            P(("groups", "prow"), None),
            P("groups", None),
        ),
        check_vma=False,
    )
```

```python
import functools
import math

import jax
import jax.numpy as jnp
import numpy as np
from jax import lax
from jax.experimental import pallas as pl
from jax.experimental.pallas import tpu as pltpu
from jax.sharding import PartitionSpec as P

MIB = 1 << 20


def swap_orbitals(block, orbitals):
    count = block.shape[1]
    return (
        block.reshape(orbitals, orbitals, count)
        .transpose(1, 0, 2)
        .reshape(orbitals * orbitals, count)
    )


def product(left, right):
    return jnp.dot(left, right, preferred_element_type=jnp.float32)


def plain_form(green_same, green_opp, interaction, pattern, occupation, hopping):
    rows, width = green_same.shape
    orbitals = hopping.shape[0]
    pairs = orbitals * orbitals
    highest = lax.Precision.HIGHEST
    row_ids = lax.axis_index("prow") * rows + jnp.arange(rows, dtype=jnp.int32)
    orbit_ids = jnp.arange(orbitals, dtype=jnp.int32)
    first_hot = (row_ids[:, None] // orbitals == orbit_ids[None, :]).astype(jnp.float32)
    second_hot = (row_ids[:, None] % orbitals == orbit_ids[None, :]).astype(jnp.float32)
    linked = jnp.dot(first_hot, pattern.astype(jnp.float32), precision=highest)
    screened = (
        interaction.astype(jnp.float32).reshape(rows, orbitals, orbitals) * linked[:, :, None]
    )
    polar_factor = occupation[:, None] - occupation[None, :]
    ladder_factor = 1.0 - occupation[:, None] - occupation[None, :]
    polar_terms = screened * polar_factor[None]
    hop_first = jnp.dot(first_hot, hopping, precision=highest)
    hop_second = jnp.dot(second_hot, hopping, precision=highest)
    pair_hopping = (
        hop_first[:, :, None] * second_hot[:, None, :]
        + first_hot[:, :, None] * hop_second[:, None, :]
    )
    kernel_direct = (polar_terms + pair_hopping).astype(jnp.bfloat16).reshape(rows, pairs)
    kernel_polar = polar_terms.astype(jnp.bfloat16).reshape(rows, pairs)
    kernel_ladder = (screened * ladder_factor[None]).astype(jnp.bfloat16).reshape(rows, pairs)
    same_piece = lax.all_gather(green_same, "prow", axis=0, tiled=True)
    opp_piece = lax.all_gather(green_opp, "prow", axis=0, tiled=True)
    new_same = (
        product(kernel_direct, same_piece)
        + product(kernel_polar, opp_piece)
        + product(kernel_ladder, swap_orbitals(same_piece, orbitals))
    )
    new_opp = (
        product(kernel_direct, opp_piece)
        + product(kernel_polar, same_piece)
        + product(kernel_ladder, swap_orbitals(opp_piece, orbitals))
    )
    next_same = (green_same.astype(jnp.float32) + 0.5 * new_same).astype(jnp.bfloat16)
    next_opp = (green_opp.astype(jnp.float32) + 0.5 * new_opp).astype(jnp.bfloat16)
    share = jnp.dot(first_hot.T, new_same + new_opp, precision=highest) * (
        1.0 / math.sqrt(orbitals)
    )
    collision = lax.psum(share, "prow")
    return (new_same, new_opp, next_same, next_opp, collision)


def build_body(orbitals, low, high, pairs, *refs):
    place_ref, inter_ref, pat_ref, hop_ref, occ_ref = refs[:5]
    both4_ref, eye4_ref, occ4_ref = refs[5:8]
    mixed_ref, polar_ref, turned_ref = refs[-3:]
    span = 4 * orbitals
    tiles = pairs // span
    start = place_ref[0]
    strips = range(0, high - low, 128)

    pitch = orbitals + 1
    room = orbitals * pitch

    @pl.when(pl.program_id(0) == 0)
    def _():
        @pl.loop(0, tiles // 2)
        def _(tile):
            cols = pl.ds(pl.multiple_of(tile * 2 * span, 128), 2 * span)
            for strip in strips:
                size = min(128, high - low - strip)
                turned = inter_ref[strip : strip + size, cols].astype(jnp.float32).T
                at = pl.multiple_of(strip // 128 * room + tile * 8 * pitch, 8)
                for m in range(8):
                    there = pl.ds(at + m * pitch, orbitals)
                    turned_ref[there, :size] = turned[m * orbitals : (m + 1) * orbitals]

    group = lax.broadcasted_iota(jnp.int32, (1, span), 1) // orbitals
    occ4 = occ4_ref[...]

    per_chunk = mixed_ref.shape[1] // span

    @pl.loop(0, per_chunk, unroll=2)
    def _(step):
        tile = pl.program_id(0) * per_chunk + step
        cols = pl.ds(pl.multiple_of(tile * span, 128), span)
        out_cols = pl.ds(pl.multiple_of(step * span, 128), span)

        def spread(values):
            row = jnp.where(group == 0, values[0], values[1])
            return jnp.where(group == 2, values[2], jnp.where(group == 3, values[3], row))

        inner = [4 * tile + m for m in range(4)]
        occ = spread([occ_ref[i] for i in inner])
        polar_factor = occ - occ4
        ladder_factor = (1.0 - occ4) - occ
        facts = {}
        for first in range(low // orbitals, -(-high // orbitals)):
            here = start + first
            linked = spread([pat_ref[here, i].astype(jnp.float32) for i in inner])
            hop_row = spread([hop_ref[here, i] for i in inner])
            unit = (group + 4 * tile == here).astype(jnp.float32)
            linked4 = both4_ref[pl.ds(here, 1), :]
            facts[first] = (linked * polar_factor, linked4 * ladder_factor, hop_row, unit)
        blocks = []
        for strip in strips:
            size = min(128, high - low - strip)
            pieces = [
                turned_ref[
                    pl.ds(strip // 128 * room + 4 * tile + m, orbitals, stride=pitch), :
                ]
                for m in range(4)
            ]
            blocks.append(jnp.concatenate(pieces, axis=0).T[:size])
        block = jnp.concatenate(blocks, axis=0)
        row = low
        while row < high:
            first, second = row // orbitals, row % orbitals
            count = min(orbitals - second, high - row)
            there = slice(row - low, row - low + count)
            polar_row, ladder_row, hop_row, unit = facts[first]
            polar = inter_ref[there, cols].astype(jnp.float32) * polar_row
            hop = (
                hop_row * eye4_ref[second : second + count]
                + unit * both4_ref[orbitals + second : orbitals + second + count]
            )
            ladder = (block[there] * ladder_row).astype(jnp.bfloat16)
            direct = (polar + hop).astype(jnp.bfloat16).astype(jnp.float32)
            held = polar.astype(jnp.bfloat16)
            polar_ref[there, out_cols] = held
            mixed_ref[there, out_cols] = (
                direct - held.astype(jnp.float32) + ladder.astype(jnp.float32)
            ).astype(jnp.bfloat16)
            row += count


def build_rows(place, interaction, smalls, made, low, high):
    rows, pairs = interaction.shape
    pattern, hopping, occupation = smalls[:3]
    orbitals = hopping.shape[0]
    height = high - low
    block = low // height
    assert low % height == 0
    shape = pltpu.HBM((rows, pairs), jnp.bfloat16)
    chunks = 4
    once = pl.Buffered(1)
    wide = pl.BlockSpec((height, pairs), lambda g, p: (block, 0), pipeline_mode=once)
    chunk = pl.BlockSpec((height, pairs // chunks), lambda g, p: (block, g))
    smem = pl.BlockSpec(memory_space=pltpu.SMEM)
    row4 = pl.BlockSpec((1, 4 * orbitals), lambda g, p: (0, 0))
    small = pl.BlockSpec((orbitals, 4 * orbitals), lambda g, p: (0, 0))
    twice = pl.BlockSpec((2 * orbitals, 4 * orbitals), lambda g, p: (0, 0))
    return pl.pallas_call(
        functools.partial(build_body, orbitals, low, high, pairs),
        grid_spec=pltpu.PrefetchScalarGridSpec(
            num_scalar_prefetch=1,
            grid=(chunks,),
            in_specs=[wide, smem, smem, smem, twice, small, row4]
            + [pl.BlockSpec(memory_space=pl.ANY)] * len(made),
            out_specs=[chunk] * 2,
            scratch_shapes=[pltpu.VMEM((-(-height // 128) * orbitals * (orbitals + 1), 128), jnp.float32)],
        ),
        out_shape=[shape] * 2,
        input_output_aliases={8 + n: n for n in range(len(made))},
        compiler_params=pltpu.CompilerParams(vmem_limit_bytes=28 * MIB),
        cost_estimate=pl.CostEstimate(flops=1024, bytes_accessed=1024, transcendentals=0),
        name="build_rows",
    )(place, interaction, *smalls, *made)


def step_body(parts, rows, opening, closing, folding, orbitals, scale, *refs):
    place_ref = refs[0]
    refs = list(refs[1:])
    chips = len(parts)
    mixed_ref, polar_ref = refs.pop(0), refs.pop(0)
    greens = []
    for count in parts:
        pieces = [refs.pop(0) for _ in range(2 * count)]
        greens.append([pieces[:count], pieces[count:]])
    sums = [] if opening else [refs.pop(0) for _ in range(2 if closing else 3)]
    olds = [refs.pop(0) for _ in range(2)] if closing else []
    held = refs.pop()
    if closing:
        totals = [refs.pop() for _ in range(3)][::-1]
    else:
        totals = refs[:2] + [refs.pop()] if folding else refs[:3]
    core = place_ref[0]
    span = greens[0][0][0].shape[1]
    now = pl.program_id(1)

    for chip in range(chips):

        @pl.when(now == chip)
        def _():
            for which in range(2):
                lane = core if which == 0 else 1 - core
                there = pl.ds(pl.multiple_of(lane * rows, 64), rows)
                pieces = greens[chip][which]
                same = pieces[0][:rows, :]
                opp = pieces[-1][pieces[-1].shape[0] - rows :, :]
                both = same.astype(jnp.float32) + opp.astype(jnp.float32)
                held[there, :span] = same
                held[there, span : 2 * span] = opp
                held[there, 2 * span :] = both.astype(jnp.bfloat16)

    @pl.when(now == 0)
    def _():
        for n in range(3):
            if n >= len(sums):
                totals[n][...] = jnp.zeros_like(totals[n])
            else:
                totals[n][...] = sums[n][...]

    mixed = product(mixed_ref[...], held[:, : 2 * span])
    totals[0][...] += mixed[:, :span]
    totals[1][...] += mixed[:, span:]
    totals[2][...] += product(polar_ref[...], held[:, 2 * span :])
    if folding:

        @pl.when(now == chips - 1)
        def _():
            for n in range(2):
                totals[n][...] += totals[2][...]

    if closing:

        @pl.when(now == chips - 1)
        def _():
            for first in range(rows // orbitals):
                part = slice(first * orbitals, (first + 1) * orbitals)
                shared = totals[2][part, :]
                both = None
                for kind in range(2):
                    slope = totals[kind][part, :] + shared
                    old = olds[kind][part, :].astype(jnp.float32)
                    refs[kind][part, :] = slope
                    refs[2 + kind][part, :] = (old + 0.5 * slope).astype(jnp.bfloat16)
                    both = slope if both is None else both + slope
                refs[4][first : first + 1, :] = jnp.sum(both, axis=0, keepdims=True) * scale


def step(place, low, mats, greens, sums, olds, orbitals, folding=False):
    chips = len(greens)
    opening, closing = not sums, bool(olds)
    rows = mats[0].shape[0]
    width = greens[0][0][0].shape[1]
    parts = tuple(len(pair[0]) for pair in greens)
    wide = 2 * rows
    span = min(width, 256) if closing else width
    tall = pl.BlockSpec((rows, span), lambda n, g, p: (0, n))
    mat = pl.BlockSpec((rows, wide), lambda n, g, p: (0, p[1 + low + g]))
    wide_sum = jax.ShapeDtypeStruct((rows, width), jnp.float32)
    scratch = [pltpu.VMEM((wide, 3 * span), jnp.bfloat16)]
    if closing:
        out_specs = [tall] * 4 + [pl.BlockSpec((rows // orbitals, span), lambda n, g, p: (0, n))]
        out_shape = [wide_sum] * 2 + [jax.ShapeDtypeStruct((rows, width), jnp.bfloat16)] * 2
        out_shape += [jax.ShapeDtypeStruct((rows // orbitals, width), jnp.float32)]
        scratch = [pltpu.VMEM((rows, span), jnp.float32)] * 3 + scratch
    else:
        kept = 2 if folding else 3
        out_specs, out_shape = [tall] * kept, [wide_sum] * kept
        scratch = [pltpu.VMEM((rows, span), jnp.float32)] * (3 - kept) + scratch
    operands = [pltpu.with_memory_space_constraint(mat_, pltpu.HBM) for mat_ in mats]
    blocks = [block for pair in greens for side in pair for block in side]
    operands += blocks
    in_specs = [mat] * 2
    mode = pl.Buffered(1 if span == width else 2)
    in_specs += [
        pl.BlockSpec((block.shape[0], span), lambda n, g, p: (0, n), pipeline_mode=mode)
        for block in blocks
    ]
    aliases = {}
    if not opening:
        if not closing:
            aliases = {1 + len(operands) + n: n for n in range(kept)}
        operands += list(sums)
        in_specs += [pl.BlockSpec((rows, span), lambda n, g, p: (0, n), pipeline_mode=mode)] * len(sums)
    if closing:
        operands += list(olds)
        in_specs += [tall] * 2
    return pl.pallas_call(
        functools.partial(
            step_body, parts, rows, opening, closing, folding, orbitals, 1.0 / math.sqrt(orbitals)
        ),
        grid_spec=pltpu.PrefetchScalarGridSpec(
            num_scalar_prefetch=1,
            grid=(width // span, chips),
            in_specs=in_specs,
            out_specs=out_specs,
            scratch_shapes=scratch,
        ),
        out_shape=out_shape,
        input_output_aliases=aliases,
        compiler_params=pltpu.CompilerParams(vmem_limit_bytes=36 * MIB),
        cost_estimate=pl.CostEstimate(flops=1024, bytes_accessed=1024, transcendentals=0),
        name="add_products",
    )(place, *operands)


def spread_blocks(block, index, stride, devices):
    blocks = [block]
    for other in range(1, 4):
        pairs_of = [(d, d ^ (other * stride)) for d in range(devices)]
        blocks.append(lax.ppermute(block, "prow", pairs_of))
    part = index // stride % 4
    low, high = part % 2 == 1, part // 2 == 1
    b = [jnp.where(low, blocks[n ^ 1], blocks[n]) for n in range(4)]
    b = [jnp.where(high, b[n ^ 2], b[n]) for n in range(4)]
    return jnp.concatenate(b, axis=0)


def after(value, *others):
    return lax.optimization_barrier((value, *others))[0]


def ring_form(green_same, green_opp, interaction, pattern, occupation, hopping):
    rows, width = green_same.shape
    orbitals = hopping.shape[0]
    pairs = orbitals * orbitals
    devices = pairs // rows
    chips = devices // 2
    me = lax.axis_index("prow")
    core = me % 2
    order = list(range(0, chips, 2)) + list(range(chips - 1, 0, -2))
    spot = [order.index(c) for c in range(chips)]
    half = chips // 2

    def away(device, far):
        way = 1 if device % 2 == 0 else -1
        return order[(spot[device // 2] - way * far) % chips]

    first_way = [(2 * away(d, 1) + d % 2, d) for d in range(devices)]
    second_way = [(b, a) for a, b in first_way]
    across = [(d, d ^ 1) for d in range(devices)]
    table = []
    for d in range(devices):
        line = [d % 2, d // 2]
        for far in range(1, half + 1):
            line += [away(d, -far), away(d, far)]
        table.append(line)
    place = lax.dynamic_index_in_dim(jnp.array(table, jnp.int32), me, 0, keepdims=False)

    def send(block, pairs_of):
        return lax.ppermute(block, "prow", pairs_of)

    interaction = pltpu.with_memory_space_constraint(interaction, pltpu.HBM)
    start = (me * (rows // orbitals)).astype(jnp.int32)[None]
    smalls = (
        pattern,
        hopping,
        occupation,
        jnp.concatenate([jnp.concatenate([pattern.astype(jnp.float32), hopping], axis=0)] * 4, axis=1),
        jnp.array(np.tile(np.eye(orbitals, dtype=np.float32), (1, 4))),
        jnp.concatenate([occupation] * 4)[None],
    )

    big = rows // 9 * 4
    cuts = [(2 * big, rows), (0, big), (big, 2 * big)]

    def build(when, made, part):
        return build_rows(when, interaction, smalls, made, *cuts[part])

    own = jnp.concatenate([green_same, green_opp], axis=0)
    moving = [send(own, first_way), None]
    mats = build(start, (), 0)
    own_later = after(own, mats[0])
    moving[1] = send(own_later, second_way)
    near = send(own_later, across)
    mats = build(start, mats, 1)

    low, sums, done = 0, (), mats[0]
    waiting = [([own], [near])]
    for far in range(1, half):
        got, passed = [], []
        for turn in range(2):
            block = after(moving[turn], done)
            onward = block if far < half - 1 else block[turn * rows : (turn + 1) * rows]
            moving[turn] = send(onward, second_way if turn else first_way)
            got.append(block)
            passed.append(send(block, across))
            if far == 1 and turn == 0:
                mats = build(after(start, block), mats, 2)
                done = mats[0]
                continue
            later = []
            if turn == 1:
                came = [([got[1]], [passed[0]]), ([got[0]], [passed[1]])]
                split = 0 if far == 1 else 1
                waiting, later = waiting + came[:split], came[split:]
            sums = step(after(place, block), low, mats, waiting, sums, (), orbitals)
            low += len(waiting)
            waiting, done = later, sums[0]
    sums = step(place, low, mats, waiting, sums, (), orbitals, folding=True)
    low += len(waiting)
    last = [after(block, sums[0]) for block in moving]
    shared = [send(block, across) for block in last]
    new_same, new_opp, next_same, next_opp, part = step(
        place, low, mats, [(last, shared)], sums, (green_same, green_opp), orbitals
    )
    if devices == 16:
        collision = spread_blocks(spread_blocks(part, me, 1, devices), me, 4, devices)
    else:
        collision = lax.all_gather(part, "prow", axis=0, tiled=True)
    return (new_same, new_opp, next_same, next_opp, collision)


def per_device(green_same, green_opp, interaction, pattern, occupation, hopping):
    rows = green_same.shape[0]
    orbitals = hopping.shape[0]
    devices = orbitals * orbitals // rows
    fits = rows % orbitals == 0 and rows % 576 == 0 and devices % 4 == 0 and devices >= 12
    form = ring_form if fits else plain_form
    return form(green_same, green_opp, interaction, pattern, occupation, hopping)


def solution(mesh):
    placed = (
        P(("groups", "prow"), None),
        P(("groups", "prow"), None),
        P(("groups", "prow"), None),
        P("groups", None),
        P("groups"),
        P("groups", None),
    )
    return jax.shard_map(
        per_device,
        mesh=mesh,
        in_specs=placed,
        out_specs=(
            P(("groups", "prow"), None),
            P(("groups", "prow"), None),
            P(("groups", "prow"), None),
            P(("groups", "prow"), None),
            P("groups", None),
        ),
        check_vma=False,
    )
```
